32 devices in a mesh: lat: 4 (over y, x), lon: 8 (over z, core).
Axes of the slice: x: 2, y: 2, z: 4, core: 2. Of those that a mesh axis runs over, the one named last changes fastest.
Arguments:
- tokens: bfloat16 [2, 48, 192, 512], P(None, 'lat', 'lon'), may hold values from -6 to 6
- level_ids: int32 [2, 48, 192], P(None, 'lat', 'lon'), may hold values from 0 to 2
- coarse_ids: int32 [2, 24, 96], P(None, 'lat', 'lon'), may hold values from 0 to 2
- first_qkv: bfloat16 [512, 1536], replicated, may hold values from -1.25 to 1.25
- first_out: bfloat16 [512, 512], replicated, may hold values from -0.25 to 0.25
- merge_weight: bfloat16 [2048, 1024], P('lon'), may hold values from -0.125 to 0.125
- second_qkv: bfloat16 [1024, 3072], P('lon'), may hold values from -1.25 to 1.25
- second_out: bfloat16 [1024, 1024], P('lon'), may hold values from -0.1875 to 0.1875
Outputs:
- skip: bfloat16 [2, 48, 192, 512], P(None, 'lat', 'lon')
- coarse: bfloat16 [2, 24, 96, 1024], P(None, 'lat', 'lon')
The draws below stay inside these ranges and needn't reach their ends.
All inputs are finite; a program needn't handle non-finite values.
Results may differ from the reference program's by a relative error of at most 0.012.
Values may be sent and summed in bfloat16 or wider, within the bound.
No kernel may reach another device: no remote copies, remote signals or barrier semaphores. Data moves between devices by JAX's collectives and lax.ppermute only.
A program may use at most 64 MiB of HBM per device.

```python
import math
import jax
import jax.numpy as jnp
from jax import lax

D1 = 512
D2 = 1024
HEADS1 = 8
HEADS2 = 16
WIN_LEVELS = 2
WIN_ROWS = 6
WIN_COLS = 12
LEVELS = 2
NLAT = 48
NLON = 192


def projection_draw(key, width):
    base = jax.random.truncated_normal(key, -4.0, 4.0, (width, 3 * width), jnp.float32) / jnp.sqrt(jnp.float32(width))
    base = jnp.clip(base, -1.25, 1.25)
    return base.astype(jnp.bfloat16)


def draw_first_qkv(key, part):
    return projection_draw(jax.random.fold_in(key, 11), D1)


def draw_second_qkv(key, part):
    return projection_draw(jax.random.fold_in(key, 13), D2)


def plant(values, key, low, high):
    index_at = [jax.random.randint(jax.random.fold_in(key, axis), (), 0, length) for axis, length in enumerate(values.shape)]
    main_axis = values.shape.index(max(values.shape))
    beside = index_at[:main_axis] + [(index_at[main_axis] + 1) % values.shape[main_axis]] + index_at[main_axis + 1:]
    return values.at[tuple(index_at)].set(low).at[tuple(beside)].set(high)


def block_levels(key, extent, cuts, low, top_value):
    loudness, own = 1.0, jax.random.fold_in(key, 6)
    for axis_at, blocks in cuts:
        heights = jnp.exp(jax.random.uniform(jax.random.fold_in(own, axis_at), (blocks,), jnp.float32, low / len(cuts), top_value / len(cuts)))
        loudness = loudness * jnp.repeat(heights, extent[axis_at] // blocks).reshape([-1 if axis == axis_at else 1 for axis in range(len(extent))])
    return loudness


def centred(stream_key, extent, scale, reach, split=(), dtype=jnp.bfloat16):
    drawn = scale * jax.random.normal(stream_key, extent, jnp.float32)
    if split:
        drawn = drawn * block_levels(stream_key, extent, split, -0.22, 0.18)
    return jnp.clip(drawn, -reach, reach).astype(dtype)


def setup_inputs(seed: int = 0) -> dict:
    splits = jax.random.split(jax.random.key(seed), 9)
    return {
        "tokens": centred(splits[0], (LEVELS, NLAT, NLON, D1), 1.0, 6.0, ((1, 4), (2, 8))),
        "level_ids": plant(jax.random.randint(splits[1], (LEVELS, NLAT, NLON), 0, 3), jax.random.fold_in(splits[1], 1), 0, 2).astype(jnp.int32),
        "coarse_ids": plant(jax.random.randint(splits[2], (LEVELS, NLAT // 2, NLON // 2), 0, 3), jax.random.fold_in(splits[2], 1), 0, 2).astype(jnp.int32),
        "first_qkv": draw_first_qkv(jax.random.fold_in(splits[8], 71), 0),
        "first_out": centred(splits[4], (D1, D1), D1 ** -0.5, 0.25),
        "merge_weight": centred(splits[5], (4 * D1, D2), (4 * D1) ** -0.5, 0.125, ((0, 8),)),
        "second_qkv": draw_second_qkv(jax.random.fold_in(splits[8], 71), 0),
        "second_out": centred(splits[7], (D2, D2), D2 ** -0.5, 0.1875, ((0, 8),)),
    }


EPSILON = 1e-05

def normalized(values):
    widened = values.astype(jnp.float32)
    center = lax.optimization_barrier(jnp.mean(widened, axis=-1, keepdims=True))
    spread = lax.optimization_barrier(jnp.mean(jnp.square(widened - center), axis=-1, keepdims=True))
    return ((widened - center) * lax.rsqrt(spread + EPSILON)).astype(jnp.bfloat16)

def window_softmax(queries, keys, values, labels, heads):
    levels, rows, columns, width = queries.shape
    stacks = levels // WIN_LEVELS
    across = columns // WIN_COLS
    head_size = width // heads

    def windows(array):
        shaped = array.reshape(stacks, WIN_LEVELS, rows, across, WIN_COLS, heads, head_size)
        shaped = shaped.transpose(0, 3, 1, 2, 4, 5, 6)
        return shaped.reshape(stacks * across, WIN_LEVELS * rows * WIN_COLS, heads, head_size).astype(jnp.float32)
    marks = labels.reshape(stacks, WIN_LEVELS, rows, across, WIN_COLS).transpose(0, 3, 1, 2, 4)
    marks = marks.reshape(stacks * across, WIN_LEVELS * rows * WIN_COLS)
    scores = jnp.einsum('wqhd,wkhd->whqk', windows(queries), windows(keys)) / math.sqrt(head_size)
    allowed = marks[:, None, :, None] == marks[:, None, None, :]
    scores = jnp.where(allowed, scores, -1e+30)
    highest = lax.optimization_barrier(jnp.max(scores, axis=-1, keepdims=True))
    expos = jnp.exp(scores - highest)
    weights = (expos / lax.optimization_barrier(jnp.sum(expos, axis=-1, keepdims=True))).astype(jnp.bfloat16)
    mixed = jnp.einsum('whqk,wkhd->wqhd', weights.astype(jnp.float32), windows(values)).astype(jnp.bfloat16)
    mixed = mixed.reshape(stacks, across, WIN_LEVELS, rows, WIN_COLS, width).transpose(0, 2, 3, 1, 4, 5)
    return mixed.reshape(levels, rows, columns, width)

def shifted_layer(field, labels, qkv_weight, out_weight, heads):
    half_rows = WIN_ROWS // 2
    half_cols = WIN_COLS // 2
    levels, height, breadth, width = field.shape
    moved = jnp.roll(field, (-half_rows, -half_cols), (1, 2))
    marks = jnp.roll(labels, (-half_rows, -half_cols), (1, 2))
    bands = height // WIN_ROWS

    def by_band(array):
        return jnp.moveaxis(array.reshape((levels, bands, WIN_ROWS) + array.shape[2:]), 1, 0)

    def one_band(pair):
        band, band_marks = pair
        normed = normalized(band).reshape(-1, width)
        packed = jnp.dot(normed, qkv_weight, preferred_element_type=jnp.float32).astype(jnp.bfloat16)
        packed = packed.reshape(levels, WIN_ROWS, breadth, 3 * width)
        mixed = window_softmax(packed[..., :width], packed[..., width:2 * width], packed[..., 2 * width:], band_marks, heads)
        update = jnp.dot(mixed.reshape(-1, width), out_weight, preferred_element_type=jnp.float32).reshape(band.shape)
        return (band.astype(jnp.float32) + update).astype(jnp.bfloat16)
    result = lax.map(one_band, (by_band(moved), by_band(marks)))
    result = jnp.moveaxis(result, 0, 1).reshape(field.shape)
    return jnp.roll(result, (half_rows, half_cols), (1, 2))

def edge_labels(ids):
    height = ids.shape[1]
    edge = (jnp.arange(height) < WIN_ROWS // 2).astype(jnp.int32)
    return ids * 2 + edge[None, :, None]

def merge_patches(field):
    levels, height, breadth, width = field.shape
    shaped = field.reshape(levels, height // 2, 2, breadth // 2, 2, width).transpose(0, 1, 3, 4, 2, 5)
    return shaped.reshape(levels, height // 2, breadth // 2, 4 * width)

def reference(tokens, level_ids, coarse_ids, first_qkv, first_out, merge_weight, second_qkv, second_out):
    skip = shifted_layer(tokens, edge_labels(level_ids), first_qkv, first_out, HEADS1)
    joined = merge_patches(skip)
    levels, height, breadth, width = joined.shape
    merged = jnp.dot(normalized(joined).reshape(-1, width), merge_weight, preferred_element_type=jnp.float32)
    merged = merged.astype(jnp.bfloat16).reshape(levels, height, breadth, merge_weight.shape[1])
    coarse = shifted_layer(merged, edge_labels(coarse_ids), second_qkv, second_out, HEADS2)
    return (skip, coarse)
```

```python
import math

import jax
import jax.numpy as jnp
from jax import lax
from jax.sharding import PartitionSpec as P

HEADS1 = 8
HEADS2 = 16
WIN_LEVELS = 2
WIN_ROWS = 6
WIN_COLS = 12


EPSILON = 1e-05


def from_behind(block, axis, distance):
    devices = range(lax.axis_size(axis))
    route = [((i - distance) % len(devices), i) for i in devices]
    return lax.ppermute(block, axis, route)


def normalized(values):
    widened = values.astype(jnp.float32)
    center = jnp.mean(widened, axis=-1, keepdims=True)
    spread = jnp.mean(jnp.square(widened - center), axis=-1, keepdims=True)
    return ((widened - center) * lax.rsqrt(spread + EPSILON)).astype(jnp.bfloat16)


def window_softmax(queries, keys, values, labels, heads):
    levels, rows, columns, width = queries.shape
    stacks = levels // WIN_LEVELS
    across = columns // WIN_COLS
    head_size = width // heads

    def windows(array):
        shaped = array.reshape(stacks, WIN_LEVELS, rows, across, WIN_COLS, heads, head_size)
        shaped = shaped.transpose(0, 3, 1, 2, 4, 5, 6)
        return shaped.reshape(stacks * across, WIN_LEVELS * rows * WIN_COLS, heads, head_size)

    marks = labels.reshape(stacks, WIN_LEVELS, rows, across, WIN_COLS).transpose(0, 3, 1, 2, 4)
    marks = marks.reshape(stacks * across, WIN_LEVELS * rows * WIN_COLS)
    scores = jnp.einsum(
        "wqhd,wkhd->whqk", windows(queries), windows(keys), preferred_element_type=jnp.float32
    )
    scores = scores / math.sqrt(head_size)
    allowed = marks[:, None, :, None] == marks[:, None, None, :]
    scores = jnp.where(allowed, scores, -1e30)
    highest = jnp.max(scores, axis=-1, keepdims=True)
    expos = jnp.exp(scores - highest)
    weights = (expos / jnp.sum(expos, axis=-1, keepdims=True)).astype(jnp.bfloat16)
    mixed = jnp.einsum(
        "whqk,wkhd->wqhd", weights, windows(values), preferred_element_type=jnp.float32
    )
    mixed = mixed.astype(jnp.bfloat16)
    mixed = mixed.reshape(stacks, across, WIN_LEVELS, rows, WIN_COLS, width).transpose(
        0, 2, 3, 1, 4, 5
    )
    return mixed.reshape(levels, rows, columns, width)


def attend_bands(queries, keys, values, labels, heads):
    levels, rows, columns, width = queries.shape
    bands = rows // WIN_ROWS

    def by_band(array):
        return jnp.moveaxis(array.reshape((levels, bands, WIN_ROWS) + array.shape[2:]), 1, 0)

    def one_band(group):
        return window_softmax(group[0], group[1], group[2], group[3], heads)

    result = lax.map(one_band, (by_band(queries), by_band(keys), by_band(values), by_band(labels)))
    return jnp.moveaxis(result, 0, 1).reshape(levels, rows, columns, width)


def shifted_layer(field, labels, qkv_product, out_product, heads):
    levels, height, breadth, width = field.shape
    half_rows = WIN_ROWS // 2
    half_cols = WIN_COLS // 2
    marks = labels.astype(jnp.bfloat16)
    below = from_behind((field[:, :half_rows], marks[:, :half_rows]), "lat", -1)
    moved = jnp.concatenate([field[:, half_rows:], below[0]], axis=1)
    moved_marks = jnp.concatenate([marks[:, half_rows:], below[1]], axis=1)
    beside = from_behind((moved[:, :, :half_cols], moved_marks[:, :, :half_cols]), "lon", -1)
    moved = jnp.concatenate([moved[:, :, half_cols:], beside[0]], axis=2)
    moved_marks = jnp.concatenate([moved_marks[:, :, half_cols:], beside[1]], axis=2)
    packed = qkv_product(normalized(moved).reshape(-1, width)).astype(jnp.bfloat16)
    packed = packed.reshape(levels, height, breadth, 3 * width)
    mixed = attend_bands(
        packed[..., :width],
        packed[..., width : 2 * width],
        packed[..., 2 * width :],
        moved_marks.astype(jnp.int32),
        heads,
    )
    update = out_product(mixed.reshape(-1, width)).reshape(field.shape)
    result = (moved.astype(jnp.float32) + update).astype(jnp.bfloat16)
    returned = from_behind(result[:, :, breadth - half_cols :], "lon", 1)
    result = jnp.concatenate([returned, result[:, :, : breadth - half_cols]], axis=2)
    returned = from_behind(result[:, height - half_rows :], "lat", 1)
    return jnp.concatenate([returned, result[:, : height - half_rows]], axis=1)


def edge_labels(ids):
    height = ids.shape[1]
    global_rows = lax.axis_index("lat") * height + jnp.arange(height)
    edge = (global_rows < WIN_ROWS // 2).astype(jnp.int32)
    return ids * 2 + edge[None, :, None]


def merge_patches(field):
    levels, height, breadth, width = field.shape
    shaped = field.reshape(levels, height // 2, 2, breadth // 2, 2, width).transpose(
        0, 1, 3, 4, 2, 5
    )
    return shaped.reshape(levels, height // 2, breadth // 2, 4 * width)


def add_rows(left, piece):
    return jnp.dot(left, piece, preferred_element_type=jnp.float32)


def exchange(block, axis, mask):
    return lax.ppermute(block, axis, [(i, i ^ mask) for i in range(lax.axis_size(axis))])


def spread(shard):
    ranks, rows, columns = lax.axis_size("lon"), shard.shape[0], shard.shape[1]
    stops = ranks // 2
    quarter = columns // 4
    corner = lax.axis_index("lat") % 4
    mine = lax.dynamic_slice(shard, (0, corner * quarter), (rows, quarter))
    far = [
        lax.ppermute(mine, "lon", [(i, (i + 2 * d) % ranks) for i in range(ranks)])
        for d in range(1, stops)
    ]
    near = jnp.concatenate(far, axis=0)
    half = near.shape[0] // 2
    first = exchange(near, "lat", 1)
    second = exchange(near, "lat", 2)
    third = jnp.concatenate([exchange(first[:half], "lat", 2), exchange(second[half:], "lat", 1)], axis=0)
    whole = jnp.zeros((stops * rows, columns), shard.dtype)
    whole = lax.dynamic_update_slice(whole, shard, (0, 0))
    for mask, part in enumerate((near, first, second, third)):
        whole = lax.dynamic_update_slice(whole, part, (rows, (corner ^ mask) * quarter))
    return jnp.concatenate([whole, exchange(whole, "lon", 1)], axis=0)


def reordered(left, rows):
    ranks = lax.axis_size("lon")
    stops = ranks // 2
    me = lax.axis_index("lon")
    pieces = [
        lax.dynamic_slice(left, (0, (((me // 2 - d) % stops) * 2 + (me % 2 ^ side)) * rows), (left.shape[0], rows))
        for side in range(2)
        for d in range(stops)
    ]
    return jnp.concatenate(pieces, axis=1)


def per_device(
    tokens, level_ids, coarse_ids, first_qkv, first_out, merge_weight, second_qkv, second_out
):

    merge_whole = spread(merge_weight)
    second_qkv_whole = spread(second_qkv)

    def second_qkv_product(left):
        return add_rows(reordered(left, second_qkv.shape[0]), second_qkv_whole)

    def second_out_product(left):
        return add_rows(left, lax.all_gather(second_out, "lon", axis=0, tiled=True))

    def first_qkv_product(left):
        return jnp.dot(left, first_qkv, preferred_element_type=jnp.float32)

    def first_out_product(left):
        return jnp.dot(left, first_out, preferred_element_type=jnp.float32)

    skip = shifted_layer(
        tokens, edge_labels(level_ids), first_qkv_product, first_out_product, HEADS1
    )
    joined = merge_patches(skip)
    levels, height, breadth, width = joined.shape
    left = normalized(joined).reshape(-1, width)
    merged = add_rows(reordered(left, merge_weight.shape[0]), merge_whole).astype(jnp.bfloat16)
    merged = merged.reshape(levels, height, breadth, merge_weight.shape[1])
    coarse = shifted_layer(
        merged, edge_labels(coarse_ids), second_qkv_product, second_out_product, HEADS2
    )
    return (skip, coarse)


def solution(mesh):
    placed = (
        P(None, "lat", "lon", None),
        P(None, "lat", "lon"),
        P(None, "lat", "lon"),
        P(),
        P(),
        P("lon", None),
        P("lon", None),
        P("lon", None),
    )
    return jax.shard_map(
        per_device,
        mesh=mesh,
        in_specs=placed,
        out_specs=(P(None, "lat", "lon", None), P(None, "lat", "lon", None)),
        check_vma=False,
    )
```

```python
import math

import jax
import jax.numpy as jnp
import numpy as np
from jax import lax
from jax.experimental import pallas as pl
from jax.experimental.pallas import tpu as pltpu
from jax.sharding import PartitionSpec as P

HEADS1 = 8
HEADS2 = 16
WIN_LEVELS = 2
WIN_ROWS = 6
WIN_COLS = 12
HALF_ROWS = WIN_ROWS // 2
HALF_COLS = WIN_COLS // 2

EPSILON = 1e-05
EXCLUDED = -1e30
LANES = 128
PACK = 16
VMEM_LIMIT = 48 * 1024 * 1024
NT = (((1,), (1,)), ((), ()))


def up(count, unit):
    return -(-count // unit) * unit


def places(levels, rows, columns):
    return np.arange(levels * rows * columns).reshape(levels, rows, columns)


def regions(levels, rows, columns, row_from, column_from):
    at = places(levels, rows, columns)
    in_rows = (np.arange(rows) >= row_from) & (np.arange(rows) < row_from + HALF_ROWS)
    in_columns = (np.arange(columns) >= column_from) & (np.arange(columns) < column_from + HALF_COLS)
    picked = (
        at[:, in_rows][:, :, ~in_columns],
        at[:, ~in_rows][:, :, in_columns],
        at[:, in_rows][:, :, in_columns],
    )
    return [part.reshape(-1) for part in picked]


def window_order(levels, rows, columns):
    at = places(levels, rows, columns)
    order = []
    for band in range(rows // WIN_ROWS):
        for across in range(columns // WIN_COLS):
            r = (HALF_ROWS + WIN_ROWS * band + np.arange(WIN_ROWS)) % rows
            c = (HALF_COLS + WIN_COLS * across + np.arange(WIN_COLS)) % columns
            order.append(at[:, r][:, :, c].reshape(-1))
    return np.concatenate(order)


def matrix(sources, columns, height=None):
    out = np.zeros((height or len(sources), columns), np.float32)
    out[np.arange(len(sources)), sources] = 1
    return jnp.asarray(out, jnp.bfloat16)


def offsets(sizes):
    return np.concatenate([[0], np.cumsum([up(size, LANES) for size in sizes])]).tolist()


def replaced(count, parts, held=None):
    starts = offsets([count] + [up(len(part) + 2, PACK) for part in parts])
    source = np.arange(count) if held is None else held.copy()
    for start, part in zip(starts[1:], parts):
        source[part] = start + np.arange(len(part))
    return source, starts[-1]


def fill(stage_ref, parts):
    start = 0
    for part in parts:
        rows = part.shape[0]
        stage_ref[start : start + rows] = part[...]
        if rows % LANES:
            stage_ref[start + rows : start + up(rows, LANES)] = jnp.zeros(
                (up(rows, LANES) - rows, part.shape[1]), stage_ref.dtype
            )
        start += up(rows, LANES)


def dot(left, right):
    return jnp.dot(left, right, preferred_element_type=jnp.float32)


def dot_nt(left, right):
    return lax.dot_general(left, right, NT, preferred_element_type=jnp.float32)


def normalized(values):
    center = jnp.mean(values, axis=-1, keepdims=True)
    moved = values - center
    spread = jnp.mean(moved * moved, axis=-1, keepdims=True)
    return (moved * lax.rsqrt(spread + EPSILON)).astype(jnp.bfloat16)


def label_bias(wide, select):
    along = dot_nt(wide, select)[:1]
    down = dot_nt(select, wide)[:, :1]
    return jnp.where(down == along, 0.0, EXCLUDED)


def attend(packed_ref, mixed_ref, first, count, width, heads, bias):
    head_size = width // heads
    lane = lax.broadcasted_iota(jnp.int32, (1, LANES), 1)
    ones = jnp.ones((count, LANES), jnp.bfloat16)
    rows = slice(first, first + count)
    for start in range(0, width, LANES):
        queries = packed_ref[rows, start : start + LANES]
        keys = packed_ref[rows, width + start : width + start + LANES]
        values = packed_ref[rows, 2 * width + start : 2 * width + start + LANES]
        values = jnp.concatenate([values, ones], axis=1)
        mixed = None
        for low in range(0, LANES, head_size):
            own = (lane >= low) & (lane < low + head_size)
            chosen = jnp.where(own, 1.0 / math.sqrt(head_size), 0.0).astype(jnp.bfloat16)
            scores = dot_nt(queries * chosen, keys) + bias
            highest = jnp.max(scores, axis=-1, keepdims=True)
            expos = jnp.exp(scores - highest).astype(jnp.bfloat16)
            summed = dot(expos, values)
            result = summed[:, :LANES] / summed[:, LANES:]
            mixed = result if mixed is None else jnp.where(own, result, mixed)
        mixed_ref[rows, start : start + LANES] = mixed.astype(jnp.bfloat16)


def flat_labels(ids, spread, rows):
    flat = jnp.sum(dot(ids.astype(jnp.bfloat16), spread) * rows.astype(jnp.float32), axis=0, keepdims=True)
    return jnp.broadcast_to(flat, (8, flat.shape[1])).astype(jnp.bfloat16)


def pack_kernel(
    heights, counts, at_ref, x_ref, ids_ref, coarse_ids_ref, spread1, rows1, spread2, rows2,
    pick_lat, pick_lon, pick_both, coarse_lat, coarse_lon, coarse_both, merge_ref, qkv_ref,
    lat_ref, lon_ref, both_ref, labels_ref, coarse_labels_ref, merge_part, qkv_part, sems,
):
    corner = at_ref[0]
    copies = []
    for slot, (whole, part) in enumerate(((merge_ref, merge_part), (qkv_ref, qkv_part))):
        wide = part.shape[1]
        start = pl.multiple_of(corner * wide, LANES)
        copies.append(pltpu.make_async_copy(whole.at[:, pl.ds(start, wide)], part, sems.at[slot]))
        copies[-1].start()

    def labels_of(ref, height):
        row = lax.broadcasted_iota(jnp.int32, ref.shape, 0)
        edge = jnp.zeros(ref.shape, jnp.bool_)
        for level in range(ref.shape[0] // height):
            edge = edge | ((row >= level * height) & (row < level * height + HALF_ROWS))
        return (ref[...] * 2 + jnp.where(edge, at_ref[1], 0)).astype(jnp.float32)

    labels = flat_labels(labels_of(ids_ref, heights[0]), spread1[...], rows1[...])
    coarse_labels = flat_labels(labels_of(coarse_ids_ref, heights[1]), spread2[...], rows2[...])
    labels_ref[...] = labels
    coarse_labels_ref[...] = coarse_labels
    trio = ((pick_lat, coarse_lat, lat_ref), (pick_lon, coarse_lon, lon_ref), (pick_both, coarse_both, both_ref))
    for (pick, coarse_pick, out_ref), count in zip(trio, counts):
        height = out_ref.shape[0]
        body = dot(pick[:height], x_ref[...])
        row = lax.broadcasted_iota(jnp.int32, (height, LANES), 0)
        fine = dot_nt(labels, pick[...])[:1]
        coarse = dot_nt(coarse_labels, coarse_pick[...])[:1]
        extra = jnp.where(row == count, fine, jnp.where(row == count + 1, coarse, 0.0))
        out_ref[:, :LANES] = (body[:, :LANES] + extra).astype(out_ref.dtype)
        out_ref[:, LANES:] = body[:, LANES:].astype(out_ref.dtype)
    for copy in copies:
        copy.wait()


def wide_labels(labels_ref, packets, counts, line):
    count = labels_ref.shape[1]
    pad = up(count, LANES) - count
    parts = [labels_ref[...].astype(jnp.float32)]
    if pad:
        parts[0] = jnp.concatenate([parts[0], jnp.zeros((8, pad), jnp.float32)], axis=1)
    for packet, size in zip(packets, counts):
        block = packet[size // PACK * PACK : size // PACK * PACK + PACK, :LANES].astype(jnp.float32)
        row = lax.broadcasted_iota(jnp.int32, block.shape, 0)
        picked = jnp.sum(jnp.where(row == size % PACK + line, block, 0.0), axis=0, keepdims=True)
        parts.append(jnp.broadcast_to(picked, (8, LANES)))
    return jnp.concatenate(parts, axis=1).astype(jnp.bfloat16)


def first_kernel(
    heads, counts, x_ref, labels_ref, lat_ref, lon_ref, both_ref, select_ref, qkv_ref, out_ref,
    mid_lat, mid_lon, mid_both, skip_lat, skip_lon, skip_both,
    y_ref, mid_lat_out, mid_lon_out, mid_both_out, skip_lat_out, skip_lon_out, skip_both_out,
    stage_ref, rolled_ref, packed_ref, mixed_ref,
):
    width = x_ref.shape[1]
    window = WIN_LEVELS * WIN_ROWS * WIN_COLS
    fill(stage_ref, (x_ref, lat_ref, lon_ref, both_ref))
    wide = wide_labels(labels_ref, (lat_ref, lon_ref, both_ref), counts, 0)
    rolled = dot(select_ref[...], stage_ref[...])
    rolled_ref[...] = rolled
    packed_ref[...] = dot(normalized(rolled), qkv_ref[...]).astype(jnp.bfloat16)
    for first in range(0, x_ref.shape[0], window):
        bias = label_bias(wide, select_ref[first : first + window])
        attend(packed_ref, mixed_ref, first, window, width, heads, bias)
    y_ref[...] = (rolled_ref[...] + dot(mixed_ref[...], out_ref[...])).astype(jnp.bfloat16)
    for pick, packet in (
        (mid_lat, mid_lat_out), (mid_lon, mid_lon_out), (mid_both, mid_both_out),
        (skip_lat, skip_lat_out), (skip_lon, skip_lon_out), (skip_both, skip_both_out),
    ):
        packet[...] = dot(pick[...], y_ref[...]).astype(jnp.bfloat16)


def start_pieces(whole_ref, pieces, at_ref, sem):
    corner, side = at_ref[0], at_ref[2]
    stops, _, rows, columns = whole_ref.shape
    quarter = columns // 4
    copies = []
    for piece, (other, mask, stop) in pieces:
        start = pl.multiple_of((corner ^ mask) * quarter, LANES)
        count = piece.shape[0]
        copies.append(
            pltpu.make_async_copy(
                piece, whole_ref.at[pl.ds(stop, count), side ^ other, :, pl.ds(start, quarter)], sem.at[len(copies)]
            )
        )
        copies[-1].start()
    return copies


def piece_keys(stops):
    half = stops // 2
    keys = [(0, 0), (1, 0), (2, 0), (3, 0), (3, half)]
    return [(other, mask, stop) for other in range(2) for mask, stop in keys]


def merge_kernel(keys, at_ref, y_ref, lat_ref, lon_ref, both_ref, select_ref, *refs):
    pieces, (out_ref, stage_ref, whole_ref, sem) = refs[: len(keys)], refs[len(keys) :]
    copies = start_pieces(whole_ref, list(zip(pieces, keys)), at_ref, sem)
    fill(stage_ref, (y_ref, lat_ref, lon_ref, both_ref))
    cells = out_ref.shape[0]
    patches = [
        dot(select_ref[first : first + cells], stage_ref[...]) for first in range(0, select_ref.shape[0], cells)
    ]
    total = 1.0 / (len(patches) * y_ref.shape[1])
    center = sum(jnp.sum(patch, axis=-1, keepdims=True) for patch in patches) * total
    moved = [patch - center for patch in patches]
    spread = sum(jnp.sum(patch * patch, axis=-1, keepdims=True) for patch in moved) * total
    scale = lax.rsqrt(spread + EPSILON)
    left = jnp.concatenate([(patch * scale).astype(jnp.bfloat16) for patch in moved], axis=1)
    for copy in copies:
        copy.wait()
    stops, sides, rows, columns = whole_ref.shape
    out_ref[...] = dot(left, whole_ref[...].reshape(stops * sides * rows, columns)).astype(jnp.bfloat16)


def second_kernel(
    heads, counts, keys, at_ref, merged_ref, labels_ref, lat_ref, lon_ref, both_ref, select_ref, out_weight,
    end_lat, end_lon, end_both, *refs
):
    pieces = refs[: len(keys)]
    z_ref, lat_out, lon_out, both_out, whole_ref, packed_ref, mixed_ref, sem = refs[len(keys) :]
    copies = start_pieces(whole_ref, list(zip(pieces, keys)), at_ref, sem)
    count, width = merged_ref.shape
    merged = merged_ref[...].astype(jnp.float32)
    left = normalized(merged)
    wide = wide_labels(labels_ref, (lat_ref, lon_ref, both_ref), counts, 1)
    bias = label_bias(wide, select_ref[...])
    for copy in copies:
        copy.wait()
    stops, sides, rows, columns = whole_ref.shape
    packed_ref[...] = dot(left, whole_ref[...].reshape(stops * sides * rows, columns)).astype(jnp.bfloat16)
    attend(packed_ref, mixed_ref, 0, count, width, heads, bias)
    z_ref[...] = (merged + dot(mixed_ref[...], out_weight[...])).astype(jnp.bfloat16)
    for pick, packet in ((end_lat, lat_out), (end_lon, lon_out), (end_both, both_out)):
        packet[...] = dot(pick[...], z_ref[...]).astype(jnp.bfloat16)


def place_kernel(own_ref, lat_ref, lon_ref, both_ref, select_ref, out_ref, stage_ref):
    fill(stage_ref, (own_ref, lat_ref, lon_ref, both_ref))
    out_ref[...] = dot(select_ref[...], stage_ref[...]).astype(out_ref.dtype)


def call(kernel, outs, scratch, *operands, scalars=0, anywhere=(), outs_anywhere=()):
    spaces = []
    for number in range(len(operands)):
        space = pltpu.VMEM
        if number < scalars:
            space = pltpu.SMEM
        elif number in anywhere:
            space = pl.ANY
        spaces.append(pl.BlockSpec(memory_space=space))
    return pl.pallas_call(
        kernel,
        out_shape=[jax.ShapeDtypeStruct(shape, jnp.bfloat16) for shape in outs],
        in_specs=spaces,
        out_specs=[
            pl.BlockSpec(memory_space=pl.ANY if number in outs_anywhere else pltpu.VMEM)
            for number in range(len(outs))
        ],
        scratch_shapes=scratch,
        compiler_params=pltpu.CompilerParams(vmem_limit_bytes=VMEM_LIMIT),
    )(*operands)


def shifted(blocks, step):
    lat, lon = lax.axis_size("lat"), lax.axis_size("lon")
    return (
        lax.ppermute(blocks[0], "lat", [(i, (i + step) % lat) for i in range(lat)]),
        lax.ppermute(blocks[1], "lon", [(i, (i + step) % lon) for i in range(lon)]),
        lax.ppermute(
            blocks[2],
            ("lat", "lon"),
            [(i * lon + j, (i + step) % lat * lon + (j + step) % lon) for i in range(lat) for j in range(lon)],
        ),
    )


def exchange(block, axis, mask):
    return lax.ppermute(block, axis, [(i, i ^ mask) for i in range(lax.axis_size(axis))])


def spread_pieces(part):
    ranks = lax.axis_size("lon")
    stops = ranks // 2
    groups = [[2 * stop + side for stop in range(stops)] for side in range(2)]
    own = lax.all_gather(part, "lon", axis=0, axis_index_groups=groups)
    half = stops // 2
    first = exchange(own, "lat", 1)
    second = exchange(own, "lat", 2)
    pieces = [own, first, second, exchange(first[:half], "lat", 2), exchange(second[half:], "lat", 1)]
    return pieces + [exchange(piece, "lon", 1) for piece in pieces]


def per_device(
    tokens, level_ids, coarse_ids, first_qkv, first_out, merge_weight, second_qkv, second_out
):
    levels, height, breadth, width = tokens.shape
    _, low, narrow = coarse_ids.shape
    wider = merge_weight.shape[1]
    cells, coarse_cells = levels * height * breadth, levels * low * narrow
    window = WIN_LEVELS * WIN_ROWS * WIN_COLS
    stops = lax.axis_size("lon") // 2
    lat, lon = lax.axis_index("lat"), lax.axis_index("lon")
    at = jnp.stack([lat % 4, (lat == 0).astype(jnp.int32), lon % 2]).astype(jnp.int32)

    start = regions(levels, height, breadth, 0, 0)
    middle = regions(levels, height, breadth, HALF_ROWS, HALF_COLS)
    end = regions(levels, low, narrow, 0, 0)
    counts = [len(part) for part in start]
    packet_rows = [up(len(part) + 2, PACK) for part in start]
    end_rows = [up(len(part) + 2, PACK) for part in end]
    order = window_order(levels, height, breadth)
    inverse = np.argsort(order)
    coarse_order = np.arange(coarse_cells)

    def flat_pair(rows, columns):
        index = np.arange(rows * columns)
        return matrix(index % columns, columns).T, matrix(index // columns, rows).T

    x = tokens.reshape(cells, width)
    lat_pk, lon_pk, both_pk, labels, coarse_labels, merge_part, qkv_part = call(
        lambda *refs: pack_kernel((height, low), counts, *refs),
        [(rows, width) for rows in packet_rows]
        + [
            (8, cells),
            (8, coarse_cells),
            (merge_weight.shape[0], wider // 4),
            (second_qkv.shape[0], second_qkv.shape[1] // 4),
        ],
        [pltpu.SemaphoreType.DMA((2,))],
        at,
        x,
        level_ids.reshape(levels * height, breadth),
        coarse_ids.reshape(levels * low, narrow),
        *flat_pair(levels * height, breadth),
        *flat_pair(levels * low, narrow),
        *[matrix(part, cells, LANES) for part in start],
        *[matrix(part, coarse_cells, LANES) for part in end],
        merge_weight,
        second_qkv,
        scalars=1,
        anywhere=(14, 15),
        outs_anywhere=(5, 6),
    )
    got = shifted((lat_pk, lon_pk, both_pk), -1)
    merge_pieces = spread_pieces(merge_part)
    qkv_pieces = spread_pieces(qkv_part)
    out_whole = lax.all_gather(second_out, "lon", axis=0, tiled=True)

    source, depth = replaced(cells, start)
    select = matrix(source[order], depth)
    held = np.empty_like(order)
    held[order] = np.arange(cells)
    y, *packets = call(
        lambda *refs: first_kernel(HEADS1, counts, *refs),
        [(cells, width)] + [(rows, width) for rows in packet_rows] * 2,
        [
            pltpu.VMEM((depth, width), jnp.bfloat16),
            pltpu.VMEM((cells, width), jnp.float32),
            pltpu.VMEM((cells, 3 * width), jnp.bfloat16),
            pltpu.VMEM((cells, width), jnp.bfloat16),
        ],
        x,
        labels,
        *got,
        select,
        first_qkv,
        first_out,
        *[matrix(inverse[part], cells, rows) for part, rows in zip(middle, packet_rows)],
        *[matrix(inverse[part], cells, rows) for part, rows in zip(start, packet_rows)],
    )
    mid = shifted(packets[:3], -1)
    back = shifted(packets[3:], 1)

    source, depth = replaced(cells, middle, held)
    fine = source.reshape(levels, low, 2, narrow, 2)
    patches = [fine[:, :, r, :, c].reshape(-1) for r, c in ((0, 0), (1, 0), (0, 1), (1, 1))]
    keys = piece_keys(stops)
    whole_shape = (stops, 2, merge_weight.shape[0], wider)
    (merged,) = call(
        lambda *refs: merge_kernel(keys, *refs),
        [(coarse_cells, wider)],
        [
            pltpu.VMEM((depth, width), jnp.bfloat16),
            pltpu.VMEM(whole_shape, jnp.bfloat16),
            pltpu.SemaphoreType.DMA((len(keys),)),
        ],
        at,
        y,
        *mid,
        matrix(np.concatenate(patches), depth),
        *merge_pieces,
        scalars=1,
        anywhere=range(6, 6 + len(keys)),
    )

    source, depth = replaced(cells, start, held)
    (skip,) = call(
        place_kernel,
        [(cells, width)],
        [pltpu.VMEM((depth, width), jnp.bfloat16)],
        y,
        *back,
        matrix(source, depth),
    )

    source, depth = replaced(coarse_cells, end)
    z, *packets = call(
        lambda *refs: second_kernel(HEADS2, counts, keys, *refs),
        [(coarse_cells, wider)] + [(rows, wider) for rows in end_rows],
        [
            pltpu.VMEM((stops, 2) + second_qkv.shape, jnp.bfloat16),
            pltpu.VMEM((coarse_cells, 3 * wider), jnp.bfloat16),
            pltpu.VMEM((coarse_cells, wider), jnp.bfloat16),
            pltpu.SemaphoreType.DMA((len(keys),)),
        ],
        at,
        merged,
        coarse_labels,
        *got,
        matrix(source, depth),
        out_whole,
        *[matrix(part, coarse_cells, rows) for part, rows in zip(end, end_rows)],
        *qkv_pieces,
        scalars=1,
        anywhere=range(11, 11 + len(keys)),
    )
    done = shifted(packets, 1)
    (coarse,) = call(
        place_kernel,
        [(coarse_cells, wider)],
        [pltpu.VMEM((depth, wider), jnp.bfloat16)],
        z,
        *done,
        matrix(source, depth),
    )
    return skip.reshape(tokens.shape), coarse.reshape(levels, low, narrow, wider)


def solution(mesh):
    placed = (
        P(None, "lat", "lon", None),
        P(None, "lat", "lon"),
        P(None, "lat", "lon"),
        P(),
        P(),
        P("lon", None),
        P("lon", None),
        P("lon", None),
    )
    return jax.shard_map(
        per_device,
        mesh=mesh,
        in_specs=placed,
        out_specs=(P(None, "lat", "lon", None), P(None, "lat", "lon", None)),
        check_vma=False,
    )
```

```python
import math

import jax
import jax.numpy as jnp
import numpy as np
from jax import lax
from jax.experimental import pallas as pl
from jax.experimental.pallas import tpu as pltpu
from jax.sharding import PartitionSpec as P

HEADS1 = 8
HEADS2 = 16
WIN_LEVELS = 2
WIN_ROWS = 6
WIN_COLS = 12
HALF_ROWS = WIN_ROWS // 2
HALF_COLS = WIN_COLS // 2

EPSILON = 1e-05
EXCLUDED = -1e30
LANES = 128
PACK = 16
VMEM_LIMIT = 32 * 1024 * 1024
NT = (((1,), (1,)), ((), ()))


def up(count, unit):
    return -(-count // unit) * unit


def places(levels, rows, columns):
    return np.arange(levels * rows * columns).reshape(levels, rows, columns)


def regions(levels, rows, columns, row_from, column_from):
    at = places(levels, rows, columns)
    in_rows = (np.arange(rows) >= row_from) & (np.arange(rows) < row_from + HALF_ROWS)
    in_columns = (np.arange(columns) >= column_from) & (np.arange(columns) < column_from + HALF_COLS)
    picked = (
        at[:, in_rows][:, :, ~in_columns],
        at[:, ~in_rows][:, :, in_columns],
        at[:, in_rows][:, :, in_columns],
    )
    return [part.reshape(-1) for part in picked]


def window_order(levels, rows, columns):
    at = places(levels, rows, columns)
    order = []
    for band in range(rows // WIN_ROWS):
        for across in range(columns // WIN_COLS):
            r = (HALF_ROWS + WIN_ROWS * band + np.arange(WIN_ROWS)) % rows
            c = (HALF_COLS + WIN_COLS * across + np.arange(WIN_COLS)) % columns
            order.append(at[:, r][:, :, c].reshape(-1))
    return np.concatenate(order)


def matrix(sources, columns, height=None):
    out = np.zeros((height or len(sources), columns), np.float32)
    out[np.arange(len(sources)), sources] = 1
    return jnp.asarray(out, jnp.bfloat16)


def offsets(sizes):
    return np.concatenate([[0], np.cumsum([up(size, LANES) for size in sizes])]).tolist()


def replaced(count, parts, held=None):
    starts = offsets([count] + [up(len(part) + 2, PACK) for part in parts])
    source = np.arange(count) if held is None else held.copy()
    for start, part in zip(starts[1:], parts):
        source[part] = start + np.arange(len(part))
    return source, starts[-1]


def fill(stage_ref, parts, held=0):
    start = 0
    for part in parts:
        rows = held if part is None else part.shape[0]
        if part is not None:
            stage_ref[start : start + rows] = part[...]
        if rows % LANES:
            stage_ref[start + rows : start + up(rows, LANES)] = jnp.zeros(
                (up(rows, LANES) - rows, stage_ref.shape[1]), stage_ref.dtype
            )
        start += up(rows, LANES)


def dot(left, right):
    return jnp.dot(left, right, preferred_element_type=jnp.float32)


def dot_nt(left, right):
    return lax.dot_general(left, right, NT, preferred_element_type=jnp.float32)


def normalized(values):
    center = jnp.mean(values, axis=-1, keepdims=True)
    moved = values - center
    spread = jnp.mean(moved * moved, axis=-1, keepdims=True)
    return (moved * lax.rsqrt(spread + EPSILON)).astype(jnp.bfloat16)


def label_bias(wide, select):
    along = dot_nt(wide, select)[:1]
    down = dot_nt(select, wide)[:, :1]
    return jnp.where(down == along, 0.0, EXCLUDED)


def attend(packed_ref, mixed_ref, first, count, width, heads, bias):
    head_size = width // heads
    lane = lax.broadcasted_iota(jnp.int32, (1, LANES), 1)
    ones = jnp.ones((count, LANES), jnp.bfloat16)
    rows = slice(first, first + count)
    for start in range(0, width, LANES):
        queries = packed_ref[rows, start : start + LANES]
        keys = packed_ref[rows, width + start : width + start + LANES]
        values = packed_ref[rows, 2 * width + start : 2 * width + start + LANES]
        values = jnp.concatenate([values, ones], axis=1)
        mixed = None
        for low in range(0, LANES, head_size):
            own = (lane >= low) & (lane < low + head_size)
            chosen = jnp.where(own, 1.0 / math.sqrt(head_size), 0.0).astype(jnp.bfloat16)
            scores = dot_nt(queries * chosen, keys) + bias
            highest = jnp.max(scores, axis=-1, keepdims=True)
            expos = jnp.exp(scores - highest).astype(jnp.bfloat16)
            summed = dot(expos, values)
            result = summed[:, :LANES] / summed[:, LANES:]
            mixed = result if mixed is None else jnp.where(own, result, mixed)
        mixed_ref[rows, start : start + LANES] = mixed.astype(jnp.bfloat16)


def fetch(sems, *pairs):
    copies = [pltpu.make_async_copy(source, target, sems.at[n]) for n, (source, target) in enumerate(pairs)]
    for copy in copies:
        copy.start()
    return copies


def flat_labels(ids_ref, edge, spread):
    levels, rows, columns = ids_ref.shape
    total = 0.0
    for level in range(levels):
        row = lax.broadcasted_iota(jnp.int32, (rows, columns), 0)
        labels = ids_ref[level] * 2 + jnp.where(row < HALF_ROWS, edge, 0)
        wide = dot(labels.astype(jnp.float32).astype(jnp.bfloat16), spread)
        place = lax.broadcasted_iota(jnp.int32, wide.shape, 1)
        low = (level * rows + lax.broadcasted_iota(jnp.int32, wide.shape, 0)) * columns
        own = (place >= low) & (place < low + columns)
        total += jnp.sum(jnp.where(own, wide, 0.0), axis=0, keepdims=True)
    return jnp.broadcast_to(total, (8, total.shape[1])).astype(jnp.bfloat16)


def pack_kernel(
    counts, at_ref, x_hbm, ids_hbm, coarse_ids_hbm, fine_hbm, coarse_hbm, *refs
):
    wholes, refs = refs[:3], refs[3:]
    outs, labels_ref, coarse_labels_ref, parts = refs[:3], refs[3], refs[4], refs[5:8]
    x_ref, ids_ref, coarse_ids_ref, fine_ref, coarse_ref, sems = refs[8:]
    corner, edge = at_ref[0], at_ref[1]
    loads = fetch(
        sems,
        (ids_hbm, ids_ref),
        (coarse_ids_hbm, coarse_ids_ref),
        (coarse_hbm, coarse_ref),
        (fine_hbm, fine_ref),
        (x_hbm, x_ref),
    )
    copies = []
    for whole, part in zip(wholes, parts):
        wide = part.shape[1]
        start = pl.multiple_of(corner * wide, LANES)
        copies.append(
            pltpu.make_async_copy(whole.at[:, pl.ds(start, wide)], part, sems.at[len(loads) + len(copies)])
        )
        copies[-1].start()
    for load in loads[:4]:
        load.wait()
    picks = 3 * LANES
    labels = flat_labels(ids_ref, edge, fine_ref[picks : picks + ids_ref.shape[2]])
    coarse_labels = flat_labels(coarse_ids_ref, edge, coarse_ref[picks : picks + coarse_ids_ref.shape[2]])
    labels_ref[...] = labels
    coarse_labels_ref[...] = coarse_labels
    loads[4].wait()
    for number, (out_ref, count) in enumerate(zip(outs, counts)):
        height = out_ref.shape[0]
        first = number * LANES
        body = dot(fine_ref[first : first + height], x_ref[...])
        row = lax.broadcasted_iota(jnp.int32, (height, LANES), 0)
        fine = dot_nt(labels, fine_ref[first : first + LANES])[:1]
        coarse = dot_nt(coarse_labels, coarse_ref[first : first + LANES])[:1]
        extra = jnp.where(row == count, fine, jnp.where(row == count + 1, coarse, 0.0))
        out_ref[:, :LANES] = (body[:, :LANES] + extra).astype(out_ref.dtype)
        out_ref[:, LANES:] = body[:, LANES:].astype(out_ref.dtype)
    for copy in copies:
        copy.wait()


def wide_labels(labels_ref, packets, counts, line):
    count = labels_ref.shape[1]
    pad = up(count, LANES) - count
    parts = [labels_ref[...].astype(jnp.float32)]
    if pad:
        parts[0] = jnp.concatenate([parts[0], jnp.zeros((8, pad), jnp.float32)], axis=1)
    for packet, size in zip(packets, counts):
        block = packet[size // PACK * PACK : size // PACK * PACK + PACK, :LANES].astype(jnp.float32)
        row = lax.broadcasted_iota(jnp.int32, block.shape, 0)
        picked = jnp.sum(jnp.where(row == size % PACK + line, block, 0.0), axis=0, keepdims=True)
        parts.append(jnp.broadcast_to(picked, (8, LANES)))
    return jnp.concatenate(parts, axis=1).astype(jnp.bfloat16)


def first_kernel(
    heads, counts, x_hbm, select_hbm, qkv_hbm, out_hbm, pick_hbm,
    labels_ref, lat_ref, lon_ref, both_ref, y_ref, *refs,
):
    packets, refs = refs[:6], refs[6:]
    select_ref, qkv_ref, out_ref, pick_ref, stage_ref, rolled_ref, packed_ref, mixed_ref, sems = refs
    cells, width = x_hbm.shape
    window = WIN_LEVELS * WIN_ROWS * WIN_COLS
    loads = fetch(
        sems,
        (x_hbm, stage_ref.at[pl.ds(0, cells)]),
        (select_hbm, select_ref),
        (qkv_hbm, qkv_ref),
        (out_hbm, out_ref),
        (pick_hbm, pick_ref),
    )
    fill(stage_ref, (None, lat_ref, lon_ref, both_ref), cells)
    wide = wide_labels(labels_ref, (lat_ref, lon_ref, both_ref), counts, 0)
    loads[0].wait()
    loads[1].wait()
    rolled = dot(select_ref[...], stage_ref[...])
    rolled_ref[...] = rolled
    loads[2].wait()
    packed_ref[...] = dot(normalized(rolled), qkv_ref[...]).astype(jnp.bfloat16)
    for first in range(0, cells, window):
        bias = label_bias(wide, select_ref[first : first + window])
        attend(packed_ref, mixed_ref, first, window, width, heads, bias)
    loads[3].wait()
    y_ref[...] = (rolled_ref[...] + dot(mixed_ref[...], out_ref[...])).astype(jnp.bfloat16)
    loads[4].wait()
    first = 0
    for packet in packets:
        height = packet.shape[0]
        packet[...] = dot(pick_ref[first : first + height], y_ref[...]).astype(jnp.bfloat16)
        first += height


def join_kernel(*refs):
    parts, (out_ref, sems) = refs[:-2], refs[-2:]
    copies = fetch(sems, *[(part, out_ref.at[number]) for number, part in enumerate(parts)])
    for copy in copies:
        copy.wait()


def start_pieces(whole_ref, pieces, at_ref, sems):
    corner, side, here = at_ref[0], at_ref[2], at_ref[3]
    stops, _, _, columns = whole_ref.shape
    quarter = columns // 4
    copies = []
    for number, piece in enumerate(pieces):
        other, mask = number // 5, number % 5 - 1
        held = whole_ref.at[:, side ^ other]
        if mask < 0:
            pairs = [(piece, held.at[here])]
        else:
            start = pl.multiple_of((corner ^ mask) * quarter, LANES)
            pairs = [
                (piece.at[back - 1], held.at[lax.rem(here + (stops - back), stops), :, pl.ds(start, quarter)])
                for back in range(1, stops)
            ]
        for source, target in pairs:
            copies.append(pltpu.make_async_copy(source, target, sems.at[len(copies)]))
            copies[-1].start()
    return copies


def piece_copies(stops):
    return 2 * (1 + 4 * (stops - 1))


def flat(whole_ref):
    stops, sides, rows, columns = whole_ref.shape
    return whole_ref[...].reshape(stops * sides * rows, columns)


def merge_kernel(at_ref, select_hbm, *refs):
    pieces, (y_ref, lat_ref, lon_ref, both_ref, out_ref) = refs[:10], refs[10:15]
    select_ref, stage_ref, whole_ref, sems, piece_sems = refs[15:]
    loads = fetch(sems, (select_hbm, select_ref))
    copies = start_pieces(whole_ref, pieces, at_ref, piece_sems)
    fill(stage_ref, (y_ref, lat_ref, lon_ref, both_ref))
    cells = out_ref.shape[0]
    loads[0].wait()
    patches = [
        dot(select_ref[first : first + cells], stage_ref[...]) for first in range(0, select_ref.shape[0], cells)
    ]
    total = 1.0 / (len(patches) * y_ref.shape[1])
    center = sum(jnp.sum(patch, axis=-1, keepdims=True) for patch in patches) * total
    moved = [patch - center for patch in patches]
    spread = sum(jnp.sum(patch * patch, axis=-1, keepdims=True) for patch in moved) * total
    scale = lax.rsqrt(spread + EPSILON)
    left = jnp.concatenate([(patch * scale).astype(jnp.bfloat16) for patch in moved], axis=1)
    for copy in copies:
        copy.wait()
    out_ref[...] = dot(left, flat(whole_ref)).astype(jnp.bfloat16)


def second_kernel(heads, counts, at_ref, select_hbm, *refs):
    pieces, (merged_ref, labels_ref, lat_ref, lon_ref, both_ref, mixed_ref) = refs[:10], refs[10:16]
    select_ref, whole_ref, packed_ref, sems, piece_sems = refs[16:]
    loads = fetch(sems, (select_hbm, select_ref))
    copies = start_pieces(whole_ref, pieces, at_ref, piece_sems)
    count, width = merged_ref.shape
    left = normalized(merged_ref[...].astype(jnp.float32))
    wide = wide_labels(labels_ref, (lat_ref, lon_ref, both_ref), counts, 1)
    loads[0].wait()
    bias = label_bias(wide, select_ref[...])
    for copy in copies:
        copy.wait()
    packed_ref[...] = dot(left, flat(whole_ref)).astype(jnp.bfloat16)
    attend(packed_ref, mixed_ref, 0, count, width, heads, bias)


def close_kernel(at_ref, pick_hbm, *refs):
    pieces, (merged_ref, mixed_ref, z_ref), packets = refs[:10], refs[10:13], refs[13:16]
    pick_ref, whole_ref, sems, piece_sems = refs[16:]
    copies = fetch(sems, (pick_hbm, pick_ref)) + start_pieces(whole_ref, pieces, at_ref, piece_sems)
    for copy in copies:
        copy.wait()
    result = merged_ref[...].astype(jnp.float32) + dot(mixed_ref[...], flat(whole_ref))
    z_ref[...] = result.astype(jnp.bfloat16)
    first = 0
    for packet in packets:
        height = packet.shape[0]
        packet[...] = dot(pick_ref[first : first + height], z_ref[...]).astype(jnp.bfloat16)
        first += height


def place_kernel(select_hbm, own_ref, lat_ref, lon_ref, both_ref, out_ref, select_ref, stage_ref, sems):
    loads = fetch(sems, (select_hbm, select_ref))
    fill(stage_ref, (own_ref, lat_ref, lon_ref, both_ref))
    loads[0].wait()
    out_ref[...] = dot(select_ref[...], stage_ref[...]).astype(out_ref.dtype)


def call(kernel, outs, scratch, scalars=(), hbm=(), vmem=(), hbm_outs=()):
    spaces = [pltpu.SMEM] * len(scalars) + [pltpu.HBM] * len(hbm) + [pltpu.VMEM] * len(vmem)
    return pl.pallas_call(
        kernel,
        out_shape=[jax.ShapeDtypeStruct(shape, jnp.bfloat16) for shape in outs],
        in_specs=[pl.BlockSpec(memory_space=space) for space in spaces],
        out_specs=[
            pl.BlockSpec(memory_space=pltpu.HBM if number in hbm_outs else pltpu.VMEM)
            for number in range(len(outs))
        ],
        scratch_shapes=scratch,
        compiler_params=pltpu.CompilerParams(vmem_limit_bytes=VMEM_LIMIT),
    )(*scalars, *hbm, *vmem)


def shifted(blocks, step):
    lat, lon = lax.axis_size("lat"), lax.axis_size("lon")
    return (
        lax.ppermute(blocks[0], "lat", [(i, (i + step) % lat) for i in range(lat)]),
        lax.ppermute(blocks[1], "lon", [(i, (i + step) % lon) for i in range(lon)]),
        lax.ppermute(
            blocks[2],
            ("lat", "lon"),
            [(i * lon + j, (i + step) % lat * lon + (j + step) % lon) for i in range(lat) for j in range(lon)],
        ),
    )


def exchange(block, axis, mask):
    return lax.ppermute(block, axis, [(i, i ^ mask) for i in range(lax.axis_size(axis))])


def spread_pieces(shard, part, by_first):
    ranks = lax.axis_size("lon")
    stops = ranks // 2
    far = [
        lax.ppermute(part, "lon", [(i, (i + 2 * back) % ranks) for i in range(ranks)]) for back in range(1, stops)
    ]
    (near,) = call(
        join_kernel,
        [(stops - 1,) + part.shape],
        [pltpu.SemaphoreType.DMA((stops - 1,))],
        hbm=far,
        hbm_outs=(0,),
    )
    first = exchange(near, "lat", 1)
    second = exchange(near, "lat", 2)
    third = exchange(first, "lat", 2) if by_first else exchange(second, "lat", 1)
    pieces = [shard, near, first, second, third]
    return pieces + [exchange(piece, "lon", 1) for piece in pieces]


def dma(count):
    return pltpu.SemaphoreType.DMA((count,))


def bf16(*shape):
    return pltpu.VMEM(shape, jnp.bfloat16)


def per_device(
    tokens, level_ids, coarse_ids, first_qkv, first_out, merge_weight, second_qkv, second_out
):
    levels, height, breadth, width = tokens.shape
    _, low, narrow = coarse_ids.shape
    wider = merge_weight.shape[1]
    cells, coarse_cells = levels * height * breadth, levels * low * narrow
    stops = lax.axis_size("lon") // 2
    lat, lon = lax.axis_index("lat"), lax.axis_index("lon")
    at = jnp.stack([lat % 4, (lat == 0).astype(jnp.int32), lon % 2, lon // 2]).astype(jnp.int32)

    start = regions(levels, height, breadth, 0, 0)
    middle = regions(levels, height, breadth, HALF_ROWS, HALF_COLS)
    end = regions(levels, low, narrow, 0, 0)
    counts = [len(part) for part in start]
    packet_rows = [up(len(part) + 2, PACK) for part in start]
    end_rows = [up(len(part) + 2, PACK) for part in end]
    order = window_order(levels, height, breadth)
    inverse = np.argsort(order)
    weights = (merge_weight, second_qkv, second_out)

    def picks(parts, rows, columns):
        return [matrix(part, columns, count) for part, count in zip(parts, rows)]

    def spreader(columns, count):
        return matrix(np.arange(count) % columns, up(columns, PACK)).T

    fine = jnp.concatenate(picks(start, [LANES] * 3, cells) + [spreader(breadth, cells)])
    coarse = jnp.concatenate(picks(end, [LANES] * 3, coarse_cells) + [spreader(narrow, coarse_cells)])
    x = tokens.reshape(cells, width)
    *packets, labels, coarse_labels, merge_part, qkv_part, out_part = call(
        lambda *refs: pack_kernel(counts, *refs),
        [(rows, width) for rows in packet_rows]
        + [(8, cells), (8, coarse_cells)]
        + [(weight.shape[0], weight.shape[1] // 4) for weight in weights],
        [
            bf16(cells, width),
            pltpu.VMEM(level_ids.shape, jnp.int32),
            pltpu.VMEM(coarse_ids.shape, jnp.int32),
            bf16(*fine.shape),
            bf16(*coarse.shape),
            dma(8),
        ],
        scalars=(at,),
        hbm=(x, level_ids, coarse_ids, fine, coarse, *weights),
        hbm_outs=(5, 6, 7),
    )
    got = shifted(packets, -1)
    merge_pieces = spread_pieces(merge_weight, merge_part, True)
    qkv_pieces = spread_pieces(second_qkv, qkv_part, False)
    out_pieces = spread_pieces(second_out, out_part, True)

    source, depth = replaced(cells, start)
    held = np.empty_like(order)
    held[order] = np.arange(cells)
    select = matrix(source[order], depth)
    pick = jnp.concatenate(
        picks([inverse[part] for part in middle], packet_rows, cells)
        + picks([inverse[part] for part in start], packet_rows, cells)
    )
    y, *packets = call(
        lambda *refs: first_kernel(HEADS1, counts, *refs),
        [(cells, width)] + [(rows, width) for rows in packet_rows] * 2,
        [
            bf16(*select.shape),
            bf16(*first_qkv.shape),
            bf16(*first_out.shape),
            bf16(*pick.shape),
            bf16(depth, width),
            pltpu.VMEM((cells, width), jnp.float32),
            bf16(cells, 3 * width),
            bf16(cells, width),
            dma(5),
        ],
        hbm=(x, select, first_qkv, first_out, pick),
        vmem=(labels, *got),
    )
    mid = shifted(packets[:3], -1)
    back = shifted(packets[3:], 1)

    source, depth = replaced(cells, middle, held)
    fine = source.reshape(levels, low, 2, narrow, 2)
    patches = [fine[:, :, r, :, c].reshape(-1) for r, c in ((0, 0), (1, 0), (0, 1), (1, 1))]
    select = matrix(np.concatenate(patches), depth)
    (merged,) = call(
        merge_kernel,
        [(coarse_cells, wider)],
        [
            bf16(*select.shape),
            bf16(depth, width),
            bf16(stops, 2, *merge_weight.shape),
            dma(1),
            dma(piece_copies(stops)),
        ],
        scalars=(at,),
        hbm=(select, *merge_pieces),
        vmem=(y, *mid),
    )

    source, depth = replaced(cells, start, held)
    select = matrix(source, depth)
    (skip,) = call(
        place_kernel,
        [(cells, width)],
        [bf16(*select.shape), bf16(depth, width), dma(1)],
        hbm=(select,),
        vmem=(y, *back),
    )

    source, depth = replaced(coarse_cells, end)
    select = matrix(source, depth)
    (mixed,) = call(
        lambda *refs: second_kernel(HEADS2, counts, *refs),
        [(coarse_cells, wider)],
        [
            bf16(*select.shape),
            bf16(stops, 2, *second_qkv.shape),
            bf16(coarse_cells, 3 * wider),
            dma(1),
            dma(piece_copies(stops)),
        ],
        scalars=(at,),
        hbm=(select, *qkv_pieces),
        vmem=(merged, coarse_labels, *got),
    )
    pick = jnp.concatenate(picks(end, end_rows, coarse_cells))
    z, *packets = call(
        close_kernel,
        [(coarse_cells, wider)] + [(rows, wider) for rows in end_rows],
        [
            bf16(*pick.shape),
            bf16(stops, 2, *second_out.shape),
            dma(1),
            dma(piece_copies(stops)),
        ],
        scalars=(at,),
        hbm=(pick, *out_pieces),
        vmem=(merged, mixed),
    )
    done = shifted(packets, 1)
    (coarse,) = call(
        place_kernel,
        [(coarse_cells, wider)],
        [bf16(*select.shape), bf16(depth, wider), dma(1)],
        hbm=(select,),
        vmem=(z, *done),
    )
    return skip.reshape(tokens.shape), coarse.reshape(levels, low, narrow, wider)


def solution(mesh):
    placed = (
        P(None, "lat", "lon", None),
        P(None, "lat", "lon"),
        P(None, "lat", "lon"),
        P(),
        P(),
        P("lon", None),
        P("lon", None),
        P("lon", None),
    )
    return jax.shard_map(
        per_device,
        mesh=mesh,
        in_specs=placed,
        out_specs=(P(None, "lat", "lon", None), P(None, "lat", "lon", None)),
        check_vma=False,
    )
```

```python
import math

import jax
import jax.numpy as jnp
import numpy as np
from jax import lax
from jax.experimental import pallas as pl
from jax.experimental.pallas import tpu as pltpu
from jax.sharding import PartitionSpec as P

HEADS1 = 8
HEADS2 = 16
WIN_LEVELS = 2
WIN_ROWS = 6
WIN_COLS = 12
HALF_ROWS = WIN_ROWS // 2
HALF_COLS = WIN_COLS // 2

EPSILON = 1e-05
EXCLUDED = -1e30
LANES = 128
PACK = 16
VMEM_LIMIT = 32 * 1024 * 1024
NT = (((1,), (1,)), ((), ()))


def up(count, unit):
    return -(-count // unit) * unit


def places(levels, rows, columns):
    return np.arange(levels * rows * columns).reshape(levels, rows, columns)


def regions(levels, rows, columns, row_from, column_from):
    at = places(levels, rows, columns)
    in_rows = (np.arange(rows) >= row_from) & (np.arange(rows) < row_from + HALF_ROWS)
    in_columns = (np.arange(columns) >= column_from) & (np.arange(columns) < column_from + HALF_COLS)
    picked = (
        at[:, in_rows][:, :, ~in_columns],
        at[:, ~in_rows][:, :, in_columns],
        at[:, in_rows][:, :, in_columns],
    )
    return [part.reshape(-1) for part in picked]


def window_order(levels, rows, columns):
    at = places(levels, rows, columns)
    order = []
    for band in range(rows // WIN_ROWS):
        for across in range(columns // WIN_COLS):
            r = (HALF_ROWS + WIN_ROWS * band + np.arange(WIN_ROWS)) % rows
            c = (HALF_COLS + WIN_COLS * across + np.arange(WIN_COLS)) % columns
            order.append(at[:, r][:, :, c].reshape(-1))
    return np.concatenate(order)


def matrix(sources, columns, height=None):
    out = np.zeros((height or len(sources), columns), np.float32)
    out[np.arange(len(sources)), sources] = 1
    return jnp.asarray(out, jnp.bfloat16)


def offsets(sizes):
    return np.concatenate([[0], np.cumsum([up(size, LANES) for size in sizes])]).tolist()


def replaced(count, parts, held=None):
    starts = offsets([count] + [up(len(part) + 2, PACK) for part in parts])
    source = np.arange(count) if held is None else held.copy()
    for start, part in zip(starts[1:], parts):
        source[part] = start + np.arange(len(part))
    return source, starts[-1]


def fill(stage_ref, parts, held=0):
    start = 0
    for part in parts:
        rows = held if part is None else part.shape[0]
        if part is not None:
            stage_ref[start : start + rows] = part[...]
        if rows % LANES:
            stage_ref[start + rows : start + up(rows, LANES)] = jnp.zeros(
                (up(rows, LANES) - rows, stage_ref.shape[1]), stage_ref.dtype
            )
        start += up(rows, LANES)


def dot(left, right):
    return jnp.dot(left, right, preferred_element_type=jnp.float32)


def dot_nt(left, right):
    return lax.dot_general(left, right, NT, preferred_element_type=jnp.float32)


def normalized(values):
    center = jnp.mean(values, axis=-1, keepdims=True)
    moved = values - center
    spread = jnp.mean(moved * moved, axis=-1, keepdims=True)
    return (moved * lax.rsqrt(spread + EPSILON)).astype(jnp.bfloat16)


def label_bias(wide, select):
    along = dot_nt(wide, select)[:1]
    down = dot_nt(select, wide)[:, :1]
    return jnp.where(down == along, 0.0, EXCLUDED)


def lane_heads(width, heads):
    head_size = width // heads
    lane = lax.broadcasted_iota(jnp.int32, (1, LANES), 1)
    for start in range(0, width, LANES):
        yield start, [
            ((start + low) // head_size, (lane >= low) & (lane < low + head_size))
            for low in range(0, LANES, head_size)
        ]


def head_expos(queries, keys, own, head_size, bias):
    chosen = jnp.where(own, 1.0 / math.sqrt(head_size), 0.0).astype(jnp.bfloat16)
    scores = dot_nt(queries * chosen, keys) + bias
    highest = jnp.max(scores, axis=-1, keepdims=True)
    return jnp.exp(scores - highest).astype(jnp.bfloat16)


def head_mix(expos, values, own, mixed):
    summed = dot(expos, values)
    result = summed[:, :LANES] / summed[:, LANES:]
    return result if mixed is None else jnp.where(own, result, mixed)


def with_ones(values):
    return jnp.concatenate([values, jnp.ones(values.shape, values.dtype)], axis=1)


def attend(packed_ref, mixed_ref, first, count, width, heads, bias):
    rows = slice(first, first + count)
    for start, members in lane_heads(width, heads):
        queries = packed_ref[rows, start : start + LANES]
        keys = packed_ref[rows, width + start : width + start + LANES]
        values = with_ones(packed_ref[rows, 2 * width + start : 2 * width + start + LANES])
        mixed = None
        for _, own in members:
            expos = head_expos(queries, keys, own, width // heads, bias)
            mixed = head_mix(expos, values, own, mixed)
        mixed_ref[rows, start : start + LANES] = mixed.astype(jnp.bfloat16)


def fetch(sems, *pairs):
    copies = [pltpu.make_async_copy(source, target, sems.at[n]) for n, (source, target) in enumerate(pairs)]
    for copy in copies:
        copy.start()
    return copies


def flat_labels(ids_ref, edge, spread):
    rows, levels, columns = ids_ref.shape
    total = 0.0
    for level in range(levels):
        row = lax.broadcasted_iota(jnp.int32, (rows, columns), 0)
        labels = ids_ref[:, level, :] * 2 + jnp.where(row < HALF_ROWS, edge, 0)
        wide = dot(labels.astype(jnp.float32).astype(jnp.bfloat16), spread)
        place = lax.broadcasted_iota(jnp.int32, wide.shape, 1)
        low = (level * rows + lax.broadcasted_iota(jnp.int32, wide.shape, 0)) * columns
        own = (place >= low) & (place < low + columns)
        total += jnp.sum(jnp.where(own, wide, 0.0), axis=0, keepdims=True)
    return jnp.broadcast_to(total, (8, total.shape[1])).astype(jnp.bfloat16)


def quarters_kernel(at_ref, merge_ref, qkv_ref, out_ref, merge_part, score_part, value_part, sems):
    corner = at_ref[0]
    wide = out_ref.shape[1] // 4

    def quarter(ref, first, columns):
        start = pl.multiple_of(first + corner * columns, LANES)
        return ref.at[:, pl.ds(start, columns)]

    copies = fetch(
        sems,
        (quarter(merge_ref, 0, merge_part.shape[1]), merge_part),
        (quarter(qkv_ref, 0, 2 * wide), score_part),
        (quarter(qkv_ref, 8 * wide, wide), value_part.at[:, pl.ds(0, wide)]),
        (quarter(out_ref, 0, wide), value_part.at[:, pl.ds(wide, wide)]),
    )
    for copy in copies:
        copy.wait()


def pack_kernel(counts, at_ref, x_hbm, ids_hbm, coarse_ids_hbm, fine_hbm, coarse_hbm, qkv_ref, out_ref, *refs):
    outs, labels_ref, coarse_labels_ref, score_own, value_own = refs[:3], refs[3], refs[4], refs[5], refs[6]
    x_ref, ids_ref, coarse_ids_ref, fine_ref, coarse_ref, sems = refs[7:]
    edge = at_ref[1]
    wide = out_ref.shape[1] // 4
    pairs = [(qkv_ref.at[:, pl.ds(0, 8 * wide)], score_own)]
    for number in range(4):
        pairs.append((qkv_ref.at[:, pl.ds((8 + number) * wide, wide)], value_own.at[:, pl.ds(2 * number * wide, wide)]))
        pairs.append((out_ref.at[:, pl.ds(number * wide, wide)], value_own.at[:, pl.ds((2 * number + 1) * wide, wide)]))
    copies = fetch(
        sems,
        (ids_hbm, ids_ref),
        (coarse_ids_hbm, coarse_ids_ref),
        (coarse_hbm, coarse_ref),
        (fine_hbm, fine_ref),
        (x_hbm, x_ref),
        *pairs,
    )
    for load in copies[:4]:
        load.wait()
    picks = 3 * LANES
    labels = flat_labels(ids_ref, edge, fine_ref[picks : picks + ids_ref.shape[2]])
    coarse_labels = flat_labels(coarse_ids_ref, edge, coarse_ref[picks : picks + coarse_ids_ref.shape[2]])
    labels_ref[...] = labels
    coarse_labels_ref[...] = coarse_labels
    copies[4].wait()
    for number, (packet, count) in enumerate(zip(outs, counts)):
        height = packet.shape[0]
        first = number * LANES
        body = dot(fine_ref[first : first + height], x_ref[...])
        row = lax.broadcasted_iota(jnp.int32, (height, LANES), 0)
        fine = dot_nt(labels, fine_ref[first : first + LANES])[:1]
        coarse = dot_nt(coarse_labels, coarse_ref[first : first + LANES])[:1]
        extra = jnp.where(row == count, fine, jnp.where(row == count + 1, coarse, 0.0))
        packet[:, :LANES] = (body[:, :LANES] + extra).astype(packet.dtype)
        packet[:, LANES:] = body[:, LANES:].astype(packet.dtype)
    for copy in copies[5:]:
        copy.wait()


def wide_labels(labels_ref, packets, counts, line):
    count = labels_ref.shape[1]
    pad = up(count, LANES) - count
    parts = [labels_ref[...].astype(jnp.float32)]
    if pad:
        parts[0] = jnp.concatenate([parts[0], jnp.zeros((8, pad), jnp.float32)], axis=1)
    for packet, size in zip(packets, counts):
        block = packet[size // PACK * PACK : size // PACK * PACK + PACK, :LANES].astype(jnp.float32)
        row = lax.broadcasted_iota(jnp.int32, block.shape, 0)
        picked = jnp.sum(jnp.where(row == size % PACK + line, block, 0.0), axis=0, keepdims=True)
        parts.append(jnp.broadcast_to(picked, (8, LANES)))
    return jnp.concatenate(parts, axis=1).astype(jnp.bfloat16)


def first_kernel(
    heads, counts, x_hbm, select_hbm, qkv_hbm, out_hbm, pick_hbm,
    labels_ref, lat_ref, lon_ref, both_ref, y_ref, *refs,
):
    packets, refs = refs[:6], refs[6:]
    select_ref, qkv_ref, out_ref, pick_ref, stage_ref, rolled_ref, packed_ref, mixed_ref, sems = refs
    cells, width = x_hbm.shape
    window = WIN_LEVELS * WIN_ROWS * WIN_COLS
    loads = fetch(
        sems,
        (x_hbm, stage_ref.at[pl.ds(0, cells)]),
        (select_hbm, select_ref),
        (qkv_hbm, qkv_ref),
        (out_hbm, out_ref),
        (pick_hbm, pick_ref),
    )
    fill(stage_ref, (None, lat_ref, lon_ref, both_ref), cells)
    wide = wide_labels(labels_ref, (lat_ref, lon_ref, both_ref), counts, 0)
    loads[0].wait()
    loads[1].wait()
    rolled = dot(select_ref[...], stage_ref[...])
    rolled_ref[...] = rolled
    loads[2].wait()
    packed_ref[...] = dot(normalized(rolled), qkv_ref[...]).astype(jnp.bfloat16)
    for first in range(0, cells, window):
        bias = label_bias(wide, select_ref[first : first + window])
        attend(packed_ref, mixed_ref, first, window, width, heads, bias)
    loads[3].wait()
    y_ref[...] = (rolled_ref[...] + dot(mixed_ref[...], out_ref[...])).astype(jnp.bfloat16)
    loads[4].wait()
    first = 0
    for packet in packets:
        height = packet.shape[0]
        packet[...] = dot(pick_ref[first : first + height], y_ref[...]).astype(jnp.bfloat16)
        first += height


def join_kernel(*refs):
    parts, (out_ref, sems) = refs[:-2], refs[-2:]
    copies = fetch(sems, *[(part, out_ref.at[number]) for number, part in enumerate(parts)])
    for copy in copies:
        copy.wait()


def start_pieces(whole_ref, pieces, at_ref, sems):
    corner, side, here = at_ref[0], at_ref[2], at_ref[3]
    stops, _, _, columns = whole_ref.shape
    quarter = columns // 4
    copies = []
    for number, piece in enumerate(pieces):
        other, kind = number // 5, number % 5
        from_side = side ^ other
        held = whole_ref.at[:, from_side]
        mask = (None, 0, 1 + from_side, 2 - from_side, 3)[kind]
        if mask is None:
            pairs = [(piece, held.at[here])]
        else:
            start = pl.multiple_of((corner ^ mask) * quarter, LANES)
            pairs = [
                (piece.at[back - 1], held.at[lax.rem(here + (stops - back), stops), :, pl.ds(start, quarter)])
                for back in range(1, stops)
            ]
        for source, target in pairs:
            copies.append(pltpu.make_async_copy(source, target, sems.at[len(copies)]))
            copies[-1].start()
    return copies


def piece_copies(stops):
    return 2 * (1 + 4 * (stops - 1))


def flat(whole_ref):
    stops, sides, rows, columns = whole_ref.shape
    return whole_ref[...].reshape(stops * sides * rows, columns)


def merge_kernel(at_ref, select_hbm, *refs):
    pieces, (y_ref, lat_ref, lon_ref, both_ref, out_ref) = refs[:10], refs[10:15]
    select_ref, stage_ref, whole_ref, sems, piece_sems = refs[15:]
    loads = fetch(sems, (select_hbm, select_ref))
    copies = start_pieces(whole_ref, pieces, at_ref, piece_sems)
    fill(stage_ref, (y_ref, lat_ref, lon_ref, both_ref))
    cells = out_ref.shape[0]
    loads[0].wait()
    patches = [
        dot(select_ref[first : first + cells], stage_ref[...]) for first in range(0, select_ref.shape[0], cells)
    ]
    total = 1.0 / (len(patches) * y_ref.shape[1])
    center = sum(jnp.sum(patch, axis=-1, keepdims=True) for patch in patches) * total
    moved = [patch - center for patch in patches]
    spread = sum(jnp.sum(patch * patch, axis=-1, keepdims=True) for patch in moved) * total
    scale = lax.rsqrt(spread + EPSILON)
    left = jnp.concatenate([(patch * scale).astype(jnp.bfloat16) for patch in moved], axis=1)
    for copy in copies:
        copy.wait()
    out_ref[...] = dot(left, flat(whole_ref)).astype(jnp.bfloat16)


def scores_kernel(heads, counts, at_ref, select_hbm, *refs):
    pieces, (merged_ref, labels_ref, lat_ref, lon_ref, both_ref, expos_ref) = refs[:10], refs[10:16]
    select_ref, whole_ref, packed_ref, sems, piece_sems = refs[16:]
    copies = fetch(sems, (select_hbm, select_ref)) + start_pieces(whole_ref, pieces, at_ref, piece_sems)
    count, width = merged_ref.shape
    left = normalized(merged_ref[...].astype(jnp.float32))
    wide = wide_labels(labels_ref, (lat_ref, lon_ref, both_ref), counts, 1)
    copies[0].wait()
    bias = label_bias(wide, select_ref[...])
    for copy in copies[1:]:
        copy.wait()
    packed_ref[...] = dot(left, flat(whole_ref)).astype(jnp.bfloat16)
    for start, members in lane_heads(width, heads):
        queries = packed_ref[:, start : start + LANES]
        keys = packed_ref[:, width + start : width + start + LANES]
        for head, own in members:
            expos = head_expos(queries, keys, own, width // heads, bias)
            expos_ref[head * count : (head + 1) * count] = expos


def close_kernel(heads, at_ref, pick_hbm, *refs):
    pieces, (merged_ref, expos_ref, z_ref), packets = refs[:10], refs[10:13], refs[13:16]
    pick_ref, whole_ref, values_ref, mixed_ref, sems, piece_sems = refs[16:]
    copies = fetch(sems, (pick_hbm, pick_ref)) + start_pieces(whole_ref, pieces, at_ref, piece_sems)
    count, width = merged_ref.shape
    merged = merged_ref[...].astype(jnp.float32)
    left = normalized(merged)
    for copy in copies:
        copy.wait()
    whole = flat(whole_ref)
    wide = width // 4
    for number in range(4):
        columns = slice(number * wide, (number + 1) * wide)
        first = 2 * number * wide
        values_ref[:, columns] = dot(left, whole[:, first : first + wide]).astype(jnp.bfloat16)
    for start, members in lane_heads(width, heads):
        values = with_ones(values_ref[:, start : start + LANES])
        mixed = None
        for head, own in members:
            mixed = head_mix(expos_ref[head * count : (head + 1) * count], values, own, mixed)
        mixed_ref[:, start : start + LANES] = mixed.astype(jnp.bfloat16)
    mixed = mixed_ref[...]
    for number in range(4):
        columns = slice(number * wide, (number + 1) * wide)
        first = (2 * number + 1) * wide
        z_ref[:, columns] = (merged[:, columns] + dot(mixed, whole[:, first : first + wide])).astype(jnp.bfloat16)
    first = 0
    for packet in packets:
        height = packet.shape[0]
        packet[...] = dot(pick_ref[first : first + height], z_ref[...]).astype(jnp.bfloat16)
        first += height


def place_kernel(select_hbm, own_ref, lat_ref, lon_ref, both_ref, out_ref, select_ref, stage_ref, sems):
    loads = fetch(sems, (select_hbm, select_ref))
    fill(stage_ref, (own_ref, lat_ref, lon_ref, both_ref))
    loads[0].wait()
    out_ref[...] = dot(select_ref[...], stage_ref[...]).astype(out_ref.dtype)


def call(kernel, outs, scratch, scalars=(), hbm=(), vmem=(), hbm_outs=(), pinned=False):
    if pinned:
        hbm = [pltpu.with_memory_space_constraint(array, pltpu.HBM) for array in hbm]
    spaces = [pltpu.SMEM] * len(scalars) + [pltpu.HBM] * len(hbm) + [pltpu.VMEM] * len(vmem)
    return pl.pallas_call(
        kernel,
        out_shape=[jax.ShapeDtypeStruct(shape, jnp.bfloat16) for shape in outs],
        in_specs=[pl.BlockSpec(memory_space=space) for space in spaces],
        out_specs=[
            pl.BlockSpec(memory_space=pltpu.HBM if number in hbm_outs else pltpu.VMEM)
            for number in range(len(outs))
        ],
        scratch_shapes=scratch,
        compiler_params=pltpu.CompilerParams(vmem_limit_bytes=VMEM_LIMIT),
    )(*scalars, *hbm, *vmem)


def shifted(blocks, step):
    lat, lon = lax.axis_size("lat"), lax.axis_size("lon")
    return (
        lax.ppermute(blocks[0], "lat", [(i, (i + step) % lat) for i in range(lat)]),
        lax.ppermute(blocks[1], "lon", [(i, (i + step) % lon) for i in range(lon)]),
        lax.ppermute(
            blocks[2],
            ("lat", "lon"),
            [(i * lon + j, (i + step) % lat * lon + (j + step) % lon) for i in range(lat) for j in range(lon)],
        ),
    )


def exchange(block, axis, mask):
    return lax.ppermute(block, axis, [(i, i ^ mask) for i in range(lax.axis_size(axis))])


def far_parts(part):
    ranks = lax.axis_size("lon")
    return [
        lax.ppermute(part, "lon", [(i, (i + 2 * back) % ranks) for i in range(ranks)])
        for back in range(1, ranks // 2)
    ]


def routed(block, turn):
    lat, lon = lax.axis_size("lat"), lax.axis_size("lon")
    pairs = [
        (i * lon + j, (i ^ (1 + (j + turn) % 2)) * lon + j) for i in range(lat) for j in range(lon)
    ]
    return lax.ppermute(block, ("lat", "lon"), pairs)


def joined_parts(far):
    (near,) = call(
        join_kernel,
        [(len(far),) + far[0].shape],
        [pltpu.SemaphoreType.DMA((len(far),))],
        hbm=far,
        hbm_outs=(0,),
    )
    return near


def own_and_swapped(pieces):
    return pieces + [exchange(piece, "lon", 1) for piece in pieces]


def after(value, *earlier):
    return lax.optimization_barrier((value, earlier))[0]


def dma(count):
    return pltpu.SemaphoreType.DMA((count,))


def bf16(*shape):
    return pltpu.VMEM(shape, jnp.bfloat16)


def per_device(
    tokens, level_ids, coarse_ids, first_qkv, first_out, merge_weight, second_qkv, second_out
):
    levels, height, breadth, width = tokens.shape
    _, low, narrow = coarse_ids.shape
    wider = merge_weight.shape[1]
    cells, coarse_cells = levels * height * breadth, levels * low * narrow
    stops = lax.axis_size("lon") // 2
    lat, lon = lax.axis_index("lat"), lax.axis_index("lon")
    at = jnp.stack([lat % 4, (lat == 0).astype(jnp.int32), lon % 2, lon // 2]).astype(jnp.int32)

    start = regions(levels, height, breadth, 0, 0)
    middle = regions(levels, height, breadth, HALF_ROWS, HALF_COLS)
    end = regions(levels, low, narrow, 0, 0)
    counts = [len(part) for part in start]
    packet_rows = [up(len(part) + 2, PACK) for part in start]
    end_rows = [up(len(part) + 2, PACK) for part in end]
    order = window_order(levels, height, breadth)
    inverse = np.argsort(order)
    rows = second_out.shape[0]
    merge_part, score_part, value_part = call(
        quarters_kernel,
        [(merge_weight.shape[0], wider // 4), (rows, wider // 2), (rows, wider // 2)],
        [dma(4)],
        scalars=(at,),
        hbm=(merge_weight, second_qkv, second_out),
        hbm_outs=(0, 1, 2),
        pinned=True,
    )

    def picks(parts, rows, columns):
        return [matrix(part, columns, count) for part, count in zip(parts, rows)]

    def spreader(columns, count):
        return matrix(np.arange(count) % columns, up(columns, PACK)).T

    fine = jnp.concatenate(picks(start, [LANES] * 3, cells) + [spreader(breadth, cells)])
    coarse = jnp.concatenate(picks(end, [LANES] * 3, coarse_cells) + [spreader(narrow, coarse_cells)])
    x = tokens.reshape(cells, width)
    *packets, labels, coarse_labels, score_own, value_own = call(
        lambda *refs: pack_kernel(counts, *refs),
        [(count, width) for count in packet_rows]
        + [(8, cells), (8, coarse_cells), (rows, 2 * wider), (rows, 2 * wider)],
        [
            bf16(cells, width),
            *[pltpu.VMEM((ids.shape[1], levels, ids.shape[2]), jnp.int32) for ids in (level_ids, coarse_ids)],
            bf16(*fine.shape),
            bf16(*coarse.shape),
            dma(14),
        ],
        scalars=(after(at, merge_part),),
        hbm=(x, *[ids.transpose(1, 0, 2) for ids in (level_ids, coarse_ids)], fine, coarse, second_qkv, second_out),
        hbm_outs=(5, 6),
        pinned=True,
    )
    got = shifted(packets, -1)
    nears, routes = [], []
    for part in (merge_part, score_part, value_part):
        near = joined_parts(far_parts(after(part, nears[-1]) if nears else part))
        first, second = routed(near, 0), routed(near, 1)
        nears.append(near)
        routes.append([near, first, second, routed(first, 1)])
    owns = after((merge_weight, score_own, value_own), routes[0][1])
    merge_pieces, score_pieces, value_pieces = [
        own_and_swapped([own] + route) for own, route in zip(owns, routes)
    ]

    source, depth = replaced(cells, start)
    held = np.empty_like(order)
    held[order] = np.arange(cells)
    select = matrix(source[order], depth)
    pick = jnp.concatenate(
        picks([inverse[part] for part in middle], packet_rows, cells)
        + picks([inverse[part] for part in start], packet_rows, cells)
    )
    got_first = after(got, nears[0])
    y, *packets = call(
        lambda *refs: first_kernel(HEADS1, counts, *refs),
        [(cells, width)] + [(count, width) for count in packet_rows] * 2,
        [
            bf16(*select.shape),
            bf16(*first_qkv.shape),
            bf16(*first_out.shape),
            bf16(*pick.shape),
            bf16(depth, width),
            pltpu.VMEM((cells, width), jnp.float32),
            bf16(cells, 3 * width),
            bf16(cells, width),
            dma(5),
        ],
        hbm=(x, select, first_qkv, first_out, pick),
        vmem=(labels, *got_first),
    )
    mid = shifted(packets[:3], -1)
    back = shifted(after(packets[3:], routes[2][1]), 1)

    source, depth = replaced(cells, middle, held)
    fine = source.reshape(levels, low, 2, narrow, 2)
    patches = [fine[:, :, r, :, c].reshape(-1) for r, c in ((0, 0), (1, 0), (0, 1), (1, 1))]
    select = matrix(np.concatenate(patches), depth)
    (merged,) = call(
        merge_kernel,
        [(coarse_cells, wider)],
        [
            bf16(*select.shape),
            bf16(depth, width),
            bf16(stops, 2, *merge_weight.shape),
            dma(1),
            dma(piece_copies(stops)),
        ],
        scalars=(at,),
        hbm=(select, *merge_pieces),
        vmem=(y, *mid),
    )

    source, depth = replaced(cells, start, held)
    select = matrix(source, depth)
    (skip,) = call(
        place_kernel,
        [(cells, width)],
        [bf16(*select.shape), bf16(depth, width), dma(1)],
        hbm=(select,),
        vmem=(y, *back),
    )

    source, depth = replaced(coarse_cells, end)
    select = matrix(source, depth)
    (expos,) = call(
        lambda *refs: scores_kernel(HEADS2, counts, *refs),
        [(HEADS2 * coarse_cells, coarse_cells)],
        [
            bf16(*select.shape),
            bf16(stops, 2, *score_own.shape),
            bf16(coarse_cells, 2 * wider),
            dma(1),
            dma(piece_copies(stops)),
        ],
        scalars=(at,),
        hbm=(select, *score_pieces),
        vmem=(merged, coarse_labels, *got),
    )
    pick = jnp.concatenate(picks(end, end_rows, coarse_cells))
    z, *packets = call(
        lambda *refs: close_kernel(HEADS2, *refs),
        [(coarse_cells, wider)] + [(count, wider) for count in end_rows],
        [
            bf16(*pick.shape),
            bf16(stops, 2, *value_own.shape),
            bf16(coarse_cells, wider),
            bf16(coarse_cells, wider),
            dma(1),
            dma(piece_copies(stops)),
        ],
        scalars=(at,),
        hbm=(pick, *value_pieces),
        vmem=(merged, expos),
    )
    done = shifted(packets, 1)
    (coarse,) = call(
        place_kernel,
        [(coarse_cells, wider)],
        [bf16(*select.shape), bf16(depth, wider), dma(1)],
        hbm=(select,),
        vmem=(z, *done),
    )
    return skip.reshape(tokens.shape), coarse.reshape(levels, low, narrow, wider)


def solution(mesh):
    placed = (
        P(None, "lat", "lon", None),
        P(None, "lat", "lon"),
        P(None, "lat", "lon"),
        P(),
        P(),
        P("lon", None),
        P("lon", None),
        P("lon", None),
    )
    return jax.shard_map(
        per_device,
        mesh=mesh,
        in_specs=placed,
        out_specs=(P(None, "lat", "lon", None), P(None, "lat", "lon", None)),
        check_vma=False,
    )
```

```python
import math

import jax
import jax.numpy as jnp
import numpy as np
from jax import lax
from jax.experimental import pallas as pl
from jax.experimental.pallas import tpu as pltpu
from jax.sharding import PartitionSpec as P

HEADS1 = 8
HEADS2 = 16
WIN_LEVELS = 2
WIN_ROWS = 6
WIN_COLS = 12
HALF_ROWS = WIN_ROWS // 2
HALF_COLS = WIN_COLS // 2

EPSILON = 1e-05
EXCLUDED = -1e30
LANES = 128
PACK = 16
VMEM_LIMIT = 32 * 1024 * 1024
NT = (((1,), (1,)), ((), ()))


def up(count, unit):
    return -(-count // unit) * unit


def places(levels, rows, columns):
    return np.arange(levels * rows * columns).reshape(levels, rows, columns)


def regions(levels, rows, columns, row_from, column_from):
    at = places(levels, rows, columns)
    in_rows = (np.arange(rows) >= row_from) & (np.arange(rows) < row_from + HALF_ROWS)
    in_columns = (np.arange(columns) >= column_from) & (np.arange(columns) < column_from + HALF_COLS)
    picked = (
        at[:, in_rows][:, :, ~in_columns],
        at[:, ~in_rows][:, :, in_columns],
        at[:, in_rows][:, :, in_columns],
    )
    return [part.reshape(-1) for part in picked]


def window_order(levels, rows, columns):
    at = places(levels, rows, columns)
    order = []
    for band in range(rows // WIN_ROWS):
        for across in range(columns // WIN_COLS):
            r = (HALF_ROWS + WIN_ROWS * band + np.arange(WIN_ROWS)) % rows
            c = (HALF_COLS + WIN_COLS * across + np.arange(WIN_COLS)) % columns
            order.append(at[:, r][:, :, c].reshape(-1))
    return np.concatenate(order)


def matrix(sources, columns, height=None):
    out = np.zeros((height or len(sources), columns), np.float32)
    out[np.arange(len(sources)), sources] = 1
    return jnp.asarray(out, jnp.bfloat16)


def offsets(sizes):
    return np.concatenate([[0], np.cumsum([up(size, LANES) for size in sizes])]).tolist()


def replaced(count, parts, held=None):
    starts = offsets([count] + [up(len(part) + 2, PACK) for part in parts])
    source = np.arange(count) if held is None else held.copy()
    for start, part in zip(starts[1:], parts):
        source[part] = start + np.arange(len(part))
    return source, starts[-1]


def fill(stage_ref, parts, held=0):
    start = 0
    for part in parts:
        rows = held if part is None else part.shape[0]
        if part is not None:
            stage_ref[start : start + rows] = part[...]
        if rows % LANES:
            stage_ref[start + rows : start + up(rows, LANES)] = jnp.zeros(
                (up(rows, LANES) - rows, stage_ref.shape[1]), stage_ref.dtype
            )
        start += up(rows, LANES)


def dot(left, right):
    return jnp.dot(left, right, preferred_element_type=jnp.float32)


def dot_nt(left, right):
    return lax.dot_general(left, right, NT, preferred_element_type=jnp.float32)


def normalized(values):
    center = jnp.mean(values, axis=-1, keepdims=True)
    moved = values - center
    spread = jnp.mean(moved * moved, axis=-1, keepdims=True)
    return (moved * lax.rsqrt(spread + EPSILON)).astype(jnp.bfloat16)


def label_bias(wide, select):
    along = dot_nt(wide, select)[:1]
    down = dot_nt(select, wide)[:, :1]
    return jnp.where(down == along, 0.0, EXCLUDED)


def lane_heads(width, heads):
    head_size = width // heads
    lane = lax.broadcasted_iota(jnp.int32, (1, LANES), 1)
    for start in range(0, width, LANES):
        yield start, [
            ((start + low) // head_size, (lane >= low) & (lane < low + head_size))
            for low in range(0, LANES, head_size)
        ]


def head_expos(queries, keys, own, head_size, bias):
    chosen = jnp.where(own, 1.0 / math.sqrt(head_size), 0.0).astype(jnp.bfloat16)
    scores = dot_nt(queries * chosen, keys) + bias
    highest = jnp.max(scores, axis=-1, keepdims=True)
    return jnp.exp(scores - highest).astype(jnp.bfloat16)


def head_mix(expos, values, own, mixed):
    summed = dot(expos, values)
    result = summed[:, :LANES] / summed[:, LANES:]
    return result if mixed is None else jnp.where(own, result, mixed)


def with_ones(values):
    return jnp.concatenate([values, jnp.ones(values.shape, values.dtype)], axis=1)


def attend(packed_ref, mixed_ref, first, count, width, heads, bias):
    rows = slice(first, first + count)
    for start, members in lane_heads(width, heads):
        queries = packed_ref[rows, start : start + LANES]
        keys = packed_ref[rows, width + start : width + start + LANES]
        values = with_ones(packed_ref[rows, 2 * width + start : 2 * width + start + LANES])
        mixed = None
        for _, own in members:
            expos = head_expos(queries, keys, own, width // heads, bias)
            mixed = head_mix(expos, values, own, mixed)
        mixed_ref[rows, start : start + LANES] = mixed.astype(jnp.bfloat16)


def fetch(sems, *pairs):
    copies = [pltpu.make_async_copy(source, target, sems.at[n]) for n, (source, target) in enumerate(pairs)]
    for copy in copies:
        copy.start()
    return copies


def flat_labels(ids_ref, edge, spread):
    rows, levels, columns = ids_ref.shape
    total = 0.0
    for level in range(levels):
        row = lax.broadcasted_iota(jnp.int32, (rows, columns), 0)
        labels = ids_ref[:, level, :] * 2 + jnp.where(row < HALF_ROWS, edge, 0)
        wide = dot(labels.astype(jnp.float32).astype(jnp.bfloat16), spread)
        place = lax.broadcasted_iota(jnp.int32, wide.shape, 1)
        low = (level * rows + lax.broadcasted_iota(jnp.int32, wide.shape, 0)) * columns
        own = (place >= low) & (place < low + columns)
        total += jnp.sum(jnp.where(own, wide, 0.0), axis=0, keepdims=True)
    return jnp.broadcast_to(total, (8, total.shape[1])).astype(jnp.bfloat16)


def block_sources(group, block, merge_ref, qkv_ref, out_ref):
    rows, wide = out_ref.shape[0], out_ref.shape[1] // 2
    if group == 0:
        at_row = pl.multiple_of((block // 2) * rows, PACK)
        at_column = pl.multiple_of((block % 2) * wide, LANES)
        return [(merge_ref.at[pl.ds(at_row, rows), pl.ds(at_column, wide)], pl.ds(0, wide))]
    if group == 1:
        return [(qkv_ref.at[:, pl.ds(pl.multiple_of(block * wide, LANES), wide)], pl.ds(0, wide))]
    half = wide // 2
    return [
        (qkv_ref.at[:, pl.ds(pl.multiple_of(4 * wide + block * half, LANES), half)], pl.ds(0, half)),
        (out_ref.at[:, pl.ds(pl.multiple_of(block * half, LANES), half)], pl.ds(half, half)),
    ]


def quarters_kernel(at_ref, merge_ref, qkv_ref, out_ref, *refs):
    parts, sems = refs[:3], refs[3]
    pairs = []
    for group, part in enumerate(parts):
        for source, columns in block_sources(group, at_ref[0], merge_ref, qkv_ref, out_ref):
            pairs.append((source, part.at[:, columns]))
    for copy in fetch(sems, *pairs):
        copy.wait()


def pack_kernel(counts, at_ref, x_hbm, ids_hbm, coarse_ids_hbm, fine_hbm, coarse_hbm, *refs):
    weights, (outs, (labels_ref, coarse_labels_ref, owns_ref)) = refs[:3], (refs[3:6], refs[6:9])
    x_ref, ids_ref, coarse_ids_ref, fine_ref, coarse_ref, sems = refs[9:]
    edge = at_ref[1]
    pairs = []
    for group in range(3):
        for block in range(4):
            for source, columns in block_sources(group, block, *weights):
                pairs.append((source, owns_ref.at[4 * group + block, :, columns]))
    copies = fetch(
        sems,
        (ids_hbm, ids_ref),
        (coarse_ids_hbm, coarse_ids_ref),
        (coarse_hbm, coarse_ref),
        (fine_hbm, fine_ref),
        (x_hbm, x_ref),
        *pairs,
    )
    for load in copies[:4]:
        load.wait()
    picks = 3 * LANES
    labels = flat_labels(ids_ref, edge, fine_ref[picks : picks + ids_ref.shape[2]])
    coarse_labels = flat_labels(coarse_ids_ref, edge, coarse_ref[picks : picks + coarse_ids_ref.shape[2]])
    labels_ref[...] = labels
    coarse_labels_ref[...] = coarse_labels
    copies[4].wait()
    for number, (packet, count) in enumerate(zip(outs, counts)):
        height = packet.shape[0]
        first = number * LANES
        body = dot(fine_ref[first : first + height], x_ref[...])
        row = lax.broadcasted_iota(jnp.int32, (height, LANES), 0)
        fine = dot_nt(labels, fine_ref[first : first + LANES])[:1]
        coarse = dot_nt(coarse_labels, coarse_ref[first : first + LANES])[:1]
        extra = jnp.where(row == count, fine, jnp.where(row == count + 1, coarse, 0.0))
        packet[:, :LANES] = (body[:, :LANES] + extra).astype(packet.dtype)
        packet[:, LANES:] = body[:, LANES:].astype(packet.dtype)
    for copy in copies[5:]:
        copy.wait()


def wide_labels(labels_ref, packets, counts, line):
    count = labels_ref.shape[1]
    pad = up(count, LANES) - count
    parts = [labels_ref[...].astype(jnp.float32)]
    if pad:
        parts[0] = jnp.concatenate([parts[0], jnp.zeros((8, pad), jnp.float32)], axis=1)
    for packet, size in zip(packets, counts):
        block = packet[size // PACK * PACK : size // PACK * PACK + PACK, :LANES].astype(jnp.float32)
        row = lax.broadcasted_iota(jnp.int32, block.shape, 0)
        picked = jnp.sum(jnp.where(row == size % PACK + line, block, 0.0), axis=0, keepdims=True)
        parts.append(jnp.broadcast_to(picked, (8, LANES)))
    return jnp.concatenate(parts, axis=1).astype(jnp.bfloat16)


def first_kernel(
    heads, counts, x_hbm, select_hbm, qkv_hbm, out_hbm, pick_hbm,
    labels_ref, lat_ref, lon_ref, both_ref, y_ref, *refs,
):
    packets, refs = refs[:6], refs[6:]
    select_ref, qkv_ref, out_ref, pick_ref, stage_ref, rolled_ref, packed_ref, mixed_ref, sems = refs
    cells, width = x_hbm.shape
    window = WIN_LEVELS * WIN_ROWS * WIN_COLS
    loads = fetch(
        sems,
        (x_hbm, stage_ref.at[pl.ds(0, cells)]),
        (select_hbm, select_ref),
        (qkv_hbm, qkv_ref),
        (out_hbm, out_ref),
        (pick_hbm, pick_ref),
    )
    fill(stage_ref, (None, lat_ref, lon_ref, both_ref), cells)
    wide = wide_labels(labels_ref, (lat_ref, lon_ref, both_ref), counts, 0)
    loads[0].wait()
    loads[1].wait()
    rolled = dot(select_ref[...], stage_ref[...])
    rolled_ref[...] = rolled
    loads[2].wait()
    packed_ref[...] = dot(normalized(rolled), qkv_ref[...]).astype(jnp.bfloat16)
    for first in range(0, cells, window):
        bias = label_bias(wide, select_ref[first : first + window])
        attend(packed_ref, mixed_ref, first, window, width, heads, bias)
    loads[3].wait()
    y_ref[...] = (rolled_ref[...] + dot(mixed_ref[...], out_ref[...])).astype(jnp.bfloat16)
    loads[4].wait()
    first = 0
    for packet in packets:
        height = packet.shape[0]
        packet[...] = dot(pick_ref[first : first + height], y_ref[...]).astype(jnp.bfloat16)
        first += height


def join_kernel(plans, *refs):
    sems, outs = refs[-1], refs[-1 - len(plans) : -1]
    pairs = []
    for plan, out_ref in zip(plans, outs):
        first = 0
        for number in plan:
            part = refs[number]
            if len(part.shape) == 2:
                pairs.append((part, out_ref.at[first]))
                first += 1
            else:
                pairs.append((part, out_ref.at[pl.ds(first, part.shape[0])]))
                first += part.shape[0]
    for copy in fetch(sems, *pairs):
        copy.wait()


def start_pieces(whole_ref, sides, at_ref, sems):
    corner, side, here = at_ref[0], at_ref[2], at_ref[3]
    stops = whole_ref.shape[0]
    copies = []

    def put(source, stop, from_side, block):
        rows, wide = source.shape
        held = whole_ref.at[stop, from_side]
        across = whole_ref.shape[3] // wide
        at_row, at_column = (block // across) * rows, (block % across) * wide
        target = held.at[pl.ds(pl.multiple_of(at_row, PACK), rows), pl.ds(pl.multiple_of(at_column, LANES), wide)]
        copies.append(pltpu.make_async_copy(source, target, sems.at[len(copies)]))
        copies[-1].start()

    for other, (own, *stacks) in enumerate(sides):
        from_side = side ^ other
        for block in range(4):
            put(own.at[block], here, from_side, block)
        for stack, mask in zip(stacks, (0, 1 + from_side, 2 - from_side, 3)):
            for back in range(1, stops):
                put(stack.at[back - 1], lax.rem(here + (stops - back), stops), from_side, corner ^ mask)
    return copies


def piece_copies(stops):
    return 2 * (4 + 4 * (stops - 1))


def flat(whole_ref):
    stops, sides, rows, columns = whole_ref.shape
    return whole_ref[...].reshape(stops * sides * rows, columns)


def cuts(refs, plan):
    return [[refs[number].at[pl.ds(first, count)] for number, first, count in side] for side in plan]


def merge_kernel(count, plan, at_ref, select_hbm, *refs):
    pieces, (y_ref, lat_ref, lon_ref, both_ref, out_ref) = cuts(refs[:count], plan), refs[count : count + 5]
    select_ref, stage_ref, whole_ref, sems, piece_sems = refs[count + 5 :]
    loads = fetch(sems, (select_hbm, select_ref))
    copies = start_pieces(whole_ref, pieces, at_ref, piece_sems)
    fill(stage_ref, (y_ref, lat_ref, lon_ref, both_ref))
    cells = out_ref.shape[0]
    loads[0].wait()
    patches = [
        dot(select_ref[first : first + cells], stage_ref[...]) for first in range(0, select_ref.shape[0], cells)
    ]
    total = 1.0 / (len(patches) * y_ref.shape[1])
    center = sum(jnp.sum(patch, axis=-1, keepdims=True) for patch in patches) * total
    moved = [patch - center for patch in patches]
    spread = sum(jnp.sum(patch * patch, axis=-1, keepdims=True) for patch in moved) * total
    scale = lax.rsqrt(spread + EPSILON)
    left = jnp.concatenate([(patch * scale).astype(jnp.bfloat16) for patch in moved], axis=1)
    for copy in copies:
        copy.wait()
    out_ref[...] = dot(left, flat(whole_ref)).astype(jnp.bfloat16)


def scores_kernel(heads, counts, number, plan, at_ref, select_hbm, *refs):
    pieces = cuts(refs[:number], plan)
    merged_ref, labels_ref, lat_ref, lon_ref, both_ref, expos_ref = refs[number : number + 6]
    select_ref, whole_ref, packed_ref, sems, piece_sems = refs[number + 6 :]
    copies = fetch(sems, (select_hbm, select_ref)) + start_pieces(whole_ref, pieces, at_ref, piece_sems)
    count, width = merged_ref.shape
    left = normalized(merged_ref[...].astype(jnp.float32))
    wide = wide_labels(labels_ref, (lat_ref, lon_ref, both_ref), counts, 1)
    copies[0].wait()
    bias = label_bias(wide, select_ref[...])
    for copy in copies[1:]:
        copy.wait()
    packed_ref[...] = dot(left, flat(whole_ref)).astype(jnp.bfloat16)
    for start, members in lane_heads(width, heads):
        queries = packed_ref[:, start : start + LANES]
        keys = packed_ref[:, width + start : width + start + LANES]
        for head, own in members:
            expos = head_expos(queries, keys, own, width // heads, bias)
            expos_ref[head * count : (head + 1) * count] = expos


def close_kernel(heads, number, plan, at_ref, pick_hbm, *refs):
    pieces, (merged_ref, expos_ref, z_ref) = cuts(refs[:number], plan), refs[number : number + 3]
    packets, refs = refs[number + 3 : number + 6], refs[number + 6 :]
    pick_ref, whole_ref, values_ref, mixed_ref, sems, piece_sems = refs
    copies = fetch(sems, (pick_hbm, pick_ref)) + start_pieces(whole_ref, pieces, at_ref, piece_sems)
    count, width = merged_ref.shape
    merged = merged_ref[...].astype(jnp.float32)
    left = normalized(merged)
    for copy in copies:
        copy.wait()
    whole = flat(whole_ref)
    wide = width // 4
    for number in range(4):
        columns = slice(number * wide, (number + 1) * wide)
        first = 2 * number * wide
        values_ref[:, columns] = dot(left, whole[:, first : first + wide]).astype(jnp.bfloat16)
    for start, members in lane_heads(width, heads):
        values = with_ones(values_ref[:, start : start + LANES])
        mixed = None
        for head, own in members:
            mixed = head_mix(expos_ref[head * count : (head + 1) * count], values, own, mixed)
        mixed_ref[:, start : start + LANES] = mixed.astype(jnp.bfloat16)
    mixed = mixed_ref[...]
    for number in range(4):
        columns = slice(number * wide, (number + 1) * wide)
        first = (2 * number + 1) * wide
        z_ref[:, columns] = (merged[:, columns] + dot(mixed, whole[:, first : first + wide])).astype(jnp.bfloat16)
    first = 0
    for packet in packets:
        height = packet.shape[0]
        packet[...] = dot(pick_ref[first : first + height], z_ref[...]).astype(jnp.bfloat16)
        first += height


def place_kernel(select_hbm, own_ref, lat_ref, lon_ref, both_ref, out_ref, select_ref, stage_ref, sems):
    loads = fetch(sems, (select_hbm, select_ref))
    fill(stage_ref, (own_ref, lat_ref, lon_ref, both_ref))
    loads[0].wait()
    out_ref[...] = dot(select_ref[...], stage_ref[...]).astype(out_ref.dtype)


def call(kernel, outs, scratch, scalars=(), hbm=(), vmem=(), hbm_outs=(), pinned=False):
    if pinned:
        hbm = [pltpu.with_memory_space_constraint(array, pltpu.HBM) for array in hbm]
    spaces = [pltpu.SMEM] * len(scalars) + [pltpu.HBM] * len(hbm) + [pltpu.VMEM] * len(vmem)
    return pl.pallas_call(
        kernel,
        out_shape=[jax.ShapeDtypeStruct(shape, jnp.bfloat16) for shape in outs],
        in_specs=[pl.BlockSpec(memory_space=space) for space in spaces],
        out_specs=[
            pl.BlockSpec(memory_space=pltpu.HBM if number in hbm_outs else pltpu.VMEM)
            for number in range(len(outs))
        ],
        scratch_shapes=scratch,
        compiler_params=pltpu.CompilerParams(vmem_limit_bytes=VMEM_LIMIT),
    )(*scalars, *hbm, *vmem)


def shifted(blocks, step):
    lat, lon = lax.axis_size("lat"), lax.axis_size("lon")
    return (
        lax.ppermute(blocks[0], "lat", [(i, (i + step) % lat) for i in range(lat)]),
        lax.ppermute(blocks[1], "lon", [(i, (i + step) % lon) for i in range(lon)]),
        lax.ppermute(
            blocks[2],
            ("lat", "lon"),
            [(i * lon + j, (i + step) % lat * lon + (j + step) % lon) for i in range(lat) for j in range(lon)],
        ),
    )


def exchange(block, axis, mask):
    return lax.ppermute(block, axis, [(i, i ^ mask) for i in range(lax.axis_size(axis))])


def far_parts(part):
    ranks = lax.axis_size("lon")
    return [
        lax.ppermute(part, "lon", [(i, (i + 2 * back) % ranks) for i in range(ranks)])
        for back in range(1, ranks // 2)
    ]


def routed(block, turn):
    lat, lon = lax.axis_size("lat"), lax.axis_size("lon")
    pairs = [
        (i * lon + j, (i ^ (1 + (j + turn) % 2)) * lon + j) for i in range(lat) for j in range(lon)
    ]
    return lax.ppermute(block, ("lat", "lon"), pairs)


def joined(*plans):
    arrays = []
    for plan in plans:
        arrays += [array for array in plan if not any(array is seen for seen in arrays)]
    numbers = [[next(n for n, seen in enumerate(arrays) if seen is array) for array in plan] for plan in plans]
    shapes = [
        (sum(1 if array.ndim == 2 else array.shape[0] for array in plan),) + plan[0].shape[-2:] for plan in plans
    ]
    return call(
        lambda *refs: join_kernel(numbers, *refs),
        shapes,
        [pltpu.SemaphoreType.DMA((sum(len(plan) for plan in plans),))],
        hbm=arrays,
        hbm_outs=range(len(plans)),
    )


def swapped(pieces):
    return [exchange(piece, "lon", 1) for piece in pieces]


def after(value, *earlier):
    return lax.optimization_barrier((value, earlier))[0]


def dma(count):
    return pltpu.SemaphoreType.DMA((count,))


def bf16(*shape):
    return pltpu.VMEM(shape, jnp.bfloat16)


def per_device(
    tokens, level_ids, coarse_ids, first_qkv, first_out, merge_weight, second_qkv, second_out
):
    levels, height, breadth, width = tokens.shape
    _, low, narrow = coarse_ids.shape
    wider = merge_weight.shape[1]
    cells, coarse_cells = levels * height * breadth, levels * low * narrow
    stops = lax.axis_size("lon") // 2
    lat, lon = lax.axis_index("lat"), lax.axis_index("lon")
    at = jnp.stack([lat % 4, (lat == 0).astype(jnp.int32), lon % 2, lon // 2]).astype(jnp.int32)

    start = regions(levels, height, breadth, 0, 0)
    middle = regions(levels, height, breadth, HALF_ROWS, HALF_COLS)
    end = regions(levels, low, narrow, 0, 0)
    counts = [len(part) for part in start]
    packet_rows = [up(len(part) + 2, PACK) for part in start]
    end_rows = [up(len(part) + 2, PACK) for part in end]
    order = window_order(levels, height, breadth)
    inverse = np.argsort(order)
    rows = second_out.shape[0]
    merge_part, score_part, value_part = call(
        quarters_kernel,
        [(rows, wider // 2)] * 3,
        [dma(4)],
        scalars=(at,),
        hbm=(merge_weight, second_qkv, second_out),
        hbm_outs=(0, 1, 2),
        pinned=True,
    )

    def picks(parts, rows, columns):
        return [matrix(part, columns, count) for part, count in zip(parts, rows)]

    def spreader(columns, count):
        return matrix(np.arange(count) % columns, up(columns, PACK)).T

    fine = jnp.concatenate(picks(start, [LANES] * 3, cells) + [spreader(breadth, cells)])
    coarse = jnp.concatenate(picks(end, [LANES] * 3, coarse_cells) + [spreader(narrow, coarse_cells)])
    x = tokens.reshape(cells, width)
    *packets, labels, coarse_labels, owns = call(
        lambda *refs: pack_kernel(counts, *refs),
        [(count, width) for count in packet_rows]
        + [(8, cells), (8, coarse_cells), (12, rows, wider // 2)],
        [
            bf16(cells, width),
            *[pltpu.VMEM((ids.shape[1], levels, ids.shape[2]), jnp.int32) for ids in (level_ids, coarse_ids)],
            bf16(*fine.shape),
            bf16(*coarse.shape),
            dma(21),
        ],
        scalars=(after(at, merge_part),),
        hbm=(x, *[ids.transpose(1, 0, 2) for ids in (level_ids, coarse_ids)], fine, coarse, merge_weight, second_qkv, second_out),
        hbm_outs=(5,),
        pinned=True,
    )
    got = shifted(packets, -1)
    far = stops - 1

    (near1,) = joined(after(far_parts(merge_part), got))
    first1 = routed(near1, 0)
    far2 = far_parts(after(score_part, near1))
    (other,) = swapped([after(owns, near1)])
    source, depth = replaced(cells, start)
    held = np.empty_like(order)
    held[order] = np.arange(cells)
    select = matrix(source[order], depth)
    pick = jnp.concatenate(
        picks([inverse[part] for part in middle], packet_rows, cells)
        + picks([inverse[part] for part in start], packet_rows, cells)
    )
    got_first = got
    y, *packets = call(
        lambda *refs: first_kernel(HEADS1, counts, *refs),
        [(cells, width)] + [(count, width) for count in packet_rows] * 2,
        [
            bf16(*select.shape),
            bf16(*first_qkv.shape),
            bf16(*first_out.shape),
            bf16(*pick.shape),
            bf16(depth, width),
            pltpu.VMEM((cells, width), jnp.float32),
            bf16(cells, 3 * width),
            bf16(cells, width),
            dma(5),
        ],
        hbm=(x, select, first_qkv, first_out, pick),
        vmem=(labels, *got_first),
    )
    (near2,) = joined(after(far2, first1, y, other))
    first2 = routed(near2, 0)
    far3 = far_parts(after(value_part, near2))
    (join1,) = joined(after([near1, first1], near2))
    second1 = routed(join1, 1)
    (near3,) = joined(after(far3, first2, second1))
    first3 = routed(near3, 0)
    (join2,) = joined(after([near2, first2], near3))
    second2 = routed(join2, 1)
    mid = shifted(after(packets[:3], near3), -1)
    last_first = after(first3, second2, mid)
    (join3,) = joined([near3, last_first])
    second3 = routed(join3, 1)
    merge_pieces = (owns, join1, second1, other, *swapped(after((join1, second1), last_first)))
    score_pieces = (owns, join2, second2, other, *swapped(after((join2, second2), last_first)))

    def plan(group):
        return [
            [(own, 4 * group, 4), (own + 1, 0, far), (own + 1, far, far), (own + 2, 0, far), (own + 2, far, far)]
            for own in (0, 3)
        ]

    merge_plan, score_plan, value_plan = plan(0), plan(1), plan(2)

    source, depth = replaced(cells, middle, held)
    fine = source.reshape(levels, low, 2, narrow, 2)
    patches = [fine[:, :, r, :, c].reshape(-1) for r, c in ((0, 0), (1, 0), (0, 1), (1, 1))]
    select = matrix(np.concatenate(patches), depth)
    (merged,) = call(
        lambda *refs: merge_kernel(len(merge_pieces), merge_plan, *refs),
        [(coarse_cells, wider)],
        [
            bf16(*select.shape),
            bf16(depth, width),
            bf16(stops, 2, *merge_weight.shape),
            dma(1),
            dma(piece_copies(stops)),
        ],
        scalars=(at,),
        hbm=(select, *merge_pieces),
        vmem=(y, *mid),
    )

    back = shifted(after(packets[3:], merged), 1)
    source, depth = replaced(cells, start, held)
    select = matrix(source, depth)
    (skip,) = call(
        place_kernel,
        [(cells, width)],
        [bf16(*select.shape), bf16(depth, width), dma(1)],
        hbm=(select,),
        vmem=(y, *back),
    )

    source, depth = replaced(coarse_cells, end)
    select = matrix(source, depth)
    (expos,) = call(
        lambda *refs: scores_kernel(HEADS2, counts, len(score_pieces), score_plan, *refs),
        [(HEADS2 * coarse_cells, coarse_cells)],
        [
            bf16(*select.shape),
            bf16(stops, 2, rows, 2 * wider),
            bf16(coarse_cells, 2 * wider),
            dma(1),
            dma(piece_copies(stops)),
        ],
        scalars=(at,),
        hbm=(select, *score_pieces),
        vmem=(merged, coarse_labels, *got),
    )
    value_swapped = swapped([after(join3, last_first), after(second3, back, expos)])
    value_pieces = (owns, join3, second3, other, *value_swapped)
    pick = jnp.concatenate(picks(end, end_rows, coarse_cells))
    z, *packets = call(
        lambda *refs: close_kernel(HEADS2, len(value_pieces), value_plan, *refs),
        [(coarse_cells, wider)] + [(count, wider) for count in end_rows],
        [
            bf16(*pick.shape),
            bf16(stops, 2, rows, 2 * wider),
            bf16(coarse_cells, wider),
            bf16(coarse_cells, wider),
            dma(1),
            dma(piece_copies(stops)),
        ],
        scalars=(at,),
        hbm=(pick, *value_pieces),
        vmem=(merged, expos),
    )
    done = shifted(packets, 1)
    (coarse,) = call(
        place_kernel,
        [(coarse_cells, wider)],
        [bf16(*select.shape), bf16(depth, wider), dma(1)],
        hbm=(select,),
        vmem=(z, *done),
    )
    return skip.reshape(tokens.shape), coarse.reshape(levels, low, narrow, wider)


def solution(mesh):
    placed = (
        P(None, "lat", "lon", None),
        P(None, "lat", "lon"),
        P(None, "lat", "lon"),
        P(),
        P(),
        P("lon", None),
        P("lon", None),
        P("lon", None),
    )
    return jax.shard_map(
        per_device,
        mesh=mesh,
        in_specs=placed,
        out_specs=(P(None, "lat", "lon", None), P(None, "lat", "lon", None)),
        check_vma=False,
    )
```

```python
import math

import jax
import jax.numpy as jnp
import numpy as np
from jax import lax
from jax.experimental import pallas as pl
from jax.experimental.pallas import tpu as pltpu
from jax.sharding import PartitionSpec as P

HEADS1 = 8
HEADS2 = 16
WIN_LEVELS = 2
WIN_ROWS = 6
WIN_COLS = 12
HALF_ROWS = WIN_ROWS // 2
HALF_COLS = WIN_COLS // 2

EPSILON = 1e-05
EXCLUDED = -1e30
LANES = 128
PACK = 16
VMEM_LIMIT = 32 * 1024 * 1024
NT = (((1,), (1,)), ((), ()))


def up(count, unit):
    return -(-count // unit) * unit


def places(levels, rows, columns):
    return np.arange(levels * rows * columns).reshape(levels, rows, columns)


def regions(levels, rows, columns, row_from, column_from):
    at = places(levels, rows, columns)
    in_rows = (np.arange(rows) >= row_from) & (np.arange(rows) < row_from + HALF_ROWS)
    in_columns = (np.arange(columns) >= column_from) & (np.arange(columns) < column_from + HALF_COLS)
    picked = (
        at[:, in_rows][:, :, ~in_columns],
        at[:, ~in_rows][:, :, in_columns],
        at[:, in_rows][:, :, in_columns],
    )
    return [part.reshape(-1) for part in picked]


def window_order(levels, rows, columns):
    at = places(levels, rows, columns)
    order = []
    for band in range(rows // WIN_ROWS):
        for across in range(columns // WIN_COLS):
            r = (HALF_ROWS + WIN_ROWS * band + np.arange(WIN_ROWS)) % rows
            c = (HALF_COLS + WIN_COLS * across + np.arange(WIN_COLS)) % columns
            order.append(at[:, r][:, :, c].reshape(-1))
    return np.concatenate(order)


def matrix(sources, columns, height=None):
    out = np.zeros((height or len(sources), columns), np.float32)
    out[np.arange(len(sources)), sources] = 1
    return jnp.asarray(out, jnp.bfloat16)


def offsets(sizes):
    return np.concatenate([[0], np.cumsum([up(size, LANES) for size in sizes])]).tolist()


def replaced(count, parts, held=None):
    starts = offsets([count] + [up(len(part) + 2, PACK) for part in parts])
    source = np.arange(count) if held is None else held.copy()
    for start, part in zip(starts[1:], parts):
        source[part] = start + np.arange(len(part))
    return source, starts[-1]


def fill(stage_ref, parts, held=0):
    start = 0
    for part in parts:
        rows = held if part is None else part.shape[0]
        if part is not None:
            stage_ref[start : start + rows] = part[...]
        if rows % LANES:
            stage_ref[start + rows : start + up(rows, LANES)] = jnp.zeros(
                (up(rows, LANES) - rows, stage_ref.shape[1]), stage_ref.dtype
            )
        start += up(rows, LANES)


def dot(left, right):
    return jnp.dot(left, right, preferred_element_type=jnp.float32)


def dot_nt(left, right):
    return lax.dot_general(left, right, NT, preferred_element_type=jnp.float32)


def normalized(values):
    center = jnp.mean(values, axis=-1, keepdims=True)
    moved = values - center
    spread = jnp.mean(moved * moved, axis=-1, keepdims=True)
    return (moved * lax.rsqrt(spread + EPSILON)).astype(jnp.bfloat16)


def label_bias(wide, select):
    along = dot_nt(wide, select)[:1]
    down = dot_nt(select, wide)[:, :1]
    return jnp.where(down == along, 0.0, EXCLUDED)


def lane_heads(width, heads):
    head_size = width // heads
    lane = lax.broadcasted_iota(jnp.int32, (1, LANES), 1)
    for start in range(0, width, LANES):
        yield start, [
            ((start + low) // head_size, (lane >= low) & (lane < low + head_size))
            for low in range(0, LANES, head_size)
        ]


def head_expos(queries, keys, own, head_size, bias):
    chosen = jnp.where(own, 1.0 / math.sqrt(head_size), 0.0).astype(jnp.bfloat16)
    scores = dot_nt(queries * chosen, keys) + bias
    highest = jnp.max(scores, axis=-1, keepdims=True)
    return jnp.exp(scores - highest).astype(jnp.bfloat16)


def head_mix(expos, values, own, mixed):
    summed = dot(expos, values)
    result = summed[:, :LANES] / summed[:, LANES:]
    return result if mixed is None else jnp.where(own, result, mixed)


def with_ones(values):
    return jnp.concatenate([values, jnp.ones(values.shape, values.dtype)], axis=1)


def attend(packed_ref, mixed_ref, first, count, width, heads, bias):
    rows = slice(first, first + count)
    for start, members in lane_heads(width, heads):
        queries = packed_ref[rows, start : start + LANES]
        keys = packed_ref[rows, width + start : width + start + LANES]
        values = with_ones(packed_ref[rows, 2 * width + start : 2 * width + start + LANES])
        mixed = None
        for _, own in members:
            expos = head_expos(queries, keys, own, width // heads, bias)
            mixed = head_mix(expos, values, own, mixed)
        mixed_ref[rows, start : start + LANES] = mixed.astype(jnp.bfloat16)


def fetch(sems, *pairs):
    copies = [pltpu.make_async_copy(source, target, sems.at[n]) for n, (source, target) in enumerate(pairs)]
    for copy in copies:
        copy.start()
    return copies


def flat_labels(ids_ref, edge, spread):
    rows, levels, columns = ids_ref.shape
    total = 0.0
    for level in range(levels):
        row = lax.broadcasted_iota(jnp.int32, (rows, columns), 0)
        labels = ids_ref[:, level, :] * 2 + jnp.where(row < HALF_ROWS, edge, 0)
        wide = dot(labels.astype(jnp.float32).astype(jnp.bfloat16), spread)
        place = lax.broadcasted_iota(jnp.int32, wide.shape, 1)
        low = (level * rows + lax.broadcasted_iota(jnp.int32, wide.shape, 0)) * columns
        own = (place >= low) & (place < low + columns)
        total += jnp.sum(jnp.where(own, wide, 0.0), axis=0, keepdims=True)
    return jnp.broadcast_to(total, (8, total.shape[1])).astype(jnp.bfloat16)


def block_sources(group, block, merge_ref, qkv_ref, out_ref):
    rows, wide = out_ref.shape[0], out_ref.shape[1] // 2
    if group == 0:
        at_row = pl.multiple_of((block // 2) * rows, PACK)
        at_column = pl.multiple_of((block % 2) * wide, LANES)
        return [(merge_ref.at[pl.ds(at_row, rows), pl.ds(at_column, wide)], pl.ds(0, wide))]
    if group == 1:
        return [(qkv_ref.at[:, pl.ds(pl.multiple_of(block * wide, LANES), wide)], pl.ds(0, wide))]
    half = wide // 2
    return [
        (qkv_ref.at[:, pl.ds(pl.multiple_of(4 * wide + block * half, LANES), half)], pl.ds(0, half)),
        (out_ref.at[:, pl.ds(pl.multiple_of(block * half, LANES), half)], pl.ds(half, half)),
    ]


def pack_kernel(counts, at_ref, x_hbm, ids_hbm, coarse_ids_hbm, fine_hbm, coarse_hbm, *refs):
    weights, outs, labels_ref, coarse_labels_ref, owns_ref, parts = refs[:3], refs[3:6], *refs[6:9], refs[9:12]
    x_ref, ids_ref, coarse_ids_ref, fine_ref, coarse_ref, sems = refs[12:]
    edge = at_ref[1]
    pairs = []
    for group, part in enumerate(parts):
        for source, columns in block_sources(group, at_ref[0], *weights):
            pairs.append((source, part.at[:, columns]))
        for block in range(4):
            for source, columns in block_sources(group, block, *weights):
                pairs.append((source, owns_ref.at[4 * group + block, :, columns]))
    copies = fetch(
        sems,
        (ids_hbm, ids_ref),
        (coarse_ids_hbm, coarse_ids_ref),
        (coarse_hbm, coarse_ref),
        (fine_hbm, fine_ref),
        (x_hbm, x_ref),
        *pairs,
    )
    for load in copies[:4]:
        load.wait()
    picks = 3 * LANES
    labels = flat_labels(ids_ref, edge, fine_ref[picks : picks + ids_ref.shape[2]])
    coarse_labels = flat_labels(coarse_ids_ref, edge, coarse_ref[picks : picks + coarse_ids_ref.shape[2]])
    labels_ref[...] = labels
    coarse_labels_ref[...] = coarse_labels
    copies[4].wait()
    for number, (packet, count) in enumerate(zip(outs, counts)):
        height = packet.shape[0]
        first = number * LANES
        body = dot(fine_ref[first : first + height], x_ref[...])
        row = lax.broadcasted_iota(jnp.int32, (height, LANES), 0)
        fine = dot_nt(labels, fine_ref[first : first + LANES])[:1]
        coarse = dot_nt(coarse_labels, coarse_ref[first : first + LANES])[:1]
        extra = jnp.where(row == count, fine, jnp.where(row == count + 1, coarse, 0.0))
        packet[:, :LANES] = (body[:, :LANES] + extra).astype(packet.dtype)
        packet[:, LANES:] = body[:, LANES:].astype(packet.dtype)
    for copy in copies[5:]:
        copy.wait()


def wide_labels(labels_ref, packets, counts, line):
    count = labels_ref.shape[1]
    pad = up(count, LANES) - count
    parts = [labels_ref[...].astype(jnp.float32)]
    if pad:
        parts[0] = jnp.concatenate([parts[0], jnp.zeros((8, pad), jnp.float32)], axis=1)
    for packet, size in zip(packets, counts):
        block = packet[size // PACK * PACK : size // PACK * PACK + PACK, :LANES].astype(jnp.float32)
        row = lax.broadcasted_iota(jnp.int32, block.shape, 0)
        picked = jnp.sum(jnp.where(row == size % PACK + line, block, 0.0), axis=0, keepdims=True)
        parts.append(jnp.broadcast_to(picked, (8, LANES)))
    return jnp.concatenate(parts, axis=1).astype(jnp.bfloat16)


def first_kernel(
    heads, counts, x_hbm, select_hbm, qkv_hbm, out_hbm, pick_hbm,
    labels_ref, lat_ref, lon_ref, both_ref, y_ref, *refs,
):
    packets, refs = refs[:6], refs[6:]
    select_ref, qkv_ref, out_ref, pick_ref, stage_ref, rolled_ref, packed_ref, mixed_ref, sems = refs
    cells, width = x_hbm.shape
    window = WIN_LEVELS * WIN_ROWS * WIN_COLS
    loads = fetch(
        sems,
        (x_hbm, stage_ref.at[pl.ds(0, cells)]),
        (select_hbm, select_ref),
        (qkv_hbm, qkv_ref),
        (out_hbm, out_ref),
        (pick_hbm, pick_ref),
    )
    fill(stage_ref, (None, lat_ref, lon_ref, both_ref), cells)
    wide = wide_labels(labels_ref, (lat_ref, lon_ref, both_ref), counts, 0)
    loads[0].wait()
    loads[1].wait()
    rolled = dot(select_ref[...], stage_ref[...])
    rolled_ref[...] = rolled
    loads[2].wait()
    packed_ref[...] = dot(normalized(rolled), qkv_ref[...]).astype(jnp.bfloat16)
    for first in range(0, cells, window):
        bias = label_bias(wide, select_ref[first : first + window])
        attend(packed_ref, mixed_ref, first, window, width, heads, bias)
    loads[3].wait()
    y_ref[...] = (rolled_ref[...] + dot(mixed_ref[...], out_ref[...])).astype(jnp.bfloat16)
    loads[4].wait()
    first = 0
    for packet in packets:
        height = packet.shape[0]
        packet[...] = dot(pick_ref[first : first + height], y_ref[...]).astype(jnp.bfloat16)
        first += height


def join_kernel(plans, *refs):
    sems, outs = refs[-1], refs[-1 - len(plans) : -1]
    pairs = []
    for plan, out_ref in zip(plans, outs):
        first = 0
        for number in plan:
            part = refs[number]
            if len(part.shape) == 2:
                pairs.append((part, out_ref.at[first]))
                first += 1
            else:
                pairs.append((part, out_ref.at[pl.ds(first, part.shape[0])]))
                first += part.shape[0]
    for copy in fetch(sems, *pairs):
        copy.wait()


def start_pieces(whole_ref, sides, at_ref, sems):
    corner, side, here = at_ref[0], at_ref[2], at_ref[3]
    stops = whole_ref.shape[0]
    copies = []

    def put(source, stop, from_side, block):
        rows, wide = source.shape
        held = whole_ref.at[stop, from_side]
        across = whole_ref.shape[3] // wide
        at_row, at_column = (block // across) * rows, (block % across) * wide
        target = held.at[pl.ds(pl.multiple_of(at_row, PACK), rows), pl.ds(pl.multiple_of(at_column, LANES), wide)]
        copies.append(pltpu.make_async_copy(source, target, sems.at[len(copies)]))
        copies[-1].start()

    for other, (own, *stacks) in enumerate(sides):
        from_side = side ^ other
        for block in range(4):
            put(own.at[block], here, from_side, block)
        for stack, mask in zip(stacks, (0, 1 + from_side, 2 - from_side, 3)):
            for back in range(1, stops):
                put(stack.at[back - 1], lax.rem(here + (stops - back), stops), from_side, corner ^ mask)
    return copies


def piece_copies(stops):
    return 2 * (4 + 4 * (stops - 1))


def flat(whole_ref):
    stops, sides, rows, columns = whole_ref.shape
    return whole_ref[...].reshape(stops * sides * rows, columns)


def cuts(refs, plan):
    return [[refs[number].at[pl.ds(first, count)] for number, first, count in side] for side in plan]


def merge_kernel(count, plan, at_ref, select_hbm, *refs):
    pieces, (y_ref, lat_ref, lon_ref, both_ref, out_ref) = cuts(refs[:count], plan), refs[count : count + 5]
    select_ref, stage_ref, whole_ref, sems, piece_sems = refs[count + 5 :]
    loads = fetch(sems, (select_hbm, select_ref))
    copies = start_pieces(whole_ref, pieces, at_ref, piece_sems)
    fill(stage_ref, (y_ref, lat_ref, lon_ref, both_ref))
    cells = out_ref.shape[0]
    loads[0].wait()
    patches = [
        dot(select_ref[first : first + cells], stage_ref[...]) for first in range(0, select_ref.shape[0], cells)
    ]
    total = 1.0 / (len(patches) * y_ref.shape[1])
    center = sum(jnp.sum(patch, axis=-1, keepdims=True) for patch in patches) * total
    moved = [patch - center for patch in patches]
    spread = sum(jnp.sum(patch * patch, axis=-1, keepdims=True) for patch in moved) * total
    scale = lax.rsqrt(spread + EPSILON)
    left = jnp.concatenate([(patch * scale).astype(jnp.bfloat16) for patch in moved], axis=1)
    for copy in copies:
        copy.wait()
    out_ref[...] = dot(left, flat(whole_ref)).astype(jnp.bfloat16)


def scores_kernel(heads, counts, number, plan, at_ref, select_hbm, *refs):
    pieces = cuts(refs[:number], plan)
    merged_ref, labels_ref, lat_ref, lon_ref, both_ref, expos_ref = refs[number : number + 6]
    select_ref, whole_ref, packed_ref, sems, piece_sems = refs[number + 6 :]
    copies = fetch(sems, (select_hbm, select_ref)) + start_pieces(whole_ref, pieces, at_ref, piece_sems)
    count, width = merged_ref.shape
    left = normalized(merged_ref[...].astype(jnp.float32))
    wide = wide_labels(labels_ref, (lat_ref, lon_ref, both_ref), counts, 1)
    copies[0].wait()
    bias = label_bias(wide, select_ref[...])
    for copy in copies[1:]:
        copy.wait()
    packed_ref[...] = dot(left, flat(whole_ref)).astype(jnp.bfloat16)
    for start, members in lane_heads(width, heads):
        queries = packed_ref[:, start : start + LANES]
        keys = packed_ref[:, width + start : width + start + LANES]
        for head, own in members:
            expos = head_expos(queries, keys, own, width // heads, bias)
            expos_ref[head * count : (head + 1) * count] = expos


def close_kernel(heads, number, plan, at_ref, pick_hbm, *refs):
    pieces, (merged_ref, expos_ref, z_ref) = cuts(refs[:number], plan), refs[number : number + 3]
    packets, refs = refs[number + 3 : number + 6], refs[number + 6 :]
    pick_ref, whole_ref, values_ref, mixed_ref, sems, piece_sems = refs
    copies = fetch(sems, (pick_hbm, pick_ref)) + start_pieces(whole_ref, pieces, at_ref, piece_sems)
    count, width = merged_ref.shape
    merged = merged_ref[...].astype(jnp.float32)
    left = normalized(merged)
    for copy in copies:
        copy.wait()
    whole = flat(whole_ref)
    wide = width // 4
    for number in range(4):
        columns = slice(number * wide, (number + 1) * wide)
        first = 2 * number * wide
        values_ref[:, columns] = dot(left, whole[:, first : first + wide]).astype(jnp.bfloat16)
    for start, members in lane_heads(width, heads):
        values = with_ones(values_ref[:, start : start + LANES])
        mixed = None
        for head, own in members:
            mixed = head_mix(expos_ref[head * count : (head + 1) * count], values, own, mixed)
        mixed_ref[:, start : start + LANES] = mixed.astype(jnp.bfloat16)
    mixed = mixed_ref[...]
    for number in range(4):
        columns = slice(number * wide, (number + 1) * wide)
        first = (2 * number + 1) * wide
        z_ref[:, columns] = (merged[:, columns] + dot(mixed, whole[:, first : first + wide])).astype(jnp.bfloat16)
    first = 0
    for packet in packets:
        height = packet.shape[0]
        packet[...] = dot(pick_ref[first : first + height], z_ref[...]).astype(jnp.bfloat16)
        first += height


def place_kernel(select_hbm, own_ref, lat_ref, lon_ref, both_ref, out_ref, select_ref, stage_ref, sems):
    loads = fetch(sems, (select_hbm, select_ref))
    fill(stage_ref, (own_ref, lat_ref, lon_ref, both_ref))
    loads[0].wait()
    out_ref[...] = dot(select_ref[...], stage_ref[...]).astype(out_ref.dtype)


def call(kernel, outs, scratch, scalars=(), hbm=(), vmem=(), hbm_outs=(), pinned=False):
    if pinned:
        hbm = [pltpu.with_memory_space_constraint(array, pltpu.HBM) for array in hbm]
    spaces = [pltpu.SMEM] * len(scalars) + [pltpu.HBM] * len(hbm) + [pltpu.VMEM] * len(vmem)
    return pl.pallas_call(
        kernel,
        out_shape=[jax.ShapeDtypeStruct(shape, jnp.bfloat16) for shape in outs],
        in_specs=[pl.BlockSpec(memory_space=space) for space in spaces],
        out_specs=[
            pl.BlockSpec(memory_space=pltpu.HBM if number in hbm_outs else pltpu.VMEM)
            for number in range(len(outs))
        ],
        scratch_shapes=scratch,
        compiler_params=pltpu.CompilerParams(vmem_limit_bytes=VMEM_LIMIT),
    )(*scalars, *hbm, *vmem)


def shifted(blocks, step):
    lat, lon = lax.axis_size("lat"), lax.axis_size("lon")
    return (
        lax.ppermute(blocks[0], "lat", [(i, (i + step) % lat) for i in range(lat)]),
        lax.ppermute(blocks[1], "lon", [(i, (i + step) % lon) for i in range(lon)]),
        lax.ppermute(
            blocks[2],
            ("lat", "lon"),
            [(i * lon + j, (i + step) % lat * lon + (j + step) % lon) for i in range(lat) for j in range(lon)],
        ),
    )


def exchange(block, axis, mask):
    return lax.ppermute(block, axis, [(i, i ^ mask) for i in range(lax.axis_size(axis))])


def far_parts(part):
    ranks = lax.axis_size("lon")
    return [
        lax.ppermute(part, "lon", [(i, (i + 2 * back) % ranks) for i in range(ranks)])
        for back in range(1, ranks // 2)
    ]


def routed(block, turn):
    lat, lon = lax.axis_size("lat"), lax.axis_size("lon")
    pairs = [
        (i * lon + j, (i ^ (1 + (j + turn) % 2)) * lon + j) for i in range(lat) for j in range(lon)
    ]
    return lax.ppermute(block, ("lat", "lon"), pairs)


def joined(*plans):
    arrays = []
    for plan in plans:
        arrays += [array for array in plan if not any(array is seen for seen in arrays)]
    numbers = [[next(n for n, seen in enumerate(arrays) if seen is array) for array in plan] for plan in plans]
    shapes = [
        (sum(1 if array.ndim == 2 else array.shape[0] for array in plan),) + plan[0].shape[-2:] for plan in plans
    ]
    return call(
        lambda *refs: join_kernel(numbers, *refs),
        shapes,
        [pltpu.SemaphoreType.DMA((sum(len(plan) for plan in plans),))],
        hbm=arrays,
        hbm_outs=range(len(plans)),
    )


def swapped(pieces):
    return [exchange(piece, "lon", 1) for piece in pieces]


def after(value, *earlier):
    return lax.optimization_barrier((value, earlier))[0]


def dma(count):
    return pltpu.SemaphoreType.DMA((count,))


def bf16(*shape):
    return pltpu.VMEM(shape, jnp.bfloat16)


def per_device(
    tokens, level_ids, coarse_ids, first_qkv, first_out, merge_weight, second_qkv, second_out
):
    levels, height, breadth, width = tokens.shape
    _, low, narrow = coarse_ids.shape
    wider = merge_weight.shape[1]
    cells, coarse_cells = levels * height * breadth, levels * low * narrow
    stops = lax.axis_size("lon") // 2
    lat, lon = lax.axis_index("lat"), lax.axis_index("lon")
    at = jnp.stack([lat % 4, (lat == 0).astype(jnp.int32), lon % 2, lon // 2]).astype(jnp.int32)

    start = regions(levels, height, breadth, 0, 0)
    middle = regions(levels, height, breadth, HALF_ROWS, HALF_COLS)
    end = regions(levels, low, narrow, 0, 0)
    counts = [len(part) for part in start]
    packet_rows = [up(len(part) + 2, PACK) for part in start]
    end_rows = [up(len(part) + 2, PACK) for part in end]
    order = window_order(levels, height, breadth)
    inverse = np.argsort(order)
    rows = second_out.shape[0]

    def picks(parts, counts, columns):
        return [matrix(part, columns, count) for part, count in zip(parts, counts)]

    def spreader(columns, count):
        return matrix(np.arange(count) % columns, up(columns, PACK)).T

    fine = jnp.concatenate(picks(start, [LANES] * 3, cells) + [spreader(breadth, cells)])
    coarse = jnp.concatenate(picks(end, [LANES] * 3, coarse_cells) + [spreader(narrow, coarse_cells)])
    x = tokens.reshape(cells, width)
    *packets, labels, coarse_labels, owns, merge_part, score_part, value_part = call(
        lambda *refs: pack_kernel(counts, *refs),
        [(count, width) for count in packet_rows]
        + [(8, cells), (8, coarse_cells), (12, rows, wider // 2)]
        + [(rows, wider // 2)] * 3,
        [
            bf16(cells, width),
            *[pltpu.VMEM((ids.shape[1], levels, ids.shape[2]), jnp.int32) for ids in (level_ids, coarse_ids)],
            bf16(*fine.shape),
            bf16(*coarse.shape),
            dma(25),
        ],
        scalars=(at,),
        hbm=(x, *[ids.transpose(1, 0, 2) for ids in (level_ids, coarse_ids)], fine, coarse, merge_weight, second_qkv, second_out),
        hbm_outs=(5, 6, 7, 8),
        pinned=True,
    )
    got = shifted(packets, -1)
    far = stops - 1

    (near1,) = joined(after(far_parts(merge_part), got))
    first1 = routed(near1, 0)
    far2 = far_parts(after(score_part, near1))
    (other,) = swapped([after(owns, near1)])
    source, depth = replaced(cells, start)
    held = np.empty_like(order)
    held[order] = np.arange(cells)
    select = matrix(source[order], depth)
    pick = jnp.concatenate(
        picks([inverse[part] for part in middle], packet_rows, cells)
        + picks([inverse[part] for part in start], packet_rows, cells)
    )
    got_first = got
    y, *packets = call(
        lambda *refs: first_kernel(HEADS1, counts, *refs),
        [(cells, width)] + [(count, width) for count in packet_rows] * 2,
        [
            bf16(*select.shape),
            bf16(*first_qkv.shape),
            bf16(*first_out.shape),
            bf16(*pick.shape),
            bf16(depth, width),
            pltpu.VMEM((cells, width), jnp.float32),
            bf16(cells, 3 * width),
            bf16(cells, width),
            dma(5),
        ],
        hbm=(x, select, first_qkv, first_out, pick),
        vmem=(labels, *got_first),
    )
    (near2,) = joined(after(far2, first1, y, other))
    first2 = routed(near2, 0)
    far3 = far_parts(after(value_part, near2))
    (join1,) = joined(after([near1, first1], near2))
    second1 = routed(join1, 1)
    (near3,) = joined(after(far3, first2, second1))
    first3 = routed(near3, 0)
    (join2,) = joined(after([near2, first2], near3))
    second2 = routed(join2, 1)
    mid = shifted(after(packets[:3], near3), -1)
    last_first = after(first3, second2, mid)
    (join3,) = joined([near3, last_first])
    second3 = routed(join3, 1)
    merge_pieces = (owns, join1, second1, other, *swapped(after((join1, second1), last_first)))
    score_pieces = (owns, join2, second2, other, *swapped(after((join2, second2), last_first)))

    def plan(group):
        return [
            [(own, 4 * group, 4), (own + 1, 0, far), (own + 1, far, far), (own + 2, 0, far), (own + 2, far, far)]
            for own in (0, 3)
        ]

    merge_plan, score_plan, value_plan = plan(0), plan(1), plan(2)

    source, depth = replaced(cells, middle, held)
    fine = source.reshape(levels, low, 2, narrow, 2)
    patches = [fine[:, :, r, :, c].reshape(-1) for r, c in ((0, 0), (1, 0), (0, 1), (1, 1))]
    select = matrix(np.concatenate(patches), depth)
    (merged,) = call(
        lambda *refs: merge_kernel(len(merge_pieces), merge_plan, *refs),
        [(coarse_cells, wider)],
        [
            bf16(*select.shape),
            bf16(depth, width),
            bf16(stops, 2, *merge_weight.shape),
            dma(1),
            dma(piece_copies(stops)),
        ],
        scalars=(at,),
        hbm=(select, *merge_pieces),
        vmem=(y, *mid),
    )

    back = shifted(after(packets[3:], merged), 1)
    source, depth = replaced(cells, start, held)
    select = matrix(source, depth)
    (skip,) = call(
        place_kernel,
        [(cells, width)],
        [bf16(*select.shape), bf16(depth, width), dma(1)],
        hbm=(select,),
        vmem=(y, *back),
    )

    source, depth = replaced(coarse_cells, end)
    select = matrix(source, depth)
    (expos,) = call(
        lambda *refs: scores_kernel(HEADS2, counts, len(score_pieces), score_plan, *refs),
        [(HEADS2 * coarse_cells, coarse_cells)],
        [
            bf16(*select.shape),
            bf16(stops, 2, rows, 2 * wider),
            bf16(coarse_cells, 2 * wider),
            dma(1),
            dma(piece_copies(stops)),
        ],
        scalars=(at,),
        hbm=(select, *score_pieces),
        vmem=(merged, coarse_labels, *got),
    )
    value_swapped = swapped([after(join3, last_first), after(second3, back, expos)])
    value_pieces = (owns, join3, second3, other, *value_swapped)
    pick = jnp.concatenate(picks(end, end_rows, coarse_cells))
    z, *packets = call(
        lambda *refs: close_kernel(HEADS2, len(value_pieces), value_plan, *refs),
        [(coarse_cells, wider)] + [(count, wider) for count in end_rows],
        [
            bf16(*pick.shape),
            bf16(stops, 2, rows, 2 * wider),
            bf16(coarse_cells, wider),
            bf16(coarse_cells, wider),
            dma(1),
            dma(piece_copies(stops)),
        ],
        scalars=(at,),
        hbm=(pick, *value_pieces),
        vmem=(merged, expos),
    )
    done = shifted(packets, 1)
    (coarse,) = call(
        place_kernel,
        [(coarse_cells, wider)],
        [bf16(*select.shape), bf16(depth, wider), dma(1)],
        hbm=(select,),
        vmem=(z, *done),
    )
    return skip.reshape(tokens.shape), coarse.reshape(levels, low, narrow, wider)


def solution(mesh):
    placed = (
        P(None, "lat", "lon", None),
        P(None, "lat", "lon"),
        P(None, "lat", "lon"),
        P(),
        P(),
        P("lon", None),
        P("lon", None),
        P("lon", None),
    )
    return jax.shard_map(
        per_device,
        mesh=mesh,
        in_specs=placed,
        out_specs=(P(None, "lat", "lon", None), P(None, "lat", "lon", None)),
        check_vma=False,
    )
```

```python
import math

import jax
import jax.numpy as jnp
import numpy as np
from jax import lax
from jax.experimental import pallas as pl
from jax.experimental.pallas import tpu as pltpu
from jax.sharding import PartitionSpec as P

HEADS1 = 8
HEADS2 = 16
WIN_LEVELS = 2
WIN_ROWS = 6
WIN_COLS = 12
HALF_ROWS = WIN_ROWS // 2
HALF_COLS = WIN_COLS // 2

EPSILON = 1e-05
EXCLUDED = -1e30
LANES = 128
PACK = 16
VMEM_LIMIT = 32 * 1024 * 1024
NT = (((1,), (1,)), ((), ()))


def up(count, unit):
    return -(-count // unit) * unit


def places(levels, rows, columns):
    return np.arange(levels * rows * columns).reshape(levels, rows, columns)


def regions(levels, rows, columns, row_from, column_from):
    at = places(levels, rows, columns)
    in_rows = (np.arange(rows) >= row_from) & (np.arange(rows) < row_from + HALF_ROWS)
    in_columns = (np.arange(columns) >= column_from) & (np.arange(columns) < column_from + HALF_COLS)
    picked = (
        at[:, in_rows][:, :, ~in_columns],
        at[:, ~in_rows][:, :, in_columns],
        at[:, in_rows][:, :, in_columns],
    )
    return [part.reshape(-1) for part in picked]


def window_order(levels, rows, columns):
    at = places(levels, rows, columns)
    order = []
    for band in range(rows // WIN_ROWS):
        for across in range(columns // WIN_COLS):
            r = (HALF_ROWS + WIN_ROWS * band + np.arange(WIN_ROWS)) % rows
            c = (HALF_COLS + WIN_COLS * across + np.arange(WIN_COLS)) % columns
            order.append(at[:, r][:, :, c].reshape(-1))
    return np.concatenate(order)


def matrix(sources, columns, height=None):
    out = np.zeros((height or len(sources), columns), np.float32)
    out[np.arange(len(sources)), sources] = 1
    return jnp.asarray(out, jnp.bfloat16)


def offsets(sizes):
    return np.concatenate([[0], np.cumsum([up(size, LANES) for size in sizes])]).tolist()


def replaced(count, parts, held=None):
    starts = offsets([count] + [up(len(part) + 2, PACK) for part in parts])
    source = np.arange(count) if held is None else held.copy()
    for start, part in zip(starts[1:], parts):
        source[part] = start + np.arange(len(part))
    return source, starts[-1]


def fill(stage_ref, parts, held=0):
    start = 0
    for part in parts:
        rows = held if part is None else part.shape[0]
        if part is not None:
            stage_ref[start : start + rows] = part[...]
        if rows % LANES:
            stage_ref[start + rows : start + up(rows, LANES)] = jnp.zeros(
                (up(rows, LANES) - rows, stage_ref.shape[1]), stage_ref.dtype
            )
        start += up(rows, LANES)


def dot(left, right):
    return jnp.dot(left, right, preferred_element_type=jnp.float32)


def dot_nt(left, right):
    return lax.dot_general(left, right, NT, preferred_element_type=jnp.float32)


def normalized(values):
    center = jnp.mean(values, axis=-1, keepdims=True)
    moved = values - center
    spread = jnp.mean(moved * moved, axis=-1, keepdims=True)
    return (moved * lax.rsqrt(spread + EPSILON)).astype(jnp.bfloat16)


def label_bias(wide, select):
    along = dot_nt(wide, select)[:1]
    down = dot_nt(select, wide)[:, :1]
    return jnp.where(down == along, 0.0, EXCLUDED)


def lane_heads(width, heads):
    head_size = width // heads
    lane = lax.broadcasted_iota(jnp.int32, (1, LANES), 1)
    for start in range(0, width, LANES):
        yield start, [
            ((start + low) // head_size, (lane >= low) & (lane < low + head_size))
            for low in range(0, LANES, head_size)
        ]


def head_expos(queries, keys, own, head_size, bias):
    chosen = jnp.where(own, 1.0 / math.sqrt(head_size), 0.0).astype(jnp.bfloat16)
    scores = dot_nt(queries * chosen, keys) + bias
    highest = jnp.max(scores, axis=-1, keepdims=True)
    return jnp.exp(scores - highest).astype(jnp.bfloat16)


def head_mix(expos, values, own, mixed):
    summed = dot(expos, values)
    result = summed[:, :LANES] / summed[:, LANES:]
    return result if mixed is None else jnp.where(own, result, mixed)


def with_ones(values):
    return jnp.concatenate([values, jnp.ones(values.shape, values.dtype)], axis=1)


def attend(packed_ref, mixed_ref, first, count, width, heads, bias):
    rows = slice(first, first + count)
    for start, members in lane_heads(width, heads):
        queries = packed_ref[rows, start : start + LANES]
        keys = packed_ref[rows, width + start : width + start + LANES]
        values = with_ones(packed_ref[rows, 2 * width + start : 2 * width + start + LANES])
        mixed = None
        for _, own in members:
            expos = head_expos(queries, keys, own, width // heads, bias)
            mixed = head_mix(expos, values, own, mixed)
        mixed_ref[rows, start : start + LANES] = mixed.astype(jnp.bfloat16)


def fetch(sems, *pairs):
    copies = [pltpu.make_async_copy(source, target, sems.at[n]) for n, (source, target) in enumerate(pairs)]
    for copy in copies:
        copy.start()
    return copies


def flat_labels(ids_ref, edge, spread):
    rows, levels, columns = ids_ref.shape
    total = 0.0
    for level in range(levels):
        row = lax.broadcasted_iota(jnp.int32, (rows, columns), 0)
        labels = ids_ref[:, level, :] * 2 + jnp.where(row < HALF_ROWS, edge, 0)
        wide = dot(labels.astype(jnp.float32).astype(jnp.bfloat16), spread)
        place = lax.broadcasted_iota(jnp.int32, wide.shape, 1)
        low = (level * rows + lax.broadcasted_iota(jnp.int32, wide.shape, 0)) * columns
        own = (place >= low) & (place < low + columns)
        total += jnp.sum(jnp.where(own, wide, 0.0), axis=0, keepdims=True)
    return jnp.broadcast_to(total, (8, total.shape[1])).astype(jnp.bfloat16)


def block_sources(group, block, merge_ref, qkv_ref, out_ref):
    rows, wide = out_ref.shape[0], out_ref.shape[1] // 2
    if group == 0:
        at_row = pl.multiple_of((block // 2) * rows, PACK)
        at_column = pl.multiple_of((block % 2) * wide, LANES)
        return [(merge_ref.at[pl.ds(at_row, rows), pl.ds(at_column, wide)], pl.ds(0, wide))]
    if group == 1:
        return [(qkv_ref.at[:, pl.ds(pl.multiple_of(block * wide, LANES), wide)], pl.ds(0, wide))]
    half = wide // 2
    return [
        (qkv_ref.at[:, pl.ds(pl.multiple_of(4 * wide + block * half, LANES), half)], pl.ds(0, half)),
        (out_ref.at[:, pl.ds(pl.multiple_of(block * half, LANES), half)], pl.ds(half, half)),
    ]


def pack_kernel(counts, at_ref, x_hbm, ids_hbm, coarse_ids_hbm, fine_hbm, coarse_hbm, *refs):
    weights, outs, labels_ref, coarse_labels_ref, owns_ref, parts = refs[:3], refs[3:6], *refs[6:9], refs[9:12]
    x_ref, ids_ref, coarse_ids_ref, fine_ref, coarse_ref, sems = refs[12:]
    edge = at_ref[1]
    pairs = []
    for group, part in enumerate(parts):
        for source, columns in block_sources(group, at_ref[0], *weights):
            pairs.append((source, part.at[:, columns]))
        for block in range(4):
            for source, columns in block_sources(group, block, *weights):
                pairs.append((source, owns_ref.at[4 * group + block, :, columns]))
    copies = fetch(
        sems,
        (ids_hbm, ids_ref),
        (coarse_ids_hbm, coarse_ids_ref),
        (coarse_hbm, coarse_ref),
        (fine_hbm, fine_ref),
        (x_hbm, x_ref),
        *pairs,
    )
    for load in copies[:4]:
        load.wait()
    picks = 3 * LANES
    labels = flat_labels(ids_ref, edge, fine_ref[picks : picks + ids_ref.shape[2]])
    coarse_labels = flat_labels(coarse_ids_ref, edge, coarse_ref[picks : picks + coarse_ids_ref.shape[2]])
    labels_ref[...] = labels
    coarse_labels_ref[...] = coarse_labels
    copies[4].wait()
    for number, (packet, count) in enumerate(zip(outs, counts)):
        height = packet.shape[0]
        first = number * LANES
        body = dot(fine_ref[first : first + height], x_ref[...])
        row = lax.broadcasted_iota(jnp.int32, (height, LANES), 0)
        fine = dot_nt(labels, fine_ref[first : first + LANES])[:1]
        coarse = dot_nt(coarse_labels, coarse_ref[first : first + LANES])[:1]
        extra = jnp.where(row == count, fine, jnp.where(row == count + 1, coarse, 0.0))
        packet[:, :LANES] = (body[:, :LANES] + extra).astype(packet.dtype)
        packet[:, LANES:] = body[:, LANES:].astype(packet.dtype)
    for copy in copies[5:]:
        copy.wait()


def wide_labels(labels_ref, packets, counts, line):
    count = labels_ref.shape[1]
    pad = up(count, LANES) - count
    parts = [labels_ref[...].astype(jnp.float32)]
    if pad:
        parts[0] = jnp.concatenate([parts[0], jnp.zeros((8, pad), jnp.float32)], axis=1)
    for packet, size in zip(packets, counts):
        block = packet[size // PACK * PACK : size // PACK * PACK + PACK, :LANES].astype(jnp.float32)
        row = lax.broadcasted_iota(jnp.int32, block.shape, 0)
        picked = jnp.sum(jnp.where(row == size % PACK + line, block, 0.0), axis=0, keepdims=True)
        parts.append(jnp.broadcast_to(picked, (8, LANES)))
    return jnp.concatenate(parts, axis=1).astype(jnp.bfloat16)


def first_kernel(
    heads, counts, x_hbm, select_hbm, qkv_hbm, out_hbm, pick_hbm,
    labels_ref, lat_ref, lon_ref, both_ref, y_ref, *refs,
):
    packets, refs = refs[:6], refs[6:]
    select_ref, qkv_ref, out_ref, pick_ref, stage_ref, rolled_ref, packed_ref, mixed_ref, sems = refs
    cells, width = x_hbm.shape
    window = WIN_LEVELS * WIN_ROWS * WIN_COLS
    loads = fetch(
        sems,
        (x_hbm, stage_ref.at[pl.ds(0, cells)]),
        (select_hbm, select_ref),
        (qkv_hbm, qkv_ref),
        (out_hbm, out_ref),
        (pick_hbm, pick_ref),
    )
    fill(stage_ref, (None, lat_ref, lon_ref, both_ref), cells)
    wide = wide_labels(labels_ref, (lat_ref, lon_ref, both_ref), counts, 0)
    loads[0].wait()
    loads[1].wait()
    rolled = dot(select_ref[...], stage_ref[...])
    rolled_ref[...] = rolled
    loads[2].wait()
    packed_ref[...] = dot(normalized(rolled), qkv_ref[...]).astype(jnp.bfloat16)
    for first in range(0, cells, window):
        bias = label_bias(wide, select_ref[first : first + window])
        attend(packed_ref, mixed_ref, first, window, width, heads, bias)
    loads[3].wait()
    y_ref[...] = (rolled_ref[...] + dot(mixed_ref[...], out_ref[...])).astype(jnp.bfloat16)
    loads[4].wait()
    first = 0
    for packet in packets:
        height = packet.shape[0]
        packet[...] = dot(pick_ref[first : first + height], y_ref[...]).astype(jnp.bfloat16)
        first += height


def join_kernel(plans, *refs):
    sems, outs = refs[-1], refs[-1 - len(plans) : -1]
    pairs = []
    for plan, out_ref in zip(plans, outs):
        first = 0
        for number in plan:
            part = refs[number]
            if len(part.shape) == 2:
                pairs.append((part, out_ref.at[first]))
                first += 1
            else:
                pairs.append((part, out_ref.at[pl.ds(first, part.shape[0])]))
                first += part.shape[0]
    for copy in fetch(sems, *pairs):
        copy.wait()


def start_pieces(whole_ref, sides, at_ref, sems):
    corner, side, here = at_ref[0], at_ref[2], at_ref[3]
    stops = whole_ref.shape[0]
    copies = []

    def put(source, stop, from_side, block):
        rows, wide = source.shape
        held = whole_ref.at[stop, from_side]
        across = whole_ref.shape[3] // wide
        at_row, at_column = (block // across) * rows, (block % across) * wide
        target = held.at[pl.ds(pl.multiple_of(at_row, PACK), rows), pl.ds(pl.multiple_of(at_column, LANES), wide)]
        copies.append(pltpu.make_async_copy(source, target, sems.at[len(copies)]))
        copies[-1].start()

    for other, (own, *stacks) in enumerate(sides):
        from_side = side ^ other
        for block in range(4):
            put(own.at[block], here, from_side, block)
        for stack, mask in zip(stacks, (0, 1 + from_side, 2 - from_side, 3)):
            for back in range(1, stops):
                put(stack.at[back - 1], lax.rem(here + (stops - back), stops), from_side, corner ^ mask)
    return copies


def piece_copies(stops):
    return 2 * (4 + 4 * (stops - 1))


def flat(whole_ref):
    stops, sides, rows, columns = whole_ref.shape
    return whole_ref[...].reshape(stops * sides * rows, columns)


def cuts(refs, plan):
    return [[refs[number].at[pl.ds(first, count)] for number, first, count in side] for side in plan]


def merge_kernel(heads, counts, number, plans, at_ref, select_hbm, coarse_select_hbm, *refs):
    pieces, refs = refs[:number], refs[number:]
    (y_ref, lat_ref, lon_ref, both_ref), labels_ref, packets = refs[:4], refs[4], refs[5:8]
    merged_ref, expos_ref, select_ref, coarse_select_ref, stage_ref = refs[8:13]
    merge_ref, score_ref, packed_ref, sems, merge_sems, score_sems = refs[13:]
    loads = fetch(sems, (select_hbm, select_ref), (coarse_select_hbm, coarse_select_ref))
    merge_copies = start_pieces(merge_ref, cuts(pieces, plans[0]), at_ref, merge_sems)
    score_copies = start_pieces(score_ref, cuts(pieces, plans[1]), at_ref, score_sems)
    fill(stage_ref, (y_ref, lat_ref, lon_ref, both_ref))
    count, width = merged_ref.shape
    loads[0].wait()
    patches = [
        dot(select_ref[first : first + count], stage_ref[...]) for first in range(0, select_ref.shape[0], count)
    ]
    total = 1.0 / (len(patches) * y_ref.shape[1])
    center = sum(jnp.sum(patch, axis=-1, keepdims=True) for patch in patches) * total
    moved = [patch - center for patch in patches]
    spread = sum(jnp.sum(patch * patch, axis=-1, keepdims=True) for patch in moved) * total
    scale = lax.rsqrt(spread + EPSILON)
    left = jnp.concatenate([(patch * scale).astype(jnp.bfloat16) for patch in moved], axis=1)
    wide = wide_labels(labels_ref, packets, counts, 1)
    loads[1].wait()
    bias = label_bias(wide, coarse_select_ref[...])
    for copy in merge_copies:
        copy.wait()
    merged = dot(left, flat(merge_ref)).astype(jnp.bfloat16)
    merged_ref[...] = merged
    left = normalized(merged.astype(jnp.float32))
    for copy in score_copies:
        copy.wait()
    packed_ref[...] = dot(left, flat(score_ref)).astype(jnp.bfloat16)
    for start, members in lane_heads(width, heads):
        queries = packed_ref[:, start : start + LANES]
        keys = packed_ref[:, width + start : width + start + LANES]
        for head, own in members:
            expos = head_expos(queries, keys, own, width // heads, bias)
            expos_ref[head * count : (head + 1) * count] = expos


def close_kernel(heads, number, plan, at_ref, pick_hbm, *refs):
    pieces, (merged_ref, expos_ref, z_ref) = cuts(refs[:number], plan), refs[number : number + 3]
    packets, refs = refs[number + 3 : number + 6], refs[number + 6 :]
    pick_ref, whole_ref, values_ref, mixed_ref, sems, piece_sems = refs
    copies = fetch(sems, (pick_hbm, pick_ref)) + start_pieces(whole_ref, pieces, at_ref, piece_sems)
    count, width = merged_ref.shape
    merged = merged_ref[...].astype(jnp.float32)
    left = normalized(merged)
    for copy in copies:
        copy.wait()
    whole = flat(whole_ref)
    wide = width // 4
    for number in range(4):
        columns = slice(number * wide, (number + 1) * wide)
        first = 2 * number * wide
        values_ref[:, columns] = dot(left, whole[:, first : first + wide]).astype(jnp.bfloat16)
    for start, members in lane_heads(width, heads):
        values = with_ones(values_ref[:, start : start + LANES])
        mixed = None
        for head, own in members:
            mixed = head_mix(expos_ref[head * count : (head + 1) * count], values, own, mixed)
        mixed_ref[:, start : start + LANES] = mixed.astype(jnp.bfloat16)
    mixed = mixed_ref[...]
    for number in range(4):
        columns = slice(number * wide, (number + 1) * wide)
        first = (2 * number + 1) * wide
        z_ref[:, columns] = (merged[:, columns] + dot(mixed, whole[:, first : first + wide])).astype(jnp.bfloat16)
    first = 0
    for packet in packets:
        height = packet.shape[0]
        packet[...] = dot(pick_ref[first : first + height], z_ref[...]).astype(jnp.bfloat16)
        first += height


def place_kernel(select_hbm, own_ref, lat_ref, lon_ref, both_ref, out_ref, select_ref, stage_ref, sems):
    loads = fetch(sems, (select_hbm, select_ref))
    fill(stage_ref, (own_ref, lat_ref, lon_ref, both_ref))
    loads[0].wait()
    out_ref[...] = dot(select_ref[...], stage_ref[...]).astype(out_ref.dtype)


def call(kernel, outs, scratch, scalars=(), hbm=(), vmem=(), hbm_outs=(), pinned=False):
    if pinned:
        hbm = [pltpu.with_memory_space_constraint(array, pltpu.HBM) for array in hbm]
    spaces = [pltpu.SMEM] * len(scalars) + [pltpu.HBM] * len(hbm) + [pltpu.VMEM] * len(vmem)
    return pl.pallas_call(
        kernel,
        out_shape=[jax.ShapeDtypeStruct(shape, jnp.bfloat16) for shape in outs],
        in_specs=[pl.BlockSpec(memory_space=space) for space in spaces],
        out_specs=[
            pl.BlockSpec(memory_space=pltpu.HBM if number in hbm_outs else pltpu.VMEM)
            for number in range(len(outs))
        ],
        scratch_shapes=scratch,
        compiler_params=pltpu.CompilerParams(vmem_limit_bytes=VMEM_LIMIT),
    )(*scalars, *hbm, *vmem)


def shifted(blocks, step):
    lat, lon = lax.axis_size("lat"), lax.axis_size("lon")
    return (
        lax.ppermute(blocks[0], "lat", [(i, (i + step) % lat) for i in range(lat)]),
        lax.ppermute(blocks[1], "lon", [(i, (i + step) % lon) for i in range(lon)]),
        lax.ppermute(
            blocks[2],
            ("lat", "lon"),
            [(i * lon + j, (i + step) % lat * lon + (j + step) % lon) for i in range(lat) for j in range(lon)],
        ),
    )


def exchange(block, axis, mask):
    return lax.ppermute(block, axis, [(i, i ^ mask) for i in range(lax.axis_size(axis))])


def far_parts(part):
    ranks = lax.axis_size("lon")
    return [
        lax.ppermute(part, "lon", [(i, (i + 2 * back) % ranks) for i in range(ranks)])
        for back in range(1, ranks // 2)
    ]


def routed(block, turn):
    lat, lon = lax.axis_size("lat"), lax.axis_size("lon")
    pairs = [
        (i * lon + j, (i ^ (1 + (j + turn) % 2)) * lon + j) for i in range(lat) for j in range(lon)
    ]
    return lax.ppermute(block, ("lat", "lon"), pairs)


def joined(*plans):
    arrays = []
    for plan in plans:
        arrays += [array for array in plan if not any(array is seen for seen in arrays)]
    numbers = [[next(n for n, seen in enumerate(arrays) if seen is array) for array in plan] for plan in plans]
    shapes = [
        (sum(1 if array.ndim == 2 else array.shape[0] for array in plan),) + plan[0].shape[-2:] for plan in plans
    ]
    return call(
        lambda *refs: join_kernel(numbers, *refs),
        shapes,
        [pltpu.SemaphoreType.DMA((sum(len(plan) for plan in plans),))],
        hbm=arrays,
        hbm_outs=range(len(plans)),
    )


def swapped(pieces):
    return [exchange(piece, "lon", 1) for piece in pieces]


def after(value, *earlier):
    return lax.optimization_barrier((value, earlier))[0]


def dma(count):
    return pltpu.SemaphoreType.DMA((count,))


def bf16(*shape):
    return pltpu.VMEM(shape, jnp.bfloat16)


def per_device(
    tokens, level_ids, coarse_ids, first_qkv, first_out, merge_weight, second_qkv, second_out
):
    levels, height, breadth, width = tokens.shape
    _, low, narrow = coarse_ids.shape
    wider = merge_weight.shape[1]
    cells, coarse_cells = levels * height * breadth, levels * low * narrow
    stops = lax.axis_size("lon") // 2
    lat, lon = lax.axis_index("lat"), lax.axis_index("lon")
    at = jnp.stack([lat % 4, (lat == 0).astype(jnp.int32), lon % 2, lon // 2]).astype(jnp.int32)

    start = regions(levels, height, breadth, 0, 0)
    middle = regions(levels, height, breadth, HALF_ROWS, HALF_COLS)
    end = regions(levels, low, narrow, 0, 0)
    counts = [len(part) for part in start]
    packet_rows = [up(len(part) + 2, PACK) for part in start]
    end_rows = [up(len(part) + 2, PACK) for part in end]
    order = window_order(levels, height, breadth)
    inverse = np.argsort(order)
    rows = second_out.shape[0]

    def picks(parts, counts, columns):
        return [matrix(part, columns, count) for part, count in zip(parts, counts)]

    def spreader(columns, count):
        return matrix(np.arange(count) % columns, up(columns, PACK)).T

    fine = jnp.concatenate(picks(start, [LANES] * 3, cells) + [spreader(breadth, cells)])
    coarse = jnp.concatenate(picks(end, [LANES] * 3, coarse_cells) + [spreader(narrow, coarse_cells)])
    x = tokens.reshape(cells, width)
    *packets, labels, coarse_labels, owns, merge_part, score_part, value_part = call(
        lambda *refs: pack_kernel(counts, *refs),
        [(count, width) for count in packet_rows]
        + [(8, cells), (8, coarse_cells), (12, rows, wider // 2)]
        + [(rows, wider // 2)] * 3,
        [
            bf16(cells, width),
            *[pltpu.VMEM((ids.shape[1], levels, ids.shape[2]), jnp.int32) for ids in (level_ids, coarse_ids)],
            bf16(*fine.shape),
            bf16(*coarse.shape),
            dma(25),
        ],
        scalars=(at,),
        hbm=(x, *[ids.transpose(1, 0, 2) for ids in (level_ids, coarse_ids)], fine, coarse, merge_weight, second_qkv, second_out),
        hbm_outs=(5, 6, 7, 8),
        pinned=True,
    )
    got = shifted(packets, -1)
    far = stops - 1

    (near1,) = joined(after(far_parts(merge_part), got))
    first1 = routed(near1, 0)
    far2 = far_parts(after(score_part, near1))
    (other,) = swapped([after(owns, near1)])
    source, depth = replaced(cells, start)
    held = np.empty_like(order)
    held[order] = np.arange(cells)
    select = matrix(source[order], depth)
    pick = jnp.concatenate(
        picks([inverse[part] for part in middle], packet_rows, cells)
        + picks([inverse[part] for part in start], packet_rows, cells)
    )
    got_first = got
    y, *packets = call(
        lambda *refs: first_kernel(HEADS1, counts, *refs),
        [(cells, width)] + [(count, width) for count in packet_rows] * 2,
        [
            bf16(*select.shape),
            bf16(*first_qkv.shape),
            bf16(*first_out.shape),
            bf16(*pick.shape),
            bf16(depth, width),
            pltpu.VMEM((cells, width), jnp.float32),
            bf16(cells, 3 * width),
            bf16(cells, width),
            dma(5),
        ],
        hbm=(x, select, first_qkv, first_out, pick),
        vmem=(labels, *got_first),
    )
    (near2,) = joined(after(far2, first1, y, other))
    first2 = routed(near2, 0)
    far3 = far_parts(after(value_part, near2))
    (join1,) = joined(after([near1, first1], near2))
    second1 = routed(join1, 1)
    (near3,) = joined(after(far3, first2, second1))
    first3 = routed(near3, 0)
    (join2,) = joined(after([near2, first2], near3))
    second2 = routed(join2, 1)
    mid = shifted(after(packets[:3], near3), -1)
    last_first = after(first3, second2, mid)
    (join3,) = joined([near3, last_first])
    second3 = routed(join3, 1)
    early_pieces = (owns, join1, second1, other, *swapped(after((join1, second1), near3)))
    early_pieces += (join2, second2, *swapped(after((join2, second2), last_first)))

    def plan(group, *rest):
        return [
            [(own, 4 * group, 4), (n, 0, far), (n, far, far), (n + 1, 0, far), (n + 1, far, far)]
            for own, n in zip((0, 3), rest)
        ]

    early_plans, value_plan = (plan(0, 1, 4), plan(1, 6, 8)), plan(2, 1, 4)

    source, depth = replaced(cells, middle, held)
    fine = source.reshape(levels, low, 2, narrow, 2)
    patches = [fine[:, :, r, :, c].reshape(-1) for r, c in ((0, 0), (1, 0), (0, 1), (1, 1))]
    select = matrix(np.concatenate(patches), depth)
    fine_depth = depth
    source, depth = replaced(coarse_cells, end)
    coarse_select = matrix(source, depth)
    merged, expos = call(
        lambda *refs: merge_kernel(HEADS2, counts, len(early_pieces), early_plans, *refs),
        [(coarse_cells, wider), (HEADS2 * coarse_cells, coarse_cells)],
        [
            bf16(*select.shape),
            bf16(*coarse_select.shape),
            bf16(fine_depth, width),
            bf16(stops, 2, *merge_weight.shape),
            bf16(stops, 2, rows, 2 * wider),
            bf16(coarse_cells, 2 * wider),
            dma(2),
            dma(piece_copies(stops)),
            dma(piece_copies(stops)),
        ],
        scalars=(at,),
        hbm=(select, coarse_select, *early_pieces),
        vmem=(y, *mid, coarse_labels, *got),
    )

    back = shifted(after(packets[3:], last_first), 1)
    source, depth = replaced(cells, start, held)
    select = matrix(source, depth)
    (skip,) = call(
        place_kernel,
        [(cells, width)],
        [bf16(*select.shape), bf16(depth, width), dma(1)],
        hbm=(select,),
        vmem=(y, *back),
    )

    source, depth = replaced(coarse_cells, end)
    select = matrix(source, depth)
    value_swapped = swapped([after(join3, last_first), after(second3, back, expos)])
    value_pieces = (owns, join3, second3, other, *value_swapped)
    pick = jnp.concatenate(picks(end, end_rows, coarse_cells))
    z, *packets = call(
        lambda *refs: close_kernel(HEADS2, len(value_pieces), value_plan, *refs),
        [(coarse_cells, wider)] + [(count, wider) for count in end_rows],
        [
            bf16(*pick.shape),
            bf16(stops, 2, rows, 2 * wider),
            bf16(coarse_cells, wider),
            bf16(coarse_cells, wider),
            dma(1),
            dma(piece_copies(stops)),
        ],
        scalars=(at,),
        hbm=(pick, *value_pieces),
        vmem=(merged, expos),
    )
    done = shifted(packets, 1)
    (coarse,) = call(
        place_kernel,
        [(coarse_cells, wider)],
        [bf16(*select.shape), bf16(depth, wider), dma(1)],
        hbm=(select,),
        vmem=(z, *done),
    )
    return skip.reshape(tokens.shape), coarse.reshape(levels, low, narrow, wider)


def solution(mesh):
    placed = (
        P(None, "lat", "lon", None),
        P(None, "lat", "lon"),
        P(None, "lat", "lon"),
        P(),
        P(),
        P("lon", None),
        P("lon", None),
        P("lon", None),
    )
    return jax.shard_map(
        per_device,
        mesh=mesh,
        in_specs=placed,
        out_specs=(P(None, "lat", "lon", None), P(None, "lat", "lon", None)),
        check_vma=False,
    )
```

```python
import math

import jax
import jax.numpy as jnp
import numpy as np
from jax import lax
from jax.experimental import pallas as pl
from jax.experimental.pallas import tpu as pltpu
from jax.sharding import PartitionSpec as P

HEADS1 = 8
HEADS2 = 16
WIN_LEVELS = 2
WIN_ROWS = 6
WIN_COLS = 12
HALF_ROWS = WIN_ROWS // 2
HALF_COLS = WIN_COLS // 2

EPSILON = 1e-05
EXCLUDED = -1e30
LANES = 128
PACK = 16
VMEM_LIMIT = 32 * 1024 * 1024
NT = (((1,), (1,)), ((), ()))


def up(count, unit):
    return -(-count // unit) * unit


def places(levels, rows, columns):
    return np.arange(levels * rows * columns).reshape(levels, rows, columns)


def regions(levels, rows, columns, row_from, column_from):
    at = places(levels, rows, columns)
    in_rows = (np.arange(rows) >= row_from) & (np.arange(rows) < row_from + HALF_ROWS)
    in_columns = (np.arange(columns) >= column_from) & (np.arange(columns) < column_from + HALF_COLS)
    picked = (
        at[:, in_rows][:, :, ~in_columns],
        at[:, ~in_rows][:, :, in_columns],
        at[:, in_rows][:, :, in_columns],
    )
    return [part.reshape(-1) for part in picked]


def window_order(levels, rows, columns):
    at = places(levels, rows, columns)
    order = []
    for band in range(rows // WIN_ROWS):
        for across in range(columns // WIN_COLS):
            r = (HALF_ROWS + WIN_ROWS * band + np.arange(WIN_ROWS)) % rows
            c = (HALF_COLS + WIN_COLS * across + np.arange(WIN_COLS)) % columns
            order.append(at[:, r][:, :, c].reshape(-1))
    return np.concatenate(order)


def matrix(sources, columns, height=None):
    out = np.zeros((height or len(sources), columns), np.float32)
    out[np.arange(len(sources)), sources] = 1
    return jnp.asarray(out, jnp.bfloat16)


def offsets(sizes):
    return np.concatenate([[0], np.cumsum([up(size, LANES) for size in sizes])]).tolist()


def replaced(count, parts, held=None):
    starts = offsets([count] + [up(len(part) + 2, PACK) for part in parts])
    source = np.arange(count) if held is None else held.copy()
    for start, part in zip(starts[1:], parts):
        source[part] = start + np.arange(len(part))
    return source, starts[-1]


def fill(stage_ref, parts, held=0):
    start = 0
    for part in parts:
        rows = held if part is None else part.shape[0]
        if part is not None:
            stage_ref[start : start + rows] = part[...]
        if rows % LANES:
            stage_ref[start + rows : start + up(rows, LANES)] = jnp.zeros(
                (up(rows, LANES) - rows, stage_ref.shape[1]), stage_ref.dtype
            )
        start += up(rows, LANES)


def dot(left, right):
    return jnp.dot(left, right, preferred_element_type=jnp.float32)


def dot_nt(left, right):
    return lax.dot_general(left, right, NT, preferred_element_type=jnp.float32)


def normalized(values):
    center = jnp.mean(values, axis=-1, keepdims=True)
    moved = values - center
    spread = jnp.mean(moved * moved, axis=-1, keepdims=True)
    return (moved * lax.rsqrt(spread + EPSILON)).astype(jnp.bfloat16)


def label_bias(wide, select):
    along = dot_nt(wide, select)[:1]
    down = dot_nt(select, wide)[:, :1]
    return jnp.where(down == along, 0.0, EXCLUDED)


def lane_heads(width, heads):
    head_size = width // heads
    lane = lax.broadcasted_iota(jnp.int32, (1, LANES), 1)
    for start in range(0, width, LANES):
        yield start, [
            ((start + low) // head_size, (lane >= low) & (lane < low + head_size))
            for low in range(0, LANES, head_size)
        ]


def head_expos(queries, keys, own, head_size, bias):
    chosen = jnp.where(own, 1.0 / math.sqrt(head_size), 0.0).astype(jnp.bfloat16)
    scores = dot_nt(queries * chosen, keys) + bias
    highest = jnp.max(scores, axis=-1, keepdims=True)
    return jnp.exp(scores - highest).astype(jnp.bfloat16)


def head_mix(expos, values, own, mixed):
    summed = dot(expos, values)
    result = summed[:, :LANES] / summed[:, LANES:]
    return result if mixed is None else jnp.where(own, result, mixed)


def with_ones(values):
    return jnp.concatenate([values, jnp.ones(values.shape, values.dtype)], axis=1)


def attend(packed_ref, mixed_ref, first, count, width, heads, bias):
    rows = slice(first, first + count)
    for start, members in lane_heads(width, heads):
        queries = packed_ref[rows, start : start + LANES]
        keys = packed_ref[rows, width + start : width + start + LANES]
        values = with_ones(packed_ref[rows, 2 * width + start : 2 * width + start + LANES])
        mixed = None
        for _, own in members:
            expos = head_expos(queries, keys, own, width // heads, bias)
            mixed = head_mix(expos, values, own, mixed)
        mixed_ref[rows, start : start + LANES] = mixed.astype(jnp.bfloat16)


def fetch(sems, *pairs):
    copies = [pltpu.make_async_copy(source, target, sems.at[n]) for n, (source, target) in enumerate(pairs)]
    for copy in copies:
        copy.start()
    return copies


def flat_labels(ids_ref, edge, spread):
    rows, levels, columns = ids_ref.shape
    total = 0.0
    for level in range(levels):
        row = lax.broadcasted_iota(jnp.int32, (rows, columns), 0)
        labels = ids_ref[:, level, :] * 2 + jnp.where(row < HALF_ROWS, edge, 0)
        wide = dot(labels.astype(jnp.float32).astype(jnp.bfloat16), spread)
        place = lax.broadcasted_iota(jnp.int32, wide.shape, 1)
        low = (level * rows + lax.broadcasted_iota(jnp.int32, wide.shape, 0)) * columns
        own = (place >= low) & (place < low + columns)
        total += jnp.sum(jnp.where(own, wide, 0.0), axis=0, keepdims=True)
    return jnp.broadcast_to(total, (8, total.shape[1])).astype(jnp.bfloat16)


def block_sources(group, block, merge_ref, qkv_ref, out_ref):
    rows, wide = out_ref.shape[0], out_ref.shape[1] // 2
    if group == 0:
        at_row = pl.multiple_of((block // 2) * rows, PACK)
        at_column = pl.multiple_of((block % 2) * wide, LANES)
        return [(merge_ref.at[pl.ds(at_row, rows), pl.ds(at_column, wide)], pl.ds(0, wide))]
    if group == 1:
        return [(qkv_ref.at[:, pl.ds(pl.multiple_of(block * wide, LANES), wide)], pl.ds(0, wide))]
    half = wide // 2
    return [
        (qkv_ref.at[:, pl.ds(pl.multiple_of(4 * wide + block * half, LANES), half)], pl.ds(0, half)),
        (out_ref.at[:, pl.ds(pl.multiple_of(block * half, LANES), half)], pl.ds(half, half)),
    ]


def pack_kernel(counts, at_ref, x_hbm, ids_hbm, coarse_ids_hbm, fine_hbm, coarse_hbm, *refs):
    weights, outs, labels_ref, coarse_labels_ref, owns_ref, parts = refs[:3], refs[3:6], *refs[6:9], refs[9:12]
    x_ref, ids_ref, coarse_ids_ref, fine_ref, coarse_ref, sems = refs[12:]
    edge = at_ref[1]
    pairs = []
    for group, part in enumerate(parts):
        for source, columns in block_sources(group, at_ref[0], *weights):
            pairs.append((source, part.at[:, columns]))
        for block in range(4):
            for source, columns in block_sources(group, block, *weights):
                pairs.append((source, owns_ref.at[4 * group + block, :, columns]))
    copies = fetch(
        sems,
        (ids_hbm, ids_ref),
        (coarse_ids_hbm, coarse_ids_ref),
        (coarse_hbm, coarse_ref),
        (fine_hbm, fine_ref),
        (x_hbm, x_ref),
        *pairs,
    )
    for load in copies[:4]:
        load.wait()
    picks = 3 * LANES
    labels = flat_labels(ids_ref, edge, fine_ref[picks : picks + ids_ref.shape[2]])
    coarse_labels = flat_labels(coarse_ids_ref, edge, coarse_ref[picks : picks + coarse_ids_ref.shape[2]])
    labels_ref[...] = labels
    coarse_labels_ref[...] = coarse_labels
    copies[4].wait()
    for number, (packet, count) in enumerate(zip(outs, counts)):
        height = packet.shape[0]
        first = number * LANES
        body = dot(fine_ref[first : first + height], x_ref[...])
        row = lax.broadcasted_iota(jnp.int32, (height, LANES), 0)
        fine = dot_nt(labels, fine_ref[first : first + LANES])[:1]
        coarse = dot_nt(coarse_labels, coarse_ref[first : first + LANES])[:1]
        extra = jnp.where(row == count, fine, jnp.where(row == count + 1, coarse, 0.0))
        packet[:, :LANES] = (body[:, :LANES] + extra).astype(packet.dtype)
        packet[:, LANES:] = body[:, LANES:].astype(packet.dtype)
    for copy in copies[5:]:
        copy.wait()


def wide_labels(labels_ref, packets, counts, line):
    count = labels_ref.shape[1]
    pad = up(count, LANES) - count
    parts = [labels_ref[...].astype(jnp.float32)]
    if pad:
        parts[0] = jnp.concatenate([parts[0], jnp.zeros((8, pad), jnp.float32)], axis=1)
    for packet, size in zip(packets, counts):
        block = packet[size // PACK * PACK : size // PACK * PACK + PACK, :LANES].astype(jnp.float32)
        row = lax.broadcasted_iota(jnp.int32, block.shape, 0)
        picked = jnp.sum(jnp.where(row == size % PACK + line, block, 0.0), axis=0, keepdims=True)
        parts.append(jnp.broadcast_to(picked, (8, LANES)))
    return jnp.concatenate(parts, axis=1).astype(jnp.bfloat16)


def first_kernel(
    heads, counts, x_hbm, select_hbm, qkv_hbm, out_hbm, pick_hbm,
    labels_ref, lat_ref, lon_ref, both_ref, y_ref, *refs,
):
    packets, refs = refs[:6], refs[6:]
    select_ref, qkv_ref, out_ref, pick_ref, stage_ref, rolled_ref, packed_ref, mixed_ref, sems = refs
    cells, width = x_hbm.shape
    window = WIN_LEVELS * WIN_ROWS * WIN_COLS
    loads = fetch(
        sems,
        (x_hbm, stage_ref.at[pl.ds(0, cells)]),
        (select_hbm, select_ref),
        (qkv_hbm, qkv_ref),
        (out_hbm, out_ref),
        (pick_hbm, pick_ref),
    )
    fill(stage_ref, (None, lat_ref, lon_ref, both_ref), cells)
    wide = wide_labels(labels_ref, (lat_ref, lon_ref, both_ref), counts, 0)
    loads[0].wait()
    loads[1].wait()
    rolled = dot(select_ref[...], stage_ref[...])
    rolled_ref[...] = rolled
    loads[2].wait()
    packed_ref[...] = dot(normalized(rolled), qkv_ref[...]).astype(jnp.bfloat16)
    for first in range(0, cells, window):
        bias = label_bias(wide, select_ref[first : first + window])
        attend(packed_ref, mixed_ref, first, window, width, heads, bias)
    loads[3].wait()
    y_ref[...] = (rolled_ref[...] + dot(mixed_ref[...], out_ref[...])).astype(jnp.bfloat16)
    loads[4].wait()
    first = 0
    for packet in packets:
        height = packet.shape[0]
        packet[...] = dot(pick_ref[first : first + height], y_ref[...]).astype(jnp.bfloat16)
        first += height


def join_kernel(plans, *refs):
    sems, outs = refs[-1], refs[-1 - len(plans) : -1]
    pairs = []
    for plan, out_ref in zip(plans, outs):
        first = 0
        for number in plan:
            part = refs[number]
            if len(part.shape) == 2:
                pairs.append((part, out_ref.at[first]))
                first += 1
            else:
                pairs.append((part, out_ref.at[pl.ds(first, part.shape[0])]))
                first += part.shape[0]
    for copy in fetch(sems, *pairs):
        copy.wait()


def start_pieces(whole_ref, sides, at_ref, sems):
    corner, side, here = at_ref[0], at_ref[2], at_ref[3]
    stops = whole_ref.shape[0]
    copies = []

    def put(source, stop, from_side, block):
        rows, wide = source.shape
        held = whole_ref.at[stop, from_side]
        across = whole_ref.shape[3] // wide
        at_row, at_column = (block // across) * rows, (block % across) * wide
        target = held.at[pl.ds(pl.multiple_of(at_row, PACK), rows), pl.ds(pl.multiple_of(at_column, LANES), wide)]
        copies.append(pltpu.make_async_copy(source, target, sems.at[len(copies)]))
        copies[-1].start()

    for other, (own, *stacks) in enumerate(sides):
        from_side = side ^ other
        for block in range(4):
            put(own.at[block], here, from_side, block)
        for stack, mask in zip(stacks, (0, 1 + from_side, 2 - from_side, 3)):
            for back in range(1, stops):
                put(stack.at[back - 1], lax.rem(here + (stops - back), stops), from_side, corner ^ mask)
    return copies


def piece_copies(stops):
    return 2 * (4 + 4 * (stops - 1))


def flat(whole_ref):
    stops, sides, rows, columns = whole_ref.shape
    return whole_ref[...].reshape(stops * sides * rows, columns)


def cuts(refs, plan):
    return [[refs[number].at[pl.ds(first, count)] for number, first, count in side] for side in plan]


def merge_kernel(heads, counts, number, plans, at_ref, select_hbm, coarse_select_hbm, *refs):
    pieces, refs = refs[:number], refs[number:]
    (y_ref, lat_ref, lon_ref, both_ref), labels_ref, packets = refs[:4], refs[4], refs[5:8]
    merged_ref, expos_ref, select_ref, coarse_select_ref, stage_ref = refs[8:13]
    merge_ref, score_ref, packed_ref, sems, merge_sems, score_sems = refs[13:]
    loads = fetch(sems, (select_hbm, select_ref), (coarse_select_hbm, coarse_select_ref))
    merge_copies = start_pieces(merge_ref, cuts(pieces, plans[0]), at_ref, merge_sems)
    score_copies = start_pieces(score_ref, cuts(pieces, plans[1]), at_ref, score_sems)
    fill(stage_ref, (y_ref, lat_ref, lon_ref, both_ref))
    count, width = merged_ref.shape
    loads[0].wait()
    patches = [
        dot(select_ref[first : first + count], stage_ref[...]) for first in range(0, select_ref.shape[0], count)
    ]
    total = 1.0 / (len(patches) * y_ref.shape[1])
    center = sum(jnp.sum(patch, axis=-1, keepdims=True) for patch in patches) * total
    moved = [patch - center for patch in patches]
    spread = sum(jnp.sum(patch * patch, axis=-1, keepdims=True) for patch in moved) * total
    scale = lax.rsqrt(spread + EPSILON)
    left = jnp.concatenate([(patch * scale).astype(jnp.bfloat16) for patch in moved], axis=1)
    wide = wide_labels(labels_ref, packets, counts, 1)
    loads[1].wait()
    bias = label_bias(wide, coarse_select_ref[...])
    for copy in merge_copies:
        copy.wait()
    merged = dot(left, flat(merge_ref)).astype(jnp.bfloat16)
    merged_ref[...] = merged
    left = normalized(merged.astype(jnp.float32))
    for copy in score_copies:
        copy.wait()
    packed_ref[...] = dot(left, flat(score_ref)).astype(jnp.bfloat16)
    for start, members in lane_heads(width, heads):
        queries = packed_ref[:, start : start + LANES]
        keys = packed_ref[:, width + start : width + start + LANES]
        for head, own in members:
            expos = head_expos(queries, keys, own, width // heads, bias)
            expos_ref[head * count : (head + 1) * count] = expos


def close_kernel(heads, number, plan, at_ref, pick_hbm, *refs):
    pieces, (merged_ref, expos_ref, z_ref) = cuts(refs[:number], plan), refs[number : number + 3]
    packets, refs = refs[number + 3 : number + 6], refs[number + 6 :]
    pick_ref, whole_ref, values_ref, mixed_ref, sems, piece_sems = refs
    copies = fetch(sems, (pick_hbm, pick_ref)) + start_pieces(whole_ref, pieces, at_ref, piece_sems)
    count, width = merged_ref.shape
    merged = merged_ref[...].astype(jnp.float32)
    left = normalized(merged)
    for copy in copies:
        copy.wait()
    whole = flat(whole_ref)
    wide = width // 4
    for number in range(4):
        columns = slice(number * wide, (number + 1) * wide)
        first = 2 * number * wide
        values_ref[:, columns] = dot(left, whole[:, first : first + wide]).astype(jnp.bfloat16)
    for start, members in lane_heads(width, heads):
        values = with_ones(values_ref[:, start : start + LANES])
        mixed = None
        for head, own in members:
            mixed = head_mix(expos_ref[head * count : (head + 1) * count], values, own, mixed)
        mixed_ref[:, start : start + LANES] = mixed.astype(jnp.bfloat16)
    mixed = mixed_ref[...]
    for number in range(4):
        columns = slice(number * wide, (number + 1) * wide)
        first = (2 * number + 1) * wide
        z_ref[:, columns] = (merged[:, columns] + dot(mixed, whole[:, first : first + wide])).astype(jnp.bfloat16)
    first = 0
    for packet in packets:
        height = packet.shape[0]
        packet[...] = dot(pick_ref[first : first + height], z_ref[...]).astype(jnp.bfloat16)
        first += height


def place_kernel(select_hbm, own_ref, lat_ref, lon_ref, both_ref, out_ref, select_ref, stage_ref, sems):
    loads = fetch(sems, (select_hbm, select_ref))
    fill(stage_ref, (own_ref, lat_ref, lon_ref, both_ref))
    loads[0].wait()
    out_ref[...] = dot(select_ref[...], stage_ref[...]).astype(out_ref.dtype)


def call(kernel, outs, scratch, scalars=(), hbm=(), vmem=(), hbm_outs=(), pinned=()):
    hbm = [
        pltpu.with_memory_space_constraint(array, pltpu.HBM) if number in pinned else array
        for number, array in enumerate(hbm)
    ]
    spaces = [pltpu.SMEM] * len(scalars) + [pltpu.HBM] * len(hbm) + [pltpu.VMEM] * len(vmem)
    return pl.pallas_call(
        kernel,
        out_shape=[jax.ShapeDtypeStruct(shape, jnp.bfloat16) for shape in outs],
        in_specs=[pl.BlockSpec(memory_space=space) for space in spaces],
        out_specs=[
            pl.BlockSpec(memory_space=pltpu.HBM if number in hbm_outs else pltpu.VMEM)
            for number in range(len(outs))
        ],
        scratch_shapes=scratch,
        compiler_params=pltpu.CompilerParams(vmem_limit_bytes=VMEM_LIMIT),
    )(*scalars, *hbm, *vmem)


def shifted(blocks, step):
    lat, lon = lax.axis_size("lat"), lax.axis_size("lon")
    return (
        lax.ppermute(blocks[0], "lat", [(i, (i + step) % lat) for i in range(lat)]),
        lax.ppermute(blocks[1], "lon", [(i, (i + step) % lon) for i in range(lon)]),
        lax.ppermute(
            blocks[2],
            ("lat", "lon"),
            [(i * lon + j, (i + step) % lat * lon + (j + step) % lon) for i in range(lat) for j in range(lon)],
        ),
    )


def exchange(block, axis, mask):
    return lax.ppermute(block, axis, [(i, i ^ mask) for i in range(lax.axis_size(axis))])


def far_parts(part):
    ranks = lax.axis_size("lon")
    return [
        lax.ppermute(part, "lon", [(i, (i + 2 * back) % ranks) for i in range(ranks)])
        for back in range(1, ranks // 2)
    ]


def routed(block, turn):
    lat, lon = lax.axis_size("lat"), lax.axis_size("lon")
    pairs = [
        (i * lon + j, (i ^ (1 + (j + turn) % 2)) * lon + j) for i in range(lat) for j in range(lon)
    ]
    return lax.ppermute(block, ("lat", "lon"), pairs)


def joined(*plans):
    arrays = []
    for plan in plans:
        arrays += [array for array in plan if not any(array is seen for seen in arrays)]
    numbers = [[next(n for n, seen in enumerate(arrays) if seen is array) for array in plan] for plan in plans]
    shapes = [
        (sum(1 if array.ndim == 2 else array.shape[0] for array in plan),) + plan[0].shape[-2:] for plan in plans
    ]
    return call(
        lambda *refs: join_kernel(numbers, *refs),
        shapes,
        [pltpu.SemaphoreType.DMA((sum(len(plan) for plan in plans),))],
        hbm=arrays,
        hbm_outs=range(len(plans)),
    )


def swapped(pieces):
    return [exchange(piece, "lon", 1) for piece in pieces]


def after(value, *earlier):
    return lax.optimization_barrier((value, earlier))[0]


def dma(count):
    return pltpu.SemaphoreType.DMA((count,))


def bf16(*shape):
    return pltpu.VMEM(shape, jnp.bfloat16)


def per_device(
    tokens, level_ids, coarse_ids, first_qkv, first_out, merge_weight, second_qkv, second_out
):
    levels, height, breadth, width = tokens.shape
    _, low, narrow = coarse_ids.shape
    wider = merge_weight.shape[1]
    cells, coarse_cells = levels * height * breadth, levels * low * narrow
    stops = lax.axis_size("lon") // 2
    lat, lon = lax.axis_index("lat"), lax.axis_index("lon")
    at = jnp.stack([lat % 4, (lat == 0).astype(jnp.int32), lon % 2, lon // 2]).astype(jnp.int32)

    start = regions(levels, height, breadth, 0, 0)
    middle = regions(levels, height, breadth, HALF_ROWS, HALF_COLS)
    end = regions(levels, low, narrow, 0, 0)
    counts = [len(part) for part in start]
    packet_rows = [up(len(part) + 2, PACK) for part in start]
    end_rows = [up(len(part) + 2, PACK) for part in end]
    order = window_order(levels, height, breadth)
    inverse = np.argsort(order)
    rows = second_out.shape[0]

    def picks(parts, counts, columns):
        return [matrix(part, columns, count) for part, count in zip(parts, counts)]

    def spreader(columns, count):
        return matrix(np.arange(count) % columns, up(columns, PACK)).T

    fine = jnp.concatenate(picks(start, [LANES] * 3, cells) + [spreader(breadth, cells)])
    coarse = jnp.concatenate(picks(end, [LANES] * 3, coarse_cells) + [spreader(narrow, coarse_cells)])
    x = tokens.reshape(cells, width)
    *packets, labels, coarse_labels, owns, merge_part, score_part, value_part = call(
        lambda *refs: pack_kernel(counts, *refs),
        [(count, width) for count in packet_rows]
        + [(8, cells), (8, coarse_cells), (12, rows, wider // 2)]
        + [(rows, wider // 2)] * 3,
        [
            bf16(cells, width),
            *[pltpu.VMEM((ids.shape[1], levels, ids.shape[2]), jnp.int32) for ids in (level_ids, coarse_ids)],
            bf16(*fine.shape),
            bf16(*coarse.shape),
            dma(25),
        ],
        scalars=(at,),
        hbm=(x, *[ids.transpose(1, 0, 2) for ids in (level_ids, coarse_ids)], fine, coarse, merge_weight, second_qkv, second_out),
        hbm_outs=(5, 6, 7, 8),
        pinned=range(8),
    )
    got = shifted(packets, -1)
    far = stops - 1

    (near1,) = joined(after(far_parts(merge_part), got))
    first1 = routed(near1, 0)
    far2 = far_parts(after(score_part, near1))
    (other,) = swapped([after(owns, near1)])
    source, depth = replaced(cells, start)
    held = np.empty_like(order)
    held[order] = np.arange(cells)
    select = matrix(source[order], depth)
    pick = jnp.concatenate(
        picks([inverse[part] for part in middle], packet_rows, cells)
        + picks([inverse[part] for part in start], packet_rows, cells)
    )
    got_first = got
    y, *packets = call(
        lambda *refs: first_kernel(HEADS1, counts, *refs),
        [(cells, width)] + [(count, width) for count in packet_rows] * 2,
        [
            bf16(*select.shape),
            bf16(*first_qkv.shape),
            bf16(*first_out.shape),
            bf16(*pick.shape),
            bf16(depth, width),
            pltpu.VMEM((cells, width), jnp.float32),
            bf16(cells, 3 * width),
            bf16(cells, width),
            dma(5),
        ],
        hbm=(x, select, first_qkv, first_out, pick),
        pinned=(3, 4),
        vmem=(labels, *got_first),
    )
    (near2,) = joined(after(far2, first1, y, other))
    first2 = routed(near2, 0)
    far3 = far_parts(after(value_part, near2))
    (join1,) = joined(after([near1, first1], near2))
    second1 = routed(join1, 1)
    (near3,) = joined(after(far3, first2, second1))
    first3 = routed(near3, 0)
    (join2,) = joined(after([near2, first2], near3))
    second2 = routed(join2, 1)
    mid = shifted(after(packets[:3], near3), -1)
    last_first = after(first3, second2, mid)
    (join3,) = joined([near3, last_first])
    second3 = routed(join3, 1)
    early_pieces = (owns, join1, second1, other, *swapped(after((join1, second1), near3)))
    early_pieces += (join2, second2, *swapped(after((join2, second2), last_first)))

    def plan(group, *rest):
        return [
            [(own, 4 * group, 4), (n, 0, far), (n, far, far), (n + 1, 0, far), (n + 1, far, far)]
            for own, n in zip((0, 3), rest)
        ]

    early_plans, value_plan = (plan(0, 1, 4), plan(1, 6, 8)), plan(2, 1, 4)

    source, depth = replaced(cells, middle, held)
    fine = source.reshape(levels, low, 2, narrow, 2)
    patches = [fine[:, :, r, :, c].reshape(-1) for r, c in ((0, 0), (1, 0), (0, 1), (1, 1))]
    select = matrix(np.concatenate(patches), depth)
    fine_depth = depth
    source, depth = replaced(coarse_cells, end)
    coarse_select = matrix(source, depth)
    merged, expos = call(
        lambda *refs: merge_kernel(HEADS2, counts, len(early_pieces), early_plans, *refs),
        [(coarse_cells, wider), (HEADS2 * coarse_cells, coarse_cells)],
        [
            bf16(*select.shape),
            bf16(*coarse_select.shape),
            bf16(fine_depth, width),
            bf16(stops, 2, *merge_weight.shape),
            bf16(stops, 2, rows, 2 * wider),
            bf16(coarse_cells, 2 * wider),
            dma(2),
            dma(piece_copies(stops)),
            dma(piece_copies(stops)),
        ],
        scalars=(at,),
        hbm=(select, coarse_select, *early_pieces),
        vmem=(y, *mid, coarse_labels, *got),
    )

    back = shifted(after(packets[3:], last_first), 1)
    source, depth = replaced(cells, start, held)
    select = matrix(source, depth)
    (skip,) = call(
        place_kernel,
        [(cells, width)],
        [bf16(*select.shape), bf16(depth, width), dma(1)],
        hbm=(select,),
        vmem=(y, *back),
    )

    source, depth = replaced(coarse_cells, end)
    select = matrix(source, depth)
    value_swapped = swapped([after(join3, last_first), after(second3, back, expos)])
    value_pieces = (owns, join3, second3, other, *value_swapped)
    pick = jnp.concatenate(picks(end, end_rows, coarse_cells))
    z, *packets = call(
        lambda *refs: close_kernel(HEADS2, len(value_pieces), value_plan, *refs),
        [(coarse_cells, wider)] + [(count, wider) for count in end_rows],
        [
            bf16(*pick.shape),
            bf16(stops, 2, rows, 2 * wider),
            bf16(coarse_cells, wider),
            bf16(coarse_cells, wider),
            dma(1),
            dma(piece_copies(stops)),
        ],
        scalars=(at,),
        hbm=(pick, *value_pieces),
        vmem=(merged, expos),
    )
    done = shifted(packets, 1)
    (coarse,) = call(
        place_kernel,
        [(coarse_cells, wider)],
        [bf16(*select.shape), bf16(depth, wider), dma(1)],
        hbm=(select,),
        vmem=(z, *done),
    )
    return skip.reshape(tokens.shape), coarse.reshape(levels, low, narrow, wider)


def solution(mesh):
    placed = (
        P(None, "lat", "lon", None),
        P(None, "lat", "lon"),
        P(None, "lat", "lon"),
        P(),
        P(),
        P("lon", None),
        P("lon", None),
        P("lon", None),
    )
    return jax.shard_map(
        per_device,
        mesh=mesh,
        in_specs=placed,
        out_specs=(P(None, "lat", "lon", None), P(None, "lat", "lon", None)),
        check_vma=False,
    )
```
